128 devices in a mesh: grp: 4 (over y), slab: 32 (over x, z, core).
Axes of the slice: x: 4, y: 4, z: 4, core: 2. Of those that a mesh axis runs over, the one named last changes fastest.
Arguments:
- right_side: float32 [256, 256, 256], P(('grp', 'slab')), may hold values from -8 to 8
- conductivity: float32 [256, 256, 256], P(('grp', 'slab')), may hold values from 0.1 to 10
Outputs:
- iterate: float32 [256, 256, 256], P(('grp', 'slab'))
- final_defect: float32 [256, 256, 256], P(('grp', 'slab'))
The draws below stay inside these ranges and needn't reach their ends.
All inputs are finite; a program needn't handle non-finite values.
Results may differ from the reference program's by a relative error of at most 0.00016.
Values sent between devices are 32-bit elements; how exact they have to be, the bound alone decides.
No kernel may reach another device: no remote copies, remote signals or barrier semaphores. Data moves between devices by JAX's collectives and lax.ppermute only.
A program may use at most 128 MiB of HBM per device.

```python
import math
import jax
import jax.numpy as jnp

NXY = 256
KF = 2
KC = 4
CYCLES = 1
NZ = 256
N_GRP = 4


def block_scale(key, shape, cuts, smallest, high):
    level = 1.0
    for axis_at, parts in cuts:
        steps = jax.random.uniform(jax.random.fold_in(jax.random.fold_in(key, 6), axis_at), (parts,), jnp.float32, smallest / len(cuts), high / len(cuts))
        level = level * jnp.repeat(jnp.exp(steps), shape[axis_at] // parts).reshape((-1,) + (1,) * (len(shape) - 1 - axis_at))
    return level


def bell_draw(own_key, dims, scale, most, split=(), kind=jnp.bfloat16):
    drawn = scale * jax.random.normal(own_key, dims, jnp.float32)
    if split:
        drawn = drawn * block_scale(own_key, dims, split, -0.22, 0.18)
    return jnp.clip(drawn, -most, most).astype(kind)


def setup_inputs(seed: int = 0) -> dict:
    arg_keys = jax.random.split(jax.random.key(seed), 3)
    return {
        "right_side": bell_draw(arg_keys[0], (NZ, NXY, NXY), 1.0, 8.0, ((0, 128),), jnp.float32),
        "conductivity": jnp.clip(jnp.exp(math.log(10.0) - 4.6051702 * jax.random.uniform(arg_keys[1], (NZ, NXY, NXY), jnp.float32) ** block_scale(arg_keys[1], (NZ, NXY, NXY), ((0, 128),), -0.2, 0.2)), 0.1, 10.0),
    }


LOWER = 0.25
UPPER = 2.0
SHIFTS = ((1, 0, 0), (-1, 0, 0), (0, 1, 0), (0, -1, 0), (0, 0, 1), (0, 0, -1))


def shifted(padded, offz, offx, offy):
    return padded[1 + offz:padded.shape[0] - 1 + offz, 1 + offx:padded.shape[1] - 1 + offx, 1 + offy:padded.shape[2] - 1 + offy]


def operate(field_zpad, coef_pad, weight):
    full = jnp.pad(field_zpad, ((0, 0), (1, 1), (1, 1)))
    center = shifted(full, 0, 0, 0)
    coef_mid = shifted(coef_pad, 0, 0, 0)
    total = jnp.zeros(center.shape, jnp.float32)
    for offset in SHIFTS:
        face = 0.5 * (coef_mid + shifted(coef_pad, *offset))
        total = total + face * (center - shifted(full, *offset))
    return weight * total


def diagonal_of(coef_pad, weight):
    coef_mid = shifted(coef_pad, 0, 0, 0)
    total = jnp.zeros(coef_mid.shape, jnp.float32)
    for offset in SHIFTS:
        total = total + 0.5 * (coef_mid + shifted(coef_pad, *offset))
    return weight * total


def restrict(field):
    planes, rows, cols = field.shape
    return jnp.mean(field.reshape(planes // 2, 2, rows // 2, 2, cols // 2, 2), axis=(1, 3, 5))


def prolong(field):
    return jnp.repeat(jnp.repeat(jnp.repeat(field, 2, axis=0), 2, axis=1), 2, axis=2)


def chebyshev(start, source, apply_op, inv_diag, count):
    center_val = (UPPER + LOWER) / 2.0
    half_width = (UPPER - LOWER) / 2.0
    ratio_val = center_val / half_width
    rho_now = 1.0 / ratio_val
    current = start
    update = inv_diag * (source - apply_op(current)) / center_val
    current = current + update
    for sweep_index in range(count - 1):
        rho_new = 1.0 / (2.0 * ratio_val - rho_now)
        update = rho_new * rho_now * update + (2.0 * rho_new / half_width) * inv_diag * (source - apply_op(current))
        current = current + update
        rho_now = rho_new
    return current


def column_total(field):
    planes, rows, cols = field.shape
    return jnp.sum(field.reshape(N_GRP, planes // N_GRP, rows, cols), axis=1)


def reference(right_side, conductivity):
    fine_coef = jnp.pad(conductivity, 1)
    coarse_coef = jnp.pad(restrict(conductivity), 1)

    def fine_apply(field):
        return operate(jnp.pad(field, ((1, 1), (0, 0), (0, 0))), fine_coef, 1.0)

    def coarse_apply(field):
        return operate(jnp.pad(field, ((1, 1), (0, 0), (0, 0))), coarse_coef, 0.25)

    inv_fine = 1.0 / diagonal_of(fine_coef, 1.0)
    coarse_diag = diagonal_of(coarse_coef, 0.25)
    inv_coarse = 1.0 / coarse_diag
    column_diag = column_total(coarse_diag)
    group_planes = coarse_diag.shape[0] // N_GRP
    iterate = jnp.zeros(right_side.shape, jnp.float32)
    for cycle_index in range(CYCLES):
        iterate = chebyshev(iterate, right_side, fine_apply, inv_fine, KF)
        defect = right_side - fine_apply(iterate)
        coarse_rhs = restrict(defect)
        smoothed = chebyshev(jnp.zeros(coarse_rhs.shape, jnp.float32), coarse_rhs, coarse_apply, inv_coarse, KC)
        column_defect = column_total(coarse_rhs - coarse_apply(smoothed))
        correction = smoothed + jnp.repeat(column_defect / column_diag, group_planes, axis=0)
        iterate = iterate + prolong(correction)
        iterate = chebyshev(iterate, right_side, fine_apply, inv_fine, KF)
    final_defect = right_side - fine_apply(iterate)
    return iterate, final_defect
```

```python
import functools

import jax
import jax.numpy as jnp
from jax import lax
from jax.experimental import pallas as pl
from jax.experimental.pallas import tpu as pltpu
from jax.sharding import PartitionSpec as P

KF = 2
KC = 4

LOWER = 0.25
UPPER = 2.0
CENTER = (UPPER + LOWER) / 2.0
HALF = (UPPER - LOWER) / 2.0
RATIO = CENTER / HALF

AXES = ("grp", "slab")
N = 256
NC = 128
PAD = 8
CH = 128
VM = pl.BlockSpec(memory_space=pltpu.VMEM)
ANY = pl.BlockSpec(memory_space=pl.ANY)
HBM = pl.BlockSpec(memory_space=pltpu.HBM)


def chebyshev_factors(count):
    rho = 1.0 / RATIO
    found = []
    for _ in range(count - 1):
        new = 1.0 / (2.0 * RATIO - rho)
        found.append((new * rho, 2.0 * new / HALF))
        rho = new
    return found


FINE = chebyshev_factors(KF)
COARSE = chebyshev_factors(KC)


def position():
    grp, slab = lax.axis_index("grp"), lax.axis_index("slab")
    slabs = lax.axis_size("slab")
    total = lax.axis_size("grp") * slabs
    index = grp * slabs + slab
    return index, lax.rem(slab, 2), total


def outer_mask():
    index, _, total = position()
    return jnp.where((index == 0) | (index == total - 1), 0.0, 1.0).astype(jnp.float32)


def lane_iota(shape):
    return lax.broadcasted_iota(jnp.int32, shape, len(shape) - 1)


def rows_of(chunk):
    return pl.multiple_of(chunk * CH, CH)


def at(ref, plane, row):
    return ref[plane, pl.ds(row + PAD, CH), :]


def window(ref, plane, row):
    return ref[plane, pl.ds(row, CH + 2 * PAD), :]


def shifted(win, by):
    return pltpu.roll(win, (-by) % win.shape[0], 0)[PAD : PAD + CH]


def put(ref, plane, row, value):
    ref[plane, pl.ds(row + PAD, CH), :] = value


def clear_pads(ref, planes):
    for p in planes:
        ref[p, 0:PAD, :] = jnp.zeros((PAD, N), jnp.float32)
        ref[p, PAD + N : 2 * PAD + N, :] = jnp.zeros((PAD, N), jnp.float32)


def left(v):
    return pltpu.roll(v, v.shape[-1] - 1, v.ndim - 1)


def right(v):
    return pltpu.roll(v, 1, v.ndim - 1)


class Copies:
    def __init__(self, sems):
        self.sems, self.used = sems, 0

    def start(self, source, target):
        copy = pltpu.make_async_copy(source, target, self.sems.at[self.used])
        self.used += 1
        copy.start()
        return copy


def clear_outside(refs):
    @pl.when(outer_mask() == 0.0)
    def _():
        for ref, plane in refs:
            ref[plane] = jnp.zeros(ref.shape[1:], jnp.float32)


def fill(copies, source, ref, plane):
    return copies.start(source, ref.at[plane, PAD : PAD + N, :])


def off_diagonal(row, here, below, above, fx, fy, fz_below, fz_above):
    v = window(*here, row)
    f = window(*fx, row)
    mid = v[PAD : PAD + CH]
    g = at(*fy, row)
    total = f[PAD : PAD + CH] * shifted(v, 1) + shifted(f * v, -1)
    total = total + (g * left(mid) + right(g * mid))
    return total + (at(*fz_below, row) * at(*below, row) + at(*fz_above, row) * at(*above, row))


def prepare(coef, p, row):
    win = window(coef, p, row)
    b = win[PAD : PAD + CH]
    down = shifted(win, 1)
    lane = lane_iota(b.shape)
    nxt = jnp.where(lane == N - 1, 0.0, left(b))
    prv = jnp.where(lane == 0, 0.0, right(b))
    over = at(coef, p + 1, row)
    around = (down + shifted(win, -1)) + (nxt + prv) + (at(coef, p - 1, row) + over)
    fy = jnp.where(lane == N - 1, 0.0, 0.5 * (b + nxt))
    return 3.0 * b + 0.5 * around, 0.5 * (b + down), fy, 0.5 * (b + over)


def pair_matrix(rows, cols):
    i = lax.broadcasted_iota(jnp.int32, (rows, cols), 0)
    j = lax.broadcasted_iota(jnp.int32, (rows, cols), 1)
    same = i // 2 == j if rows > cols else j // 2 == i
    return jnp.where(same, 1.0, 0.0).astype(jnp.bfloat16)


def dot(x, y):
    total = None
    for _ in range(3):
        part = x.astype(jnp.bfloat16)
        x = x - part.astype(jnp.float32)
        term = jnp.dot(part, y, preferred_element_type=jnp.float32)
        total = term if total is None else total + term
    return total


def first_kernel(g, b, bs, out, coef, sems):
    _, par, _ = position()
    inner = 1 - par
    copies = Copies(sems)
    started = [fill(copies, bs.at[par], coef, 2), fill(copies, b.at[inner], coef, 1), fill(copies, b.at[par], coef, 0)]
    clear_pads(coef, [1])
    for copy in started:
        copy.wait()

    @pl.loop(0, N // CH)
    def _(chunk):
        row = rows_of(chunk)
        diag = prepare(coef, 1, row)[0]
        out[0, pl.ds(row, CH), :] = g[par, pl.ds(row, CH), :]
        out[1, pl.ds(row, CH), :] = g[inner, pl.ds(row, CH), :] / (CENTER * diag)


FXS, FYS, IVS, FZS, XS, DGS, COARSE_AT, STATE = 0, 4, 8, 12, 17, 20, 22, 23


def make_state(g, gs, b, bs, bx, state, coef, rhs, copies, also):
    _, par, _ = position()
    inner = 1 - par
    alive = outer_mask()
    O2, O1, A, B, I1, I2 = range(6)
    source = {O2: bx.at[par], O1: bx.at[inner], A: b.at[par], B: b.at[inner], I1: bs.at[par], I2: bs.at[inner]}
    given = [g.at[par], g.at[inner], gs.at[par]]
    started = [fill(copies, ref, coef, p) for p, ref in source.items()]
    started += [copies.start(ref, rhs.at[k + 1]) for k, ref in enumerate(given)]
    clear_pads(coef, range(6))
    clear_pads(state, range(FXS, FXS + 4))
    clear_pads(state, range(XS, XS + 3))
    for copy in started:
        copy.wait()
    clear_outside([(coef, O2), (coef, O1)])

    @pl.loop(0, N // CH)
    def _(chunk):
        row = rows_of(chunk)
        put(state, FZS, row, 0.5 * (at(coef, O2, row) + at(coef, O1, row)))
        for k, p in enumerate((O1, A, B, I1)):
            diag, fx, fy, fz = prepare(coef, p, row)
            inv = 1.0 / diag
            if p == O1:
                inv = inv * alive
            else:
                put(state, XS + k - 1, row, rhs[k, pl.ds(row, CH), :] * inv * (1.0 / CENTER))
            if p in (A, B):
                put(state, DGS + k - 1, row, diag)
            put(state, FXS + k, row, fx)
            put(state, FYS + k, row, fy)
            put(state, FZS + 1 + k, row, fz)
            put(state, IVS + k, row, inv)
        also(row)


def ready_kernel(g, gs, b, bs, bx, sent, state, xa, coef, rhs, red, cpl, sems):
    del sent
    O2, O1, A, B, I1, I2 = range(6)

    def also(row):
        xa[pl.ds(row, CH), :] = at(state, XS, row)
        for k, (p, q) in enumerate(((A, B), (O1, O2), (I1, I2))):
            red[pl.ds(k * N + row, CH), :] = at(coef, p, row) + at(coef, q, row)

    make_state(g, gs, b, bs, bx, state, coef, rhs, Copies(sems), also)
    cpl[...] = dot(red[...], pair_matrix(N, NC))
    bc, bo, bi = (
        0.125 * (cpl[pl.ds(k * N, NC, 2), :] + cpl[pl.ds(k * N + 1, NC, 2), :]) for k in range(3)
    )
    row_at = lax.broadcasted_iota(jnp.int32, (NC, NC), 0)
    lane = lane_iota((NC, NC))
    around = (
        jnp.where(lane == NC - 1, 0.0, left(bc))
        + jnp.where(lane == 0, 0.0, right(bc))
        + jnp.where(row_at == NC - 1, 0.0, pltpu.roll(bc, NC - 1, 0))
        + jnp.where(row_at == 0, 0.0, pltpu.roll(bc, 1, 0))
    )
    diag = 0.25 * (3.0 * bc + 0.5 * (around + bo + bi))
    state[COARSE_AT, 0:NC, 0:NC] = bc
    state[COARSE_AT, 0:NC, NC:N] = 1.0 / (CENTER * diag)


def pre_smooth(state, rhs, x1, e2, r1, x2, done):
    O1, A, B, I1 = range(4)

    @pl.loop(0, N // CH)
    def _(chunk):
        row = rows_of(chunk)
        put(x1, 1, row, rhs[O1, pl.ds(row, CH), :] * at(state, IVS + O1, row) * (1.0 / CENTER))

    step_a, step_b = FINE[0]
    first = [(x1, 0), (x1, 1), (state, XS), (state, XS + 1), (state, XS + 2), (x1, 2)]

    def faces(k):
        return (state, FXS + k), (state, FYS + k), (state, FZS + k), (state, FZS + k + 1)

    @pl.loop(0, N // CH)
    def _(chunk):
        row = rows_of(chunk)
        for k in (O1, A, B, I1):
            res = off_diagonal(row, first[k + 1], first[k], first[k + 2], *faces(k))
            res = res + (1.0 - 1.0 / CENTER) * rhs[k, pl.ds(row, CH), :]
            here = at(*first[k + 1], row)
            move = step_a * here + step_b * (at(state, IVS + k, row) * res)
            put(e2, k, row, move)
            if k in (A, B):
                r1[k - A, pl.ds(row, CH), :] = res
                if x2 is not None:
                    x2[3 + k - A, pl.ds(row, CH), :] = here + move

    @pl.loop(0, N // CH)
    def _(chunk):
        row = rows_of(chunk)
        found = []
        for k in (A, B):
            res = r1[k - A, pl.ds(row, CH), :] - at(state, DGS + k - A, row) * at(e2, k, row)
            found.append(res + off_diagonal(row, (e2, k), (e2, k - 1), (e2, k + 1), *faces(k)))
        done(row, *found)


SPLIT = 2
HELD = 5


def pre_kernel(g, gs, bs, bx, state, sx, xi, pack, over, side, rhs, x1, e2, r1, red, cpl, packed, sems):
    _, par, _ = position()
    inner = 1 - par
    copies = Copies(sems)
    started = [copies.start(ref, rhs.at[k]) for k, ref in enumerate((sx.at[0], g.at[par], g.at[inner], gs.at[par]))]
    started += [fill(copies, sx.at[1], x1, 0), fill(copies, xi, x1, 2)]
    leaving = [copies.start(bs.at[par], over.at[2]), copies.start(bx.at[inner], side.at[2])]
    clear_pads(x1, range(3))
    clear_pads(e2, range(4))
    for copy in started:
        copy.wait()

    def done(row, ra, rb):
        red[pl.ds(row, CH), :] = ra + rb
        for ref in (over, side):
            ref[0, pl.ds(row, CH), :] = ra
            ref[1, pl.ds(row, CH), :] = rb

    pre_smooth(state, rhs, x1, e2, r1, side, done)
    cpl[0:N, :] = dot(red[...], pair_matrix(N, NC))
    rc = 0.125 * (cpl[pl.ds(0, NC, 2), :] + cpl[pl.ds(1, NC, 2), :])
    fields = (rc * state[COARSE_AT, 0:NC, NC:N], state[COARSE_AT, 0:NC, 0:NC])
    for k, field in enumerate(fields):
        base = k * (NC + 16)
        cpl[base : base + 8, :] = jnp.zeros((8, NC), jnp.float32)
        cpl[base + NC + 8 : base + NC + 16, :] = jnp.zeros((8, NC), jnp.float32)
        cpl[base + 8 : base + NC + 8, :] = field
    each = NC // 2 // SPLIT
    for part in range(SPLIT):
        for odd, first in ((0, 4), (1, 9)):
            for k in range(2):
                for j in range(HELD):
                    rows = cpl[pl.ds(k * (NC + 16) + first + j + part * each * 2, each, 2), :]
                    packed[pl.ds(part * each * 4 * HELD + (odd * 2 + k) * HELD + j, each, 4 * HELD), :] = rows
        piece = pl.ds(part * each * 4 * HELD, each * 4 * HELD)
        leaving.append(copies.start(packed.at[piece], pack.at[piece]))
    for copy in leaving:
        copy.wait()
    clear_outside([(side, 2)])


def coarse_kernel(recv, other, over, pack, cpl, packed, sems):
    del over
    index, par, _ = position()
    rows = 2 * HELD
    planes = recv.shape[0] // rows
    plane_at = lax.broadcasted_iota(jnp.int32, (planes, NC), 0)
    lane = lane_iota((planes, NC))

    def up(v):
        return pltpu.roll(v, planes - 1, 0)

    def down(v):
        return pltpu.roll(v, 1, 0)

    def row_of(field, n):
        if n >= 0:
            return recv[pl.ds(field * HELD + jnp.where(par == 0, 4 - n, n), planes, rows), :]
        return other[pl.ds(field * HELD + jnp.where(par == 0, -n - 1, 5 + n), planes, rows), :]

    u1 = {j: row_of(0, j) for j in range(-4, 5)}
    bc = {j: row_of(1, j) for j in range(-4, 5)}
    fr = {j: 0.125 * (bc[j] + bc[j + 1]) for j in range(-4, 4)}
    fz, fy, dg, iv = {}, {}, {}, {}
    for j in range(-3, 4):
        zn = jnp.where(plane_at == planes - 1, 0.0, up(bc[j]))
        zp = jnp.where(plane_at == 0, 0.0, down(bc[j]))
        yn = jnp.where(lane == NC - 1, 0.0, left(bc[j]))
        yp = jnp.where(lane == 0, 0.0, right(bc[j]))
        fz[j] = jnp.where(plane_at == planes - 1, 0.0, 0.125 * (bc[j] + zn))
        fy[j] = jnp.where(lane == NC - 1, 0.0, 0.125 * (bc[j] + yn))
        dg[j] = 0.75 * bc[j] + 0.125 * (zn + zp + yn + yp + bc[j - 1] + bc[j + 1])
        row = index + jnp.where(par == 0, -j, j)
        inside = (row >= 0) & (row < NC)
        iv[j] = jnp.where(inside, 1.0 / jnp.where(inside, dg[j], 1.0), 0.0)

    def off(v, j):
        total = fr[j] * v[j + 1] + fr[j - 1] * v[j - 1]
        total = total + fz[j] * up(v[j]) + down(fz[j] * v[j])
        return total + fy[j] * left(v[j]) + right(fy[j] * v[j])

    reach = 3
    res = {j: (CENTER - 1.0) * dg[j] * u1[j] + off(u1, j) for j in range(-reach, reach + 1)}
    step = u1
    total = u1[0]
    for k, (step_a, step_b) in enumerate(COARSE):
        step = {j: step_a * step[j] + step_b * iv[j] * res[j] for j in range(-reach, reach + 1)}
        total = total + step[0]
        reach -= 1
        res = {j: res[j] - dg[j] * step[j] + off(step, j) for j in range(-reach, reach + 1)}
    groups = lax.axis_size("grp")
    each = planes // groups
    column = jnp.sum(res[0].reshape(groups, each, NC), axis=1, keepdims=True)
    weight = jnp.sum(dg[0].reshape(groups, each, NC), axis=1, keepdims=True)
    lift = jnp.broadcast_to(column / weight, (groups, each, NC)).reshape(planes, NC)
    cpl[0:8, :] = jnp.zeros((8, NC), jnp.float32)
    cpl[planes + 8 : planes + 16, :] = jnp.zeros((8, NC), jnp.float32)
    cpl[8 : planes + 8, :] = total + lift
    for k in range(5):
        packed[pl.ds(k, planes, 5), :] = cpl[pl.ds(6 + k, planes), :]
    Copies(sems).start(packed, pack).wait()


def post_kernel(
    b, bs, bx, own, over, side, w, x5, r5,
    coef, fx, fy, fz, iv, dg, before, x2v, pw, r3, e4, r4, e5, half, wide, x5v, r5v, sems,
):
    _, par, _ = position()
    inner = 1 - par
    order = (par, inner)
    alive = outer_mask()
    copies = Copies(sems)
    source = (over.at[2], bx.at[par], bx.at[inner], b.at[par], b.at[inner], bs.at[par], bs.at[inner], side.at[2])
    started = [fill(copies, ref, coef, p) for p, ref in enumerate(source)]
    source = (over.at[1], over.at[0], own.at[0], own.at[1], side.at[1], side.at[0])
    started += [copies.start(ref, before.at[k]) for k, ref in enumerate(source)]
    started.append(copies.start(own.at[3:5], x2v))
    clear_pads(coef, range(8))
    clear_pads(fx, range(4))
    clear_pads(pw, range(8))
    clear_pads(e4, range(6))
    clear_pads(e5, range(4))
    spread = dot(w[...], pair_matrix(NC, N))
    for side in (0, 1):
        wide[side] = spread[:, side * NC : (side + 1) * NC]
    for k, planes in enumerate(((0,), (1, 2), (3, 4), (5, 6), (7,))):
        z = jnp.where(par == 0, k, 4 - k)
        for side in (0, 1):
            part = wide[side, pl.ds(z, NC, 5), :]
            half[pl.ds(0, NC, 2), :] = part
            half[pl.ds(1, NC, 2), :] = part
            for p in planes:
                pw[p, PAD : PAD + N, side * NC : (side + 1) * NC] = half[...]
    for copy in started:
        copy.wait()
    clear_outside([(coef, 0), (coef, 1), (coef, 2)])

    @pl.loop(0, N // CH)
    def _(chunk):
        row = rows_of(chunk)
        for k in range(6):
            p = k + 1
            win = window(coef, p, row)
            ahead = pltpu.roll(win, win.shape[0] - 1, 0)
            mid = win[PAD : PAD + CH]
            lane = lane_iota(mid.shape)
            nxt = jnp.where(lane == N - 1, 0.0, left(mid))
            prv = jnp.where(lane == 0, 0.0, right(mid))
            under, over = at(coef, p - 1, row), at(coef, p + 1, row)
            around = (ahead[PAD : PAD + CH] + shifted(win, -1)) + (nxt + prv) + (under + over)
            diag = 3.0 * mid + 0.5 * around
            if k < 2:
                inv = alive / jnp.where(diag > 0.0, diag, 1.0)
            else:
                inv = 1.0 / diag
            fxw = 0.5 * (win + ahead)
            fyc = jnp.where(lane == N - 1, 0.0, 0.5 * (mid + nxt))
            below, above = 0.5 * (mid + under), 0.5 * (mid + over)
            if 1 <= k <= 4:
                put(fx, k - 1, row, fxw[PAD : PAD + CH])
                fy[k - 1, pl.ds(row, CH), :] = fyc
                fz[k - 1, pl.ds(row, CH), :] = below
                iv[k - 1, pl.ds(row, CH), :] = inv
                if k == 4:
                    fz[4, pl.ds(row, CH), :] = above
            if k in (2, 3):
                dg[k - 2, pl.ds(row, CH), :] = diag
            v = window(pw, p, row)
            here = v[PAD : PAD + CH]
            total = fxw[PAD : PAD + CH] * shifted(v, 1) + shifted(fxw * v, -1)
            total = total + (fyc * left(here) + right(fyc * here))
            total = total + (below * at(pw, p - 1, row) + above * at(pw, p + 1, row))
            res = (before[k, pl.ds(row, CH), :] - diag * here) + total
            if 1 <= k <= 4:
                r3[k - 1, pl.ds(row, CH), :] = res
            put(e4, k, row, (1.0 / CENTER) * (inv * res))

    step_a, step_b = FINE[0]

    def off(v, k, shift, row):
        win, f = window(v, k + shift, row), window(fx, k, row)
        here = win[PAD : PAD + CH]
        g = fy[k, pl.ds(row, CH), :]
        total = f[PAD : PAD + CH] * shifted(win, 1) + shifted(f * win, -1)
        total = total + (g * left(here) + right(g * here))
        total = total + fz[k, pl.ds(row, CH), :] * at(v, k + shift - 1, row)
        return total + fz[k + 1, pl.ds(row, CH), :] * at(v, k + shift + 1, row)

    @pl.loop(0, N // CH)
    def _(chunk):
        row = rows_of(chunk)
        for k in range(4):
            res = off(e4, k, 1, row) + (1.0 - 1.0 / CENTER) * r3[k, pl.ds(row, CH), :]
            here = at(e4, k + 1, row)
            move = step_a * here + step_b * (iv[k, pl.ds(row, CH), :] * res)
            put(e5, k, row, move)
            if k in (1, 2):
                r4[k - 1, pl.ds(row, CH), :] = res
                x5v[k - 1, pl.ds(row, CH), :] = (x2v[k - 1, pl.ds(row, CH), :] + at(pw, k + 2, row)) + (here + move)

    leaving = [copies.start(x5v.at[k], x5.at[order[k]]) for k in range(2)]

    @pl.loop(0, N // CH)
    def _(chunk):
        row = rows_of(chunk)
        for k in (1, 2):
            res = r4[k - 1, pl.ds(row, CH), :] - dg[k - 1, pl.ds(row, CH), :] * at(e5, k, row)
            r5v[k - 1, pl.ds(row, CH), :] = res + off(e5, k, 0, row)

    leaving += [copies.start(r5v.at[k], r5.at[order[k]]) for k in range(2)]
    for copy in leaving:
        copy.wait()


def call(kernel, outs, scratch, sems, cost, *operands, limit=24):
    return pl.pallas_call(
        kernel,
        out_shape=[jax.ShapeDtypeStruct(s, jnp.float32) for s, _ in outs],
        in_specs=[spec for _, spec in operands],
        out_specs=[spec for _, spec in outs],
        scratch_shapes=[pltpu.VMEM(s, jnp.float32) for s in scratch] + [pltpu.SemaphoreType.DMA((sems,))],
        compiler_params=pltpu.CompilerParams(vmem_limit_bytes=limit * 1024 * 1024),
        cost_estimate=pl.CostEstimate(flops=cost, bytes_accessed=cost, transcendentals=0),
    )(*(array for array, _ in operands))


def local(right_side, conductivity):
    total = lax.axis_size("grp") * lax.axis_size("slab")
    inside = [(i, i ^ 1) for i in range(total)]
    across = [(i, (i + 1) % total) for i in range(1, total, 2)] + [((i + 1) % total, i) for i in range(1, total, 2)]

    def swap(v):
        return lax.ppermute(v, AXES, inside)

    def cross(v):
        return lax.ppermute(v, AXES, across)

    def everywhere(v):
        rows = v.shape[0]
        return lax.all_to_all(v.reshape(rows, 1, NC), AXES, 0, 0, tiled=True).reshape(rows, NC)

    plane, padded = (N, N), (N + 2 * PAD, N)
    two = (2,) + plane
    g, b = right_side, conductivity
    bs = swap(b)
    bx = cross(b)
    gs = swap(g)
    (send,) = call(first_kernel, [(two, VM)], [(3,) + padded], 3, 1 << 20, (g, VM), (b, ANY), (bs, ANY))
    sx = cross(send)
    state, xa = call(
        ready_kernel,
        [((STATE,) + padded, VM), (plane, VM)],
        [(6,) + padded, (4,) + plane, (3 * N, N), (3 * N, NC)],
        9,
        6 << 20,
        (g, ANY), (gs, ANY), (b, ANY), (bs, ANY), (bx, ANY), (send, ANY),
    )
    xi = swap(xa)
    pack, over, side = call(
        pre_kernel,
        [((2 * HELD * total, NC), HBM), ((3,) + plane, VM), ((5,) + plane, VM)],
        [(4,) + plane, (3,) + padded, (4,) + padded, two, plane, (2 * (NC + 16), NC), (2 * HELD * total, NC)],
        8 + SPLIT,
        6 << 20,
        (g, ANY), (gs, ANY), (bs, ANY), (bx, ANY), (state, VM), (sx, ANY), (xi, ANY),
    )
    from_over = cross(over)
    from_side = swap(side)
    own = swap(from_side)
    got = everywhere(pack)
    (back,) = call(
        coarse_kernel,
        [((5 * NC, NC), HBM)],
        [(total + 16, NC), (5 * NC, NC)],
        1,
        4 << 20,
        (got, VM), (swap(got), VM), (from_over, ANY),
    )
    w = everywhere(back)
    x5, r5 = call(
        post_kernel,
        [(two, HBM), (two, HBM)],
        [(8,) + padded, (4,) + padded, (4,) + plane, (5,) + plane, (4,) + plane, two, (6,) + plane, two, (8,) + padded, (4,) + plane, (6,) + padded, two, (4,) + padded, (N, NC), (2, 5 * NC, NC), two, two],
        20,
        8 << 20,
        (b, ANY), (bs, ANY), (bx, ANY), (own, ANY), (from_over, ANY), (from_side, ANY), (w, VM),
    )
    return x5, r5


def solution(mesh):
    spec = P(AXES, None, None)
    return jax.shard_map(
        local, mesh=mesh, in_specs=(spec, spec), out_specs=(spec, spec), check_vma=False
    )
```

```python
import functools

import jax
import jax.numpy as jnp
from jax import lax
from jax.experimental import pallas as pl
from jax.experimental.pallas import tpu as pltpu
from jax.sharding import PartitionSpec as P

KF = 2
KC = 4

LOWER = 0.25
UPPER = 2.0
CENTER = (UPPER + LOWER) / 2.0
HALF = (UPPER - LOWER) / 2.0
RATIO = CENTER / HALF

AXES = ("grp", "slab")
N = 256
NC = 128
PAD = 8
CH = 256
VM = pl.BlockSpec(memory_space=pltpu.VMEM)
ANY = pl.BlockSpec(memory_space=pl.ANY)
HBM = pl.BlockSpec(memory_space=pltpu.HBM)


def chebyshev_factors(count):
    rho = 1.0 / RATIO
    found = []
    for _ in range(count - 1):
        new = 1.0 / (2.0 * RATIO - rho)
        found.append((new * rho, 2.0 * new / HALF))
        rho = new
    return found


FINE = chebyshev_factors(KF)
COARSE = chebyshev_factors(KC)


def position():
    grp, slab = lax.axis_index("grp"), lax.axis_index("slab")
    slabs = lax.axis_size("slab")
    total = lax.axis_size("grp") * slabs
    index = grp * slabs + slab
    return index, lax.rem(slab, 2), total


def outer_mask():
    index, _, total = position()
    return jnp.where((index == 0) | (index == total - 1), 0.0, 1.0).astype(jnp.float32)


def lane_iota(shape):
    return lax.broadcasted_iota(jnp.int32, shape, len(shape) - 1)


def rows_of(chunk):
    return pl.multiple_of(chunk * CH, CH)


def whole_planes(body):
    assert CH == N
    body(0)


def at(ref, plane, row):
    return ref[plane, pl.ds(row + PAD, CH), :]


def window(ref, plane, row):
    return ref[plane, pl.ds(row, CH + 2 * PAD), :]


def shifted(win, by):
    return pltpu.roll(win, (-by) % win.shape[0], 0)[PAD : PAD + CH]


def put(ref, plane, row, value):
    ref[plane, pl.ds(row + PAD, CH), :] = value


def clear_pads(ref, planes):
    for p in planes:
        ref[p, 0:PAD, :] = jnp.zeros((PAD, N), jnp.float32)
        ref[p, PAD + N : 2 * PAD + N, :] = jnp.zeros((PAD, N), jnp.float32)


def left(v):
    return pltpu.roll(v, v.shape[-1] - 1, v.ndim - 1)


def right(v):
    return pltpu.roll(v, 1, v.ndim - 1)


class Copies:
    def __init__(self, sems):
        self.sems, self.used = sems, 0

    def start(self, source, target):
        copy = pltpu.make_async_copy(source, target, self.sems.at[self.used])
        self.used += 1
        copy.start()
        return copy

    def again(self, source, target):
        pltpu.make_async_copy(source, target, self.sems.at[self.used]).start()

    def handle(self, source, target):
        copy = pltpu.make_async_copy(source, target, self.sems.at[self.used])
        self.used += 1
        return copy


def clear_outside(refs):
    @pl.when(outer_mask() == 0.0)
    def _():
        for ref, plane in refs:
            ref[plane] = jnp.zeros(ref.shape[1:], jnp.float32)


def fill(copies, source, ref, plane):
    return copies.start(source, ref.at[plane, PAD : PAD + N, :])


def lateral(row, here, fx, fy):
    v = window(*here, row)
    f = window(*fx, row)
    mid = v[PAD : PAD + CH]
    g = at(*fy, row)
    total = f[PAD : PAD + CH] * shifted(v, 1) + shifted(f * v, -1)
    return total + (g * left(mid) + right(g * mid))


def inverse(v):
    return 1.0 / v


def prepare(coef, p, row):
    win = window(coef, p, row)
    b = win[PAD : PAD + CH]
    down = shifted(win, 1)
    lane = lane_iota(b.shape)
    nxt = jnp.where(lane == N - 1, 0.0, left(b))
    prv = jnp.where(lane == 0, 0.0, right(b))
    over = at(coef, p + 1, row)
    around = (down + shifted(win, -1)) + (nxt + prv) + (at(coef, p - 1, row) + over)
    fy = jnp.where(lane == N - 1, 0.0, 0.5 * (b + nxt))
    return 3.0 * b + 0.5 * around, 0.5 * (b + down), fy, 0.5 * (b + over)


def pair_matrix(rows, cols):
    i = lax.broadcasted_iota(jnp.int32, (rows, cols), 0)
    j = lax.broadcasted_iota(jnp.int32, (rows, cols), 1)
    same = i // 2 == j if rows > cols else j // 2 == i
    return jnp.where(same, 1.0, 0.0).astype(jnp.bfloat16)


def dot(x, y):
    total = None
    for _ in range(3):
        part = x.astype(jnp.bfloat16)
        x = x - part.astype(jnp.float32)
        term = jnp.dot(part, y, preferred_element_type=jnp.float32)
        total = term if total is None else total + term
    return total


def first_kernel(g, b, bs, out, coef, sems):
    _, par, _ = position()
    inner = 1 - par
    copies = Copies(sems)
    started = [fill(copies, bs.at[par], coef, 2), fill(copies, b.at[inner], coef, 1), fill(copies, b.at[par], coef, 0)]
    clear_pads(coef, [1])
    for copy in started:
        copy.wait()

    @pl.loop(0, N // CH)
    def _(chunk):
        row = rows_of(chunk)
        diag = prepare(coef, 1, row)[0]
        out[0, pl.ds(row, CH), :] = g[par, pl.ds(row, CH), :]
        out[1, pl.ds(row, CH), :] = g[inner, pl.ds(row, CH), :] / (CENTER * diag)


(FXO, FXA, FYO, FYA, IVO, IVA, IVI, Z0, Z1, Z2, Z3, Z4, XA, XI, PA, PI, DA, EB, PB, X2B, COARSE_AT, STATE) = range(22)


def ready_kernel(g, gs, b, bs, bx, sent, state, xa, coef, rhs, mine, red, cpl, sems):
    del sent
    _, par, _ = position()
    inner = 1 - par
    alive = outer_mask()
    O2, O1, A, B, I1, I2 = range(6)
    FXB, FXI, FYB, FYI, IVB, DB, XB, RB = range(8)
    copies = Copies(sems)
    source = {O2: bx.at[par], O1: bx.at[inner], A: b.at[par], B: b.at[inner], I1: bs.at[par], I2: bs.at[inner]}
    given = [g.at[par], g.at[inner], gs.at[par]]
    started = [fill(copies, ref, coef, p) for p, ref in source.items()]
    started += [copies.start(ref, rhs.at[k]) for k, ref in enumerate(given)]
    clear_pads(coef, range(6))
    clear_pads(state, (FXO, FXA, XA, XI, EB))
    clear_pads(mine, (FXB, FXI, XB))
    for copy in started:
        copy.wait()
    clear_outside([(coef, O2), (coef, O1)])
    keep = {
        O1: ((state, FXO), (state, FYO), (state, IVO), (state, Z1), None, None),
        A: ((state, FXA), (state, FYA), (state, IVA), (state, Z2), (state, DA), (state, XA)),
        B: ((mine, FXB), (mine, FYB), (mine, IVB), (state, Z3), (mine, DB), (mine, XB)),
        I1: ((mine, FXI), (mine, FYI), (state, IVI), (state, Z4), None, (state, XI)),
    }

    @pl.loop(0, N // CH)
    def _(chunk):
        row = rows_of(chunk)
        put(state, Z0, row, 0.5 * (at(coef, O2, row) + at(coef, O1, row)))
        for k, p in enumerate((O1, A, B, I1)):
            diag, fx, fy, fz = prepare(coef, p, row)
            to_fx, to_fy, to_iv, to_fz, to_dg, to_x = keep[p]
            inv = 1.0 / diag
            if p == O1:
                inv = inv * alive
            put(*to_fx, row, fx)
            put(*to_fy, row, fy)
            put(*to_iv, row, inv)
            put(*to_fz, row, fz)
            if to_dg:
                put(*to_dg, row, diag)
            if to_x:
                x1 = rhs[k - 1, pl.ds(row, CH), :] * inv * (1.0 / CENTER)
                put(*to_x, row, x1)
                if p == A:
                    xa[pl.ds(row, CH), :] = x1
        for k, (p, q) in enumerate(((A, B), (O1, O2), (I1, I2))):
            red[pl.ds(k * N + row, CH), :] = at(coef, p, row) + at(coef, q, row)

    step_a, step_b = FINE[0]
    left_over = 1.0 - 1.0 / CENTER

    @pl.loop(0, N // CH)
    def _(chunk):
        row = rows_of(chunk)
        here = at(mine, XB, row)
        part = lateral(row, (state, XA), (state, FXA), (state, FYA)) + at(state, Z2, row) * here
        put(state, PA, row, part + left_over * rhs[0, pl.ds(row, CH), :])
        part = lateral(row, (state, XI), (mine, FXI), (mine, FYI)) + at(state, Z3, row) * here
        put(state, PI, row, part + left_over * rhs[2, pl.ds(row, CH), :])
        res = lateral(row, (mine, XB), (mine, FXB), (mine, FYB)) + left_over * rhs[1, pl.ds(row, CH), :]
        res = res + (at(state, Z2, row) * at(state, XA, row) + at(state, Z3, row) * at(state, XI, row))
        move = step_a * here + step_b * (at(mine, IVB, row) * res)
        put(state, EB, row, move)
        put(state, X2B, row, here + move)
        put(mine, RB, row, res - at(mine, DB, row) * move)

    @pl.loop(0, N // CH)
    def _(chunk):
        row = rows_of(chunk)
        put(state, PB, row, at(mine, RB, row) + lateral(row, (state, EB), (mine, FXB), (mine, FYB)))

    cpl[...] = dot(red[...], pair_matrix(N, NC))
    bc, bo, bi = (
        0.125 * (cpl[pl.ds(k * N, NC, 2), :] + cpl[pl.ds(k * N + 1, NC, 2), :]) for k in range(3)
    )
    row_at = lax.broadcasted_iota(jnp.int32, (NC, NC), 0)
    lane = lane_iota((NC, NC))
    around = (
        jnp.where(lane == NC - 1, 0.0, left(bc))
        + jnp.where(lane == 0, 0.0, right(bc))
        + jnp.where(row_at == NC - 1, 0.0, pltpu.roll(bc, NC - 1, 0))
        + jnp.where(row_at == 0, 0.0, pltpu.roll(bc, 1, 0))
    )
    diag = 0.25 * (3.0 * bc + 0.5 * (around + bo + bi))
    state[COARSE_AT, 0:NC, 0:NC] = bc
    state[COARSE_AT, 0:NC, NC:N] = 1.0 / (CENTER * diag)


SPLIT = 2
HELD = 5


def pre_kernel(bs, bx, state, sx, xi, pack, side, x1, e2, part, red, cpl, packed, own, zeros, sems):
    _, par, _ = position()
    inner = 1 - par
    copies = Copies(sems)
    leaving = [copies.start(bs.at[par], side.at[2])]
    beyond = outer_mask() == 0.0

    @pl.when(beyond)
    def _():
        zeros[...] = jnp.zeros((N, N), jnp.float32)
        copies.again(zeros, side.at[3])

    @pl.when(jnp.logical_not(beyond))
    def _():
        copies.again(bx.at[inner], side.at[3])

    leaving.append(copies.handle(bx.at[inner], side.at[3]))
    clear_pads(x1, [0])
    clear_pads(e2, [0])

    @pl.loop(0, N // CH)
    def _(chunk):
        row = rows_of(chunk)
        put(x1, 0, row, sx[0, pl.ds(row, CH), :] * at(state, IVO, row) * (1.0 / CENTER))

    step_a, step_b = FINE[0]

    @pl.loop(0, N // CH)
    def _(chunk):
        row = rows_of(chunk)
        here = at(x1, 0, row)
        res = lateral(row, (x1, 0), (state, FXO), (state, FYO)) + (1.0 - 1.0 / CENTER) * sx[0, pl.ds(row, CH), :]
        res = res + (at(state, Z0, row) * sx[1, pl.ds(row, CH), :] + at(state, Z1, row) * at(state, XA, row))
        e2o = step_a * here + step_b * (at(state, IVO, row) * res)
        res = at(state, PA, row) + at(state, Z1, row) * here
        e2a = step_a * at(state, XA, row) + step_b * (at(state, IVA, row) * res)
        put(e2, 0, row, e2a)
        own[2, pl.ds(row, CH), :] = at(state, XA, row) + e2a
        own[3, pl.ds(row, CH), :] = at(state, X2B, row)
        res = res - at(state, DA, row) * e2a
        part[pl.ds(row, CH), :] = res + (at(state, Z1, row) * e2o + at(state, Z2, row) * at(state, EB, row))
        res = at(state, PI, row) + at(state, Z4, row) * xi[pl.ds(row, CH), :]
        e2i = step_a * at(state, XI, row) + step_b * (at(state, IVI, row) * res)
        own[1, pl.ds(row, CH), :] = at(state, PB, row) + (at(state, Z2, row) * e2a + at(state, Z3, row) * e2i)

    leaving += [copies.start(own.at[1], side.at[1]), copies.start(own.at[2:4], side.at[4:6])]

    @pl.loop(0, N // CH)
    def _(chunk):
        row = rows_of(chunk)
        res = part[pl.ds(row, CH), :] + lateral(row, (e2, 0), (state, FXA), (state, FYA))
        own[0, pl.ds(row, CH), :] = res
        red[pl.ds(row, CH), :] = res + own[1, pl.ds(row, CH), :]

    leaving.append(copies.start(own.at[0], side.at[0]))
    cpl[0:N, :] = dot(red[...], pair_matrix(N, NC))
    rc = 0.125 * (cpl[pl.ds(0, NC, 2), :] + cpl[pl.ds(1, NC, 2), :])
    fields = (rc * state[COARSE_AT, 0:NC, NC:N], state[COARSE_AT, 0:NC, 0:NC])
    for k, field in enumerate(fields):
        base = k * (NC + 16)
        cpl[base : base + 8, :] = jnp.zeros((8, NC), jnp.float32)
        cpl[base + NC + 8 : base + NC + 16, :] = jnp.zeros((8, NC), jnp.float32)
        cpl[base + 8 : base + NC + 8, :] = field
    each = NC // 2 // SPLIT
    for part in range(SPLIT):
        for odd, first in ((0, 4), (1, 9)):
            for k in range(2):
                for j in range(HELD):
                    rows = cpl[pl.ds(k * (NC + 16) + first + j + part * each * 2, each, 2), :]
                    packed[pl.ds(part * each * 4 * HELD + (odd * 2 + k) * HELD + j, each, 4 * HELD), :] = rows
        piece = pl.ds(part * each * 4 * HELD, each * 4 * HELD)
        leaving.append(copies.start(packed.at[piece], pack.at[piece]))
    for copy in leaving:
        copy.wait()


def coarse_kernel(recv, other, pack, cpl, packed, sems):
    index, par, _ = position()
    rows = 2 * HELD
    planes = recv.shape[0] // rows
    plane_at = lax.broadcasted_iota(jnp.int32, (planes, NC), 0)
    lane = lane_iota((planes, NC))

    def up(v):
        return pltpu.roll(v, planes - 1, 0)

    def down(v):
        return pltpu.roll(v, 1, 0)

    def row_of(field, n):
        if n >= 0:
            return recv[pl.ds(field * HELD + jnp.where(par == 0, 4 - n, n), planes, rows), :]
        return other[pl.ds(field * HELD + jnp.where(par == 0, -n - 1, 5 + n), planes, rows), :]

    u1 = {j: row_of(0, j) for j in range(-4, 5)}
    bc = {j: row_of(1, j) for j in range(-4, 5)}
    fr = {j: 0.125 * (bc[j] + bc[j + 1]) for j in range(-4, 4)}
    fz, fy, dg, iv = {}, {}, {}, {}
    for j in range(-3, 4):
        zn = jnp.where(plane_at == planes - 1, 0.0, up(bc[j]))
        zp = jnp.where(plane_at == 0, 0.0, down(bc[j]))
        yn = jnp.where(lane == NC - 1, 0.0, left(bc[j]))
        yp = jnp.where(lane == 0, 0.0, right(bc[j]))
        fz[j] = jnp.where(plane_at == planes - 1, 0.0, 0.125 * (bc[j] + zn))
        fy[j] = jnp.where(lane == NC - 1, 0.0, 0.125 * (bc[j] + yn))
        dg[j] = 0.75 * bc[j] + 0.125 * (zn + zp + yn + yp + bc[j - 1] + bc[j + 1])
        row = index + jnp.where(par == 0, -j, j)
        inside = (row >= 0) & (row < NC)
        iv[j] = jnp.where(inside, 1.0 / jnp.where(inside, dg[j], 1.0), 0.0)

    def off(v, j):
        total = fr[j] * v[j + 1] + fr[j - 1] * v[j - 1]
        total = total + fz[j] * up(v[j]) + down(fz[j] * v[j])
        return total + fy[j] * left(v[j]) + right(fy[j] * v[j])

    reach = 3
    res = {j: (CENTER - 1.0) * dg[j] * u1[j] + off(u1, j) for j in range(-reach, reach + 1)}
    step = u1
    total = u1[0]
    for k, (step_a, step_b) in enumerate(COARSE):
        step = {j: step_a * step[j] + step_b * iv[j] * res[j] for j in range(-reach, reach + 1)}
        total = total + step[0]
        reach -= 1
        res = {j: res[j] - dg[j] * step[j] + off(step, j) for j in range(-reach, reach + 1)}
    groups = lax.axis_size("grp")
    each = planes // groups
    column = jnp.sum(res[0].reshape(groups, each, NC), axis=1, keepdims=True)
    weight = jnp.sum(dg[0].reshape(groups, each, NC), axis=1, keepdims=True)
    lift = jnp.broadcast_to(column / weight, (groups, each, NC)).reshape(planes, NC)
    cpl[0:8, :] = jnp.zeros((8, NC), jnp.float32)
    cpl[planes + 8 : planes + 16, :] = jnp.zeros((8, NC), jnp.float32)
    cpl[8 : planes + 8, :] = total + lift
    for k in range(5):
        packed[pl.ds(k, planes, 5), :] = cpl[pl.ds(6 + k, planes), :]
    Copies(sems).start(packed, pack).wait()


def post_kernel(
    b, bs, bx, own, over, side, w, x5, r5,
    coef, fx, fy, fz, iv, dg, before, x2v, pw, r3, e4, r4, e5, half, wide, x5v, r5v, sems,
):
    _, par, _ = position()
    inner = 1 - par
    order = (par, inner)
    alive = outer_mask()
    copies = Copies(sems)
    source = (over.at[2], bx.at[par], bx.at[inner], b.at[par], b.at[inner], bs.at[par], bs.at[inner], side.at[3])
    earlier = (over.at[1], over.at[0], own.at[0], own.at[1], side.at[1], side.at[0])
    started = {}
    for p in range(8):
        started[p] = [fill(copies, source[p], coef, p)]
        if 1 <= p <= 6:
            started[p].append(copies.start(earlier[p - 1], before.at[p - 1]))
    x2_copy = copies.start(own.at[4:6], x2v)
    clear_pads(coef, range(8))
    clear_pads(fx, range(4))
    clear_pads(pw, range(8))
    clear_pads(e4, range(6))
    clear_pads(e5, range(4))
    spread = dot(w[...], 0.5 * pair_matrix(NC, N))
    for side in (0, 1):
        wide[side] = spread[:, side * NC : (side + 1) * NC]
    for k, planes in enumerate(((0,), (1, 2), (3, 4), (5, 6), (7,))):
        z = jnp.where(par == 0, k, 4 - k)
        for side in (0, 1):
            part = wide[side, pl.ds(z, NC, 5), :]
            half[pl.ds(0, NC, 2), :] = part
            half[pl.ds(1, NC, 2), :] = part
            for p in planes:
                pw[p, PAD : PAD + N, side * NC : (side + 1) * NC] = half[...]

    def arrived(planes):
        for p in planes:
            for copy in started[p]:
                copy.wait()

    arrived(range(3))
    clear_outside([(coef, 0), (coef, 1), (coef, 2)])

    @whole_planes
    def _(row):
        for k in range(6):
            p = k + 1
            if k > 0:
                arrived([p + 1])
            win = window(coef, p, row)
            ahead = pltpu.roll(win, win.shape[0] - 1, 0)
            mid = win[PAD : PAD + CH]
            lane = lane_iota(mid.shape)
            nxt = jnp.where(lane == N - 1, 0.0, left(mid))
            prv = jnp.where(lane == 0, 0.0, right(mid))
            under, over = at(coef, p - 1, row), at(coef, p + 1, row)
            around = (ahead[PAD : PAD + CH] + shifted(win, -1)) + (nxt + prv) + (under + over)
            diag = 6.0 * mid + around
            if k < 2:
                inv = alive * inverse(jnp.where(diag > 0.0, diag, 1.0))
            else:
                inv = inverse(diag)
            fxw = win + ahead
            fyc = jnp.where(lane == N - 1, 0.0, mid + nxt)
            below, above = mid + under, mid + over
            if 1 <= k <= 4:
                put(fx, k - 1, row, fxw[PAD : PAD + CH])
                fy[k - 1, pl.ds(row, CH), :] = fyc
                fz[k - 1, pl.ds(row, CH), :] = below
                iv[k - 1, pl.ds(row, CH), :] = inv
                if k == 4:
                    fz[4, pl.ds(row, CH), :] = above
            if k in (2, 3):
                dg[k - 2, pl.ds(row, CH), :] = diag
            v = window(pw, p, row)
            here = v[PAD : PAD + CH]
            total = fxw[PAD : PAD + CH] * shifted(v, 1) + shifted(fxw * v, -1)
            total = total + (fyc * left(here) + right(fyc * here))
            total = total + (below * at(pw, p - 1, row) + above * at(pw, p + 1, row))
            res = (before[k, pl.ds(row, CH), :] - diag * here) + total
            if 1 <= k <= 4:
                r3[k - 1, pl.ds(row, CH), :] = res
            put(e4, k, row, (1.0 / CENTER) * (inv * res))

    x2_copy.wait()
    step_a, step_b = FINE[0]

    def off(v, k, shift, row):
        win, f = window(v, k + shift, row), window(fx, k, row)
        here = win[PAD : PAD + CH]
        g = fy[k, pl.ds(row, CH), :]
        total = f[PAD : PAD + CH] * shifted(win, 1) + shifted(f * win, -1)
        total = total + (g * left(here) + right(g * here))
        total = total + fz[k, pl.ds(row, CH), :] * at(v, k + shift - 1, row)
        return total + fz[k + 1, pl.ds(row, CH), :] * at(v, k + shift + 1, row)

    @whole_planes
    def _(row):
        for k in range(4):
            res = off(e4, k, 1, row) + (1.0 - 1.0 / CENTER) * r3[k, pl.ds(row, CH), :]
            here = at(e4, k + 1, row)
            move = step_a * here + step_b * (iv[k, pl.ds(row, CH), :] * res)
            put(e5, k, row, move)
            if k in (1, 2):
                r4[k - 1, pl.ds(row, CH), :] = res
                x5v[k - 1, pl.ds(row, CH), :] = x2v[k - 1, pl.ds(row, CH), :] + 2.0 * (at(pw, k + 2, row) + (here + move))

    leaving = [copies.start(x5v.at[k], x5.at[order[k]]) for k in range(2)]

    @whole_planes
    def _(row):
        for k in (1, 2):
            res = r4[k - 1, pl.ds(row, CH), :] - dg[k - 1, pl.ds(row, CH), :] * at(e5, k, row)
            r5v[k - 1, pl.ds(row, CH), :] = res + off(e5, k, 0, row)
            leaving.append(copies.start(r5v.at[k - 1], r5.at[order[k - 1]]))

    for copy in leaving:
        copy.wait()


def call(kernel, outs, scratch, sems, cost, *operands, limit=24):
    return pl.pallas_call(
        kernel,
        out_shape=[jax.ShapeDtypeStruct(s, jnp.float32) for s, _ in outs],
        in_specs=[spec for _, spec in operands],
        out_specs=[spec for _, spec in outs],
        scratch_shapes=[pltpu.VMEM(s, jnp.float32) for s in scratch] + [pltpu.SemaphoreType.DMA((sems,))],
        compiler_params=pltpu.CompilerParams(vmem_limit_bytes=limit * 1024 * 1024),
        cost_estimate=pl.CostEstimate(flops=cost, bytes_accessed=cost, transcendentals=0),
    )(*(array for array, _ in operands))


def local(right_side, conductivity):
    total = lax.axis_size("grp") * lax.axis_size("slab")
    inside = [(i, i ^ 1) for i in range(total)]
    across = [(i, (i + 1) % total) for i in range(1, total, 2)] + [((i + 1) % total, i) for i in range(1, total, 2)]

    def swap(v):
        return lax.ppermute(v, AXES, inside)

    between = [pair for pair in across if abs(pair[0] - pair[1]) == 1]

    def cross(v, ends=True):
        return lax.ppermute(v, AXES, across if ends else between)

    def everywhere(v):
        rows = v.shape[0]
        return lax.all_to_all(v.reshape(rows, 1, NC), AXES, 0, 0, tiled=True).reshape(rows, NC)

    plane, padded = (N, N), (N + 2 * PAD, N)
    two = (2,) + plane
    g, b = right_side, conductivity
    bs = swap(b)
    bx = cross(b)
    gs = swap(g)
    (send,) = call(first_kernel, [(two, VM)], [(3,) + padded], 3, 1 << 20, (g, VM), (b, ANY), (bs, ANY))
    sx = cross(send, False)
    state, xa = call(
        ready_kernel,
        [((STATE,) + padded, VM), (plane, VM)],
        [(6,) + padded, (3,) + plane, (8,) + padded, (3 * N, N), (3 * N, NC)],
        9,
        6 << 20,
        (g, ANY), (gs, ANY), (b, ANY), (bs, ANY), (bx, ANY), (send, ANY),
    )
    xi = swap(xa)
    pack, side = call(
        pre_kernel,
        [((2 * HELD * total, NC), HBM), ((6,) + plane, HBM)],
        [(1,) + padded, (1,) + padded, plane, plane, (2 * (NC + 16), NC), (2 * HELD * total, NC), (4,) + plane, plane],
        5 + SPLIT,
        6 << 20,
        (bs, ANY), (bx, ANY), (state, VM), (sx, VM), (xi, VM),
    )
    from_over = cross(side, False)
    from_side = swap(side)
    own = swap(from_side)
    got = everywhere(pack)
    (back,) = call(
        coarse_kernel,
        [((5 * NC, NC), HBM)],
        [(total + 16, NC), (5 * NC, NC)],
        1,
        4 << 20,
        (got, VM), (swap(got), VM),
    )
    w = everywhere(back)
    x5, r5 = call(
        post_kernel,
        [(two, HBM), (two, HBM)],
        [(8,) + padded, (4,) + padded, (4,) + plane, (5,) + plane, (4,) + plane, two, (6,) + plane, two, (8,) + padded, (4,) + plane, (6,) + padded, two, (4,) + padded, (N, NC), (2, 5 * NC, NC), two, two],
        20,
        8 << 20,
        (b, ANY), (bs, ANY), (bx, ANY), (own, ANY), (from_over, ANY), (from_side, ANY), (w, VM),
    )
    return x5, r5


def solution(mesh):
    spec = P(AXES, None, None)
    return jax.shard_map(
        local, mesh=mesh, in_specs=(spec, spec), out_specs=(spec, spec), check_vma=False
    )
```

```python
import functools

import jax
import jax.numpy as jnp
from jax import lax
from jax.experimental import pallas as pl
from jax.experimental.pallas import tpu as pltpu
from jax.sharding import PartitionSpec as P

KF = 2
KC = 4

LOWER = 0.25
UPPER = 2.0
CENTER = (UPPER + LOWER) / 2.0
HALF = (UPPER - LOWER) / 2.0
RATIO = CENTER / HALF

AXES = ("grp", "slab")
N = 256
NC = 128
PAD = 8
CH = 256
VM = pl.BlockSpec(memory_space=pltpu.VMEM)
ANY = pl.BlockSpec(memory_space=pl.ANY)
HBM = pl.BlockSpec(memory_space=pltpu.HBM)


def chebyshev_factors(count):
    rho = 1.0 / RATIO
    found = []
    for _ in range(count - 1):
        new = 1.0 / (2.0 * RATIO - rho)
        found.append((new * rho, 2.0 * new / HALF))
        rho = new
    return found


FINE = chebyshev_factors(KF)
COARSE = chebyshev_factors(KC)


def position():
    grp, slab = lax.axis_index("grp"), lax.axis_index("slab")
    slabs = lax.axis_size("slab")
    total = lax.axis_size("grp") * slabs
    index = grp * slabs + slab
    return index, lax.rem(slab, 2), total


def outer_mask():
    index, _, total = position()
    return jnp.where((index == 0) | (index == total - 1), 0.0, 1.0).astype(jnp.float32)


def lane_iota(shape):
    return lax.broadcasted_iota(jnp.int32, shape, len(shape) - 1)


def rows_of(chunk):
    return pl.multiple_of(chunk * CH, CH)


def whole_planes(body):
    assert CH == N
    body(0)


def at(ref, plane, row):
    return ref[plane, pl.ds(row + PAD, CH), :]


def window(ref, plane, row):
    return ref[plane, pl.ds(row, CH + 2 * PAD), :]


def shifted(win, by):
    return pltpu.roll(win, (-by) % win.shape[0], 0)[PAD : PAD + CH]


def put(ref, plane, row, value):
    ref[plane, pl.ds(row + PAD, CH), :] = value


def clear_pads(ref, planes):
    for p in planes:
        ref[p, 0:PAD, :] = jnp.zeros((PAD, N), jnp.float32)
        ref[p, PAD + N : 2 * PAD + N, :] = jnp.zeros((PAD, N), jnp.float32)


def left(v):
    return pltpu.roll(v, v.shape[-1] - 1, v.ndim - 1)


def right(v):
    return pltpu.roll(v, 1, v.ndim - 1)


class Copies:
    def __init__(self, sems):
        self.sems, self.used = sems, 0

    def start(self, source, target):
        copy = pltpu.make_async_copy(source, target, self.sems.at[self.used])
        self.used += 1
        copy.start()
        return copy

    def again(self, source, target):
        pltpu.make_async_copy(source, target, self.sems.at[self.used]).start()

    def handle(self, source, target):
        copy = pltpu.make_async_copy(source, target, self.sems.at[self.used])
        self.used += 1
        return copy


def clear_outside(refs):
    @pl.when(outer_mask() == 0.0)
    def _():
        for ref, plane in refs:
            ref[plane] = jnp.zeros(ref.shape[1:], jnp.float32)


def fill(copies, source, ref, plane):
    return copies.start(source, ref.at[plane, PAD : PAD + N, :])


def lateral(row, here, fx, fy):
    v = window(*here, row)
    f = window(*fx, row)
    mid = v[PAD : PAD + CH]
    g = at(*fy, row)
    total = f[PAD : PAD + CH] * shifted(v, 1) + shifted(f * v, -1)
    return total + (g * left(mid) + right(g * mid))


def inverse(v):
    return 1.0 / v


def prepare(coef, p, row):
    win = window(coef, p, row)
    b = win[PAD : PAD + CH]
    down = shifted(win, 1)
    lane = lane_iota(b.shape)
    nxt = jnp.where(lane == N - 1, 0.0, left(b))
    prv = jnp.where(lane == 0, 0.0, right(b))
    over = at(coef, p + 1, row)
    around = (down + shifted(win, -1)) + (nxt + prv) + (at(coef, p - 1, row) + over)
    fy = jnp.where(lane == N - 1, 0.0, 0.5 * (b + nxt))
    return 3.0 * b + 0.5 * around, 0.5 * (b + down), fy, 0.5 * (b + over)


def pair_matrix(rows, cols):
    i = lax.broadcasted_iota(jnp.int32, (rows, cols), 0)
    j = lax.broadcasted_iota(jnp.int32, (rows, cols), 1)
    same = i // 2 == j if rows > cols else j // 2 == i
    return jnp.where(same, 1.0, 0.0).astype(jnp.bfloat16)


def dot(x, y):
    total = None
    for _ in range(3):
        part = x.astype(jnp.bfloat16)
        x = x - part.astype(jnp.float32)
        term = jnp.dot(part, y, preferred_element_type=jnp.float32)
        total = term if total is None else total + term
    return total


def first_kernel(g, b, bs, out, coef, sems):
    _, par, _ = position()
    inner = 1 - par
    copies = Copies(sems)
    started = [fill(copies, bs.at[par], coef, 2), fill(copies, b.at[inner], coef, 1), fill(copies, b.at[par], coef, 0)]
    clear_pads(coef, [1])
    for copy in started:
        copy.wait()

    @pl.loop(0, N // CH)
    def _(chunk):
        row = rows_of(chunk)
        diag = prepare(coef, 1, row)[0]
        out[0, pl.ds(row, CH), :] = g[par, pl.ds(row, CH), :]
        out[1, pl.ds(row, CH), :] = g[inner, pl.ds(row, CH), :] / (CENTER * diag)


(FXO, FXA, FYO, FYA, IVO, IVA, IVI, Z0, Z1, Z2, Z3, Z4, XA, XI, PA, PI, DA, EB, PB, X2B, COARSE_AT, STATE) = range(22)


def ready_kernel(g, gs, b, bs, bx, sent, state, xa, coef, rhs, mine, red, cpl, sems):
    del sent
    _, par, _ = position()
    inner = 1 - par
    alive = outer_mask()
    O2, O1, A, B, I1, I2 = range(6)
    FXB, FXI, FYB, FYI, IVB, DB, XB, RB = range(8)
    copies = Copies(sems)
    source = {O2: bx.at[par], O1: bx.at[inner], A: b.at[par], B: b.at[inner], I1: bs.at[par], I2: bs.at[inner]}
    given = [g.at[par], g.at[inner], gs.at[par]]
    started = [fill(copies, ref, coef, p) for p, ref in source.items()]
    started += [copies.start(ref, rhs.at[k]) for k, ref in enumerate(given)]
    clear_pads(coef, range(6))
    clear_pads(state, (FXO, FXA, XA, XI, EB))
    clear_pads(mine, (FXB, FXI, XB))
    for copy in started:
        copy.wait()
    clear_outside([(coef, O2), (coef, O1)])
    keep = {
        O1: ((state, FXO), (state, FYO), (state, IVO), (state, Z1), None, None),
        A: ((state, FXA), (state, FYA), (state, IVA), (state, Z2), (state, DA), (state, XA)),
        B: ((mine, FXB), (mine, FYB), (mine, IVB), (state, Z3), (mine, DB), (mine, XB)),
        I1: ((mine, FXI), (mine, FYI), (state, IVI), (state, Z4), None, (state, XI)),
    }

    @pl.loop(0, N // CH)
    def _(chunk):
        row = rows_of(chunk)
        put(state, Z0, row, 0.5 * (at(coef, O2, row) + at(coef, O1, row)))
        for k, p in enumerate((O1, A, B, I1)):
            diag, fx, fy, fz = prepare(coef, p, row)
            to_fx, to_fy, to_iv, to_fz, to_dg, to_x = keep[p]
            inv = 1.0 / diag
            if p == O1:
                inv = inv * alive
            put(*to_fx, row, fx)
            put(*to_fy, row, fy)
            put(*to_iv, row, inv)
            put(*to_fz, row, fz)
            if to_dg:
                put(*to_dg, row, diag)
            if to_x:
                x1 = rhs[k - 1, pl.ds(row, CH), :] * inv * (1.0 / CENTER)
                put(*to_x, row, x1)
                if p == A:
                    xa[pl.ds(row, CH), :] = x1
        for k, (p, q) in enumerate(((A, B), (O1, O2), (I1, I2))):
            red[pl.ds(k * N + row, CH), :] = at(coef, p, row) + at(coef, q, row)

    step_a, step_b = FINE[0]
    left_over = 1.0 - 1.0 / CENTER

    @pl.loop(0, N // CH)
    def _(chunk):
        row = rows_of(chunk)
        here = at(mine, XB, row)
        part = lateral(row, (state, XA), (state, FXA), (state, FYA)) + at(state, Z2, row) * here
        put(state, PA, row, part + left_over * rhs[0, pl.ds(row, CH), :])
        part = lateral(row, (state, XI), (mine, FXI), (mine, FYI)) + at(state, Z3, row) * here
        put(state, PI, row, part + left_over * rhs[2, pl.ds(row, CH), :])
        res = lateral(row, (mine, XB), (mine, FXB), (mine, FYB)) + left_over * rhs[1, pl.ds(row, CH), :]
        res = res + (at(state, Z2, row) * at(state, XA, row) + at(state, Z3, row) * at(state, XI, row))
        move = step_a * here + step_b * (at(mine, IVB, row) * res)
        put(state, EB, row, move)
        put(state, X2B, row, here + move)
        put(mine, RB, row, res - at(mine, DB, row) * move)

    @pl.loop(0, N // CH)
    def _(chunk):
        row = rows_of(chunk)
        put(state, PB, row, at(mine, RB, row) + lateral(row, (state, EB), (mine, FXB), (mine, FYB)))

    cpl[...] = dot(red[...], pair_matrix(N, NC))
    bc, bo, bi = (
        0.125 * (cpl[pl.ds(k * N, NC, 2), :] + cpl[pl.ds(k * N + 1, NC, 2), :]) for k in range(3)
    )
    row_at = lax.broadcasted_iota(jnp.int32, (NC, NC), 0)
    lane = lane_iota((NC, NC))
    around = (
        jnp.where(lane == NC - 1, 0.0, left(bc))
        + jnp.where(lane == 0, 0.0, right(bc))
        + jnp.where(row_at == NC - 1, 0.0, pltpu.roll(bc, NC - 1, 0))
        + jnp.where(row_at == 0, 0.0, pltpu.roll(bc, 1, 0))
    )
    diag = 0.25 * (3.0 * bc + 0.5 * (around + bo + bi))
    state[COARSE_AT, 0:NC, 0:NC] = bc
    state[COARSE_AT, 0:NC, NC:N] = 1.0 / (CENTER * diag)


SPLIT = 2
HELD = 5


def pre_kernel(bs, bx, state, sx, xi, pack, side, x1, e2, part, red, cpl, packed, own, zeros, sems):
    _, par, _ = position()
    inner = 1 - par
    copies = Copies(sems)
    leaving = [copies.start(bs.at[par], side.at[2])]
    beyond = outer_mask() == 0.0

    @pl.when(beyond)
    def _():
        zeros[...] = jnp.zeros((N, N), jnp.float32)
        copies.again(zeros, side.at[3])

    @pl.when(jnp.logical_not(beyond))
    def _():
        copies.again(bx.at[inner], side.at[3])

    leaving.append(copies.handle(bx.at[inner], side.at[3]))
    clear_pads(x1, [0])
    clear_pads(e2, [0])

    @pl.loop(0, N // CH)
    def _(chunk):
        row = rows_of(chunk)
        put(x1, 0, row, sx[0, pl.ds(row, CH), :] * at(state, IVO, row) * (1.0 / CENTER))

    step_a, step_b = FINE[0]

    @pl.loop(0, N // CH)
    def _(chunk):
        row = rows_of(chunk)
        here = at(x1, 0, row)
        res = lateral(row, (x1, 0), (state, FXO), (state, FYO)) + (1.0 - 1.0 / CENTER) * sx[0, pl.ds(row, CH), :]
        res = res + (at(state, Z0, row) * sx[1, pl.ds(row, CH), :] + at(state, Z1, row) * at(state, XA, row))
        e2o = step_a * here + step_b * (at(state, IVO, row) * res)
        res = at(state, PA, row) + at(state, Z1, row) * here
        e2a = step_a * at(state, XA, row) + step_b * (at(state, IVA, row) * res)
        put(e2, 0, row, e2a)
        own[2, pl.ds(row, CH), :] = at(state, XA, row) + e2a
        own[3, pl.ds(row, CH), :] = at(state, X2B, row)
        res = res - at(state, DA, row) * e2a
        part[pl.ds(row, CH), :] = res + (at(state, Z1, row) * e2o + at(state, Z2, row) * at(state, EB, row))
        res = at(state, PI, row) + at(state, Z4, row) * xi[pl.ds(row, CH), :]
        e2i = step_a * at(state, XI, row) + step_b * (at(state, IVI, row) * res)
        own[1, pl.ds(row, CH), :] = at(state, PB, row) + (at(state, Z2, row) * e2a + at(state, Z3, row) * e2i)

    leaving += [copies.start(own.at[1], side.at[1]), copies.start(own.at[2:4], side.at[4:6])]

    @pl.loop(0, N // CH)
    def _(chunk):
        row = rows_of(chunk)
        res = part[pl.ds(row, CH), :] + lateral(row, (e2, 0), (state, FXA), (state, FYA))
        own[0, pl.ds(row, CH), :] = res
        red[pl.ds(row, CH), :] = res + own[1, pl.ds(row, CH), :]

    leaving.append(copies.start(own.at[0], side.at[0]))
    cpl[0:N, :] = dot(red[...], pair_matrix(N, NC))
    rc = 0.125 * (cpl[pl.ds(0, NC, 2), :] + cpl[pl.ds(1, NC, 2), :])
    fields = (rc * state[COARSE_AT, 0:NC, NC:N], state[COARSE_AT, 0:NC, 0:NC])
    for k, field in enumerate(fields):
        base = k * (NC + 16)
        cpl[base : base + 8, :] = jnp.zeros((8, NC), jnp.float32)
        cpl[base + NC + 8 : base + NC + 16, :] = jnp.zeros((8, NC), jnp.float32)
        cpl[base + 8 : base + NC + 8, :] = field
    each = NC // 2 // SPLIT
    for part in range(SPLIT):
        for odd, first in ((0, 4), (1, 9)):
            for k in range(2):
                for j in range(HELD):
                    rows = cpl[pl.ds(k * (NC + 16) + first + j + part * each * 2, each, 2), :]
                    packed[pl.ds(part * each * 4 * HELD + (odd * 2 + k) * HELD + j, each, 4 * HELD), :] = rows
        piece = pl.ds(part * each * 4 * HELD, each * 4 * HELD)
        leaving.append(copies.start(packed.at[piece], pack.at[piece]))
    for copy in leaving:
        copy.wait()


def coarse_kernel(recv, other, pack, cpl, packed, sems):
    index, par, _ = position()
    rows = 2 * HELD
    planes = recv.shape[0] // rows
    plane_at = lax.broadcasted_iota(jnp.int32, (planes, NC), 0)
    lane = lane_iota((planes, NC))

    def up(v):
        return pltpu.roll(v, planes - 1, 0)

    def down(v):
        return pltpu.roll(v, 1, 0)

    def row_of(field, n):
        if n >= 0:
            return recv[pl.ds(field * HELD + jnp.where(par == 0, 4 - n, n), planes, rows), :]
        return other[pl.ds(field * HELD + jnp.where(par == 0, -n - 1, 5 + n), planes, rows), :]

    u1 = {j: row_of(0, j) for j in range(-4, 5)}
    bc = {j: row_of(1, j) for j in range(-4, 5)}
    fr = {j: 0.125 * (bc[j] + bc[j + 1]) for j in range(-4, 4)}
    fz, fy, dg, iv = {}, {}, {}, {}
    for j in range(-3, 4):
        zn = jnp.where(plane_at == planes - 1, 0.0, up(bc[j]))
        zp = jnp.where(plane_at == 0, 0.0, down(bc[j]))
        yn = jnp.where(lane == NC - 1, 0.0, left(bc[j]))
        yp = jnp.where(lane == 0, 0.0, right(bc[j]))
        fz[j] = jnp.where(plane_at == planes - 1, 0.0, 0.125 * (bc[j] + zn))
        fy[j] = jnp.where(lane == NC - 1, 0.0, 0.125 * (bc[j] + yn))
        dg[j] = 0.75 * bc[j] + 0.125 * (zn + zp + yn + yp + bc[j - 1] + bc[j + 1])
        row = index + jnp.where(par == 0, -j, j)
        inside = (row >= 0) & (row < NC)
        iv[j] = jnp.where(inside, 1.0 / jnp.where(inside, dg[j], 1.0), 0.0)

    def off(v, j):
        total = fr[j] * v[j + 1] + fr[j - 1] * v[j - 1]
        total = total + fz[j] * up(v[j]) + down(fz[j] * v[j])
        return total + fy[j] * left(v[j]) + right(fy[j] * v[j])

    reach = 3
    res = {j: (CENTER - 1.0) * dg[j] * u1[j] + off(u1, j) for j in range(-reach, reach + 1)}
    step = u1
    total = u1[0]
    for k, (step_a, step_b) in enumerate(COARSE):
        step = {j: step_a * step[j] + step_b * iv[j] * res[j] for j in range(-reach, reach + 1)}
        total = total + step[0]
        reach -= 1
        res = {j: res[j] - dg[j] * step[j] + off(step, j) for j in range(-reach, reach + 1)}
    groups = lax.axis_size("grp")
    each = planes // groups
    column = jnp.sum(res[0].reshape(groups, each, NC), axis=1, keepdims=True)
    weight = jnp.sum(dg[0].reshape(groups, each, NC), axis=1, keepdims=True)
    lift = jnp.broadcast_to(column / weight, (groups, each, NC)).reshape(planes, NC)
    cpl[0:8, :] = jnp.zeros((8, NC), jnp.float32)
    cpl[planes + 8 : planes + 16, :] = jnp.zeros((8, NC), jnp.float32)
    cpl[8 : planes + 8, :] = total + lift
    for k in range(5):
        packed[pl.ds(k, planes, 5), :] = cpl[pl.ds(6 + k, planes), :]
    Copies(sems).start(packed, pack).wait()


def post_kernel(
    b, bs, bx, own, over, side, w, x5, r5,
    coef, fx, fy, fz, iv, dg, before, x2v, pw, r3, e4, r4, e5, half, wide, x5v, r5v, sems,
):
    _, par, _ = position()
    inner = 1 - par
    order = (par, inner)
    alive = outer_mask()
    copies = Copies(sems)
    source = (over.at[2], bx.at[par], bx.at[inner], b.at[par], b.at[inner], bs.at[par], bs.at[inner], side.at[3])
    earlier = (over.at[1], over.at[0], own.at[0], own.at[1], side.at[1], side.at[0])
    started = {}
    for p in range(8):
        started[p] = [fill(copies, source[p], coef, p)]
        if 1 <= p <= 6:
            started[p].append(copies.start(earlier[p - 1], before.at[p - 1]))
    x2_copy = copies.start(own.at[4:6], x2v)
    clear_pads(coef, range(8))
    clear_pads(fx, range(4))
    clear_pads(pw, range(5))
    clear_pads(e4, range(6))
    clear_pads(e5, range(4))
    spread = dot(w[...], 0.5 * pair_matrix(NC, N))
    for side in (0, 1):
        wide[side] = spread[:, side * NC : (side + 1) * NC]
    held = (0, 1, 1, 2, 2, 3, 3, 4)
    for k in range(5):
        z = jnp.where(par == 0, k, 4 - k)
        for side in (0, 1):
            part = wide[side, pl.ds(z, NC, 5), :]
            half[pl.ds(0, NC, 2), :] = part
            half[pl.ds(1, NC, 2), :] = part
            pw[k, PAD : PAD + N, side * NC : (side + 1) * NC] = half[...]

    def arrived(planes):
        for p in planes:
            for copy in started[p]:
                copy.wait()

    arrived(range(3))
    clear_outside([(coef, 0), (coef, 1), (coef, 2)])

    @whole_planes
    def _(row):
        for k in range(6):
            p = k + 1
            if k > 0:
                arrived([p + 1])
            win = window(coef, p, row)
            ahead = pltpu.roll(win, win.shape[0] - 1, 0)
            mid = win[PAD : PAD + CH]
            lane = lane_iota(mid.shape)
            nxt = jnp.where(lane == N - 1, 0.0, left(mid))
            prv = jnp.where(lane == 0, 0.0, right(mid))
            under, over = at(coef, p - 1, row), at(coef, p + 1, row)
            around = (ahead[PAD : PAD + CH] + shifted(win, -1)) + (nxt + prv) + (under + over)
            diag = 6.0 * mid + around
            if k < 2:
                inv = alive * inverse(jnp.where(diag > 0.0, diag, 1.0))
            else:
                inv = inverse(diag)
            fxw = win + ahead
            fyc = jnp.where(lane == N - 1, 0.0, mid + nxt)
            below, above = mid + under, mid + over
            if 1 <= k <= 4:
                put(fx, k - 1, row, fxw[PAD : PAD + CH])
                fy[k - 1, pl.ds(row, CH), :] = fyc
                fz[k - 1, pl.ds(row, CH), :] = below
                iv[k - 1, pl.ds(row, CH), :] = inv
                if k == 4:
                    fz[4, pl.ds(row, CH), :] = above
            if k in (2, 3):
                dg[k - 2, pl.ds(row, CH), :] = diag
            v = window(pw, held[p], row)
            here = v[PAD : PAD + CH]
            total = fxw[PAD : PAD + CH] * shifted(v, 1) + shifted(fxw * v, -1)
            total = total + (fyc * left(here) + right(fyc * here))
            total = total + (below * at(pw, held[p - 1], row) + above * at(pw, held[p + 1], row))
            res = (before[k, pl.ds(row, CH), :] - diag * here) + total
            if 1 <= k <= 4:
                r3[k - 1, pl.ds(row, CH), :] = res
            put(e4, k, row, (1.0 / CENTER) * (inv * res))

    x2_copy.wait()
    step_a, step_b = FINE[0]

    def off(v, k, shift, row):
        win, f = window(v, k + shift, row), window(fx, k, row)
        here = win[PAD : PAD + CH]
        g = fy[k, pl.ds(row, CH), :]
        total = f[PAD : PAD + CH] * shifted(win, 1) + shifted(f * win, -1)
        total = total + (g * left(here) + right(g * here))
        total = total + fz[k, pl.ds(row, CH), :] * at(v, k + shift - 1, row)
        return total + fz[k + 1, pl.ds(row, CH), :] * at(v, k + shift + 1, row)

    @whole_planes
    def _(row):
        for k in range(4):
            res = off(e4, k, 1, row) + (1.0 - 1.0 / CENTER) * r3[k, pl.ds(row, CH), :]
            here = at(e4, k + 1, row)
            move = step_a * here + step_b * (iv[k, pl.ds(row, CH), :] * res)
            put(e5, k, row, move)
            if k in (1, 2):
                r4[k - 1, pl.ds(row, CH), :] = res
                x5v[k - 1, pl.ds(row, CH), :] = x2v[k - 1, pl.ds(row, CH), :] + 2.0 * (at(pw, held[k + 2], row) + (here + move))

    leaving = [copies.start(x5v.at[k], x5.at[order[k]]) for k in range(2)]

    @whole_planes
    def _(row):
        for k in (1, 2):
            res = r4[k - 1, pl.ds(row, CH), :] - dg[k - 1, pl.ds(row, CH), :] * at(e5, k, row)
            r5v[k - 1, pl.ds(row, CH), :] = res + off(e5, k, 0, row)
            leaving.append(copies.start(r5v.at[k - 1], r5.at[order[k - 1]]))

    for copy in leaving:
        copy.wait()


def call(kernel, outs, scratch, sems, cost, *operands, limit=24):
    return pl.pallas_call(
        kernel,
        out_shape=[jax.ShapeDtypeStruct(s, jnp.float32) for s, _ in outs],
        in_specs=[spec for _, spec in operands],
        out_specs=[spec for _, spec in outs],
        scratch_shapes=[pltpu.VMEM(s, jnp.float32) for s in scratch] + [pltpu.SemaphoreType.DMA((sems,))],
        compiler_params=pltpu.CompilerParams(vmem_limit_bytes=limit * 1024 * 1024),
        cost_estimate=pl.CostEstimate(flops=cost, bytes_accessed=cost, transcendentals=0),
    )(*(array for array, _ in operands))


def local(right_side, conductivity):
    total = lax.axis_size("grp") * lax.axis_size("slab")
    inside = [(i, i ^ 1) for i in range(total)]
    across = [(i, (i + 1) % total) for i in range(1, total, 2)] + [((i + 1) % total, i) for i in range(1, total, 2)]

    def swap(v):
        return lax.ppermute(v, AXES, inside)

    between = [pair for pair in across if abs(pair[0] - pair[1]) == 1]

    def cross(v, ends=True):
        return lax.ppermute(v, AXES, across if ends else between)

    def everywhere(v):
        rows = v.shape[0]
        return lax.all_to_all(v.reshape(rows, 1, NC), AXES, 0, 0, tiled=True).reshape(rows, NC)

    plane, padded = (N, N), (N + 2 * PAD, N)
    two = (2,) + plane
    g, b = right_side, conductivity
    bs = swap(b)
    bx = cross(b)
    gs = swap(g)
    (send,) = call(first_kernel, [(two, VM)], [(3,) + padded], 3, 1 << 20, (g, VM), (b, ANY), (bs, ANY))
    sx = cross(send, False)
    state, xa = call(
        ready_kernel,
        [((STATE,) + padded, VM), (plane, VM)],
        [(6,) + padded, (3,) + plane, (8,) + padded, (3 * N, N), (3 * N, NC)],
        9,
        6 << 20,
        (g, ANY), (gs, ANY), (b, ANY), (bs, ANY), (bx, ANY), (send, ANY),
    )
    xi = swap(xa)
    pack, side = call(
        pre_kernel,
        [((2 * HELD * total, NC), HBM), ((6,) + plane, HBM)],
        [(1,) + padded, (1,) + padded, plane, plane, (2 * (NC + 16), NC), (2 * HELD * total, NC), (4,) + plane, plane],
        5 + SPLIT,
        6 << 20,
        (bs, ANY), (bx, ANY), (state, VM), (sx, VM), (xi, VM),
    )
    from_over = cross(side, False)
    from_side = swap(side)
    own = swap(from_side)
    got = everywhere(pack)
    (back,) = call(
        coarse_kernel,
        [((5 * NC, NC), HBM)],
        [(total + 16, NC), (5 * NC, NC)],
        1,
        4 << 20,
        (got, VM), (swap(got), VM),
    )
    w = everywhere(back)
    x5, r5 = call(
        post_kernel,
        [(two, HBM), (two, HBM)],
        [(8,) + padded, (4,) + padded, (4,) + plane, (5,) + plane, (4,) + plane, two, (6,) + plane, two, (5,) + padded, (4,) + plane, (6,) + padded, two, (4,) + padded, (N, NC), (2, 5 * NC, NC), two, two],
        20,
        8 << 20,
        (b, ANY), (bs, ANY), (bx, ANY), (own, ANY), (from_over, ANY), (from_side, ANY), (w, VM),
    )
    return x5, r5


def solution(mesh):
    spec = P(AXES, None, None)
    return jax.shard_map(
        local, mesh=mesh, in_specs=(spec, spec), out_specs=(spec, spec), check_vma=False
    )
```

```python
import functools

import jax
import jax.numpy as jnp
from jax import lax
from jax.experimental import pallas as pl
from jax.experimental.pallas import tpu as pltpu
from jax.sharding import PartitionSpec as P

KF = 2
KC = 4

LOWER = 0.25
UPPER = 2.0
CENTER = (UPPER + LOWER) / 2.0
HALF = (UPPER - LOWER) / 2.0
RATIO = CENTER / HALF

AXES = ("grp", "slab")
N = 256
NC = 128
PAD = 8
CH = 256
VM = pl.BlockSpec(memory_space=pltpu.VMEM)
ANY = pl.BlockSpec(memory_space=pl.ANY)
HBM = pl.BlockSpec(memory_space=pltpu.HBM)


def chebyshev_factors(count):
    rho = 1.0 / RATIO
    found = []
    for _ in range(count - 1):
        new = 1.0 / (2.0 * RATIO - rho)
        found.append((new * rho, 2.0 * new / HALF))
        rho = new
    return found


FINE = chebyshev_factors(KF)
COARSE = chebyshev_factors(KC)


def position():
    grp, slab = lax.axis_index("grp"), lax.axis_index("slab")
    slabs = lax.axis_size("slab")
    total = lax.axis_size("grp") * slabs
    index = grp * slabs + slab
    return index, lax.rem(slab, 2), total


def outer_mask():
    index, _, total = position()
    return jnp.where((index == 0) | (index == total - 1), 0.0, 1.0).astype(jnp.float32)


def lane_iota(shape):
    return lax.broadcasted_iota(jnp.int32, shape, len(shape) - 1)


def rows_of(chunk):
    return pl.multiple_of(chunk * CH, CH)


def whole_planes(body):
    assert CH == N
    body(0)


def at(ref, plane, row):
    return ref[plane, pl.ds(row + PAD, CH), :]


def window(ref, plane, row):
    return ref[plane, pl.ds(row, CH + 2 * PAD), :]


def shifted(win, by):
    return pltpu.roll(win, (-by) % win.shape[0], 0)[PAD : PAD + CH]


def put(ref, plane, row, value):
    ref[plane, pl.ds(row + PAD, CH), :] = value


def clear_pads(ref, planes):
    for p in planes:
        ref[p, 0:PAD, :] = jnp.zeros((PAD, N), jnp.float32)
        ref[p, PAD + N : 2 * PAD + N, :] = jnp.zeros((PAD, N), jnp.float32)


def left(v):
    return pltpu.roll(v, v.shape[-1] - 1, v.ndim - 1)


def right(v):
    return pltpu.roll(v, 1, v.ndim - 1)


class Copies:
    def __init__(self, sems):
        self.sems, self.used = sems, 0

    def start(self, source, target):
        copy = pltpu.make_async_copy(source, target, self.sems.at[self.used])
        self.used += 1
        copy.start()
        return copy

    def again(self, source, target):
        pltpu.make_async_copy(source, target, self.sems.at[self.used]).start()

    def handle(self, source, target):
        copy = pltpu.make_async_copy(source, target, self.sems.at[self.used])
        self.used += 1
        return copy


def clear_outside(refs):
    @pl.when(outer_mask() == 0.0)
    def _():
        for ref, plane in refs:
            ref[plane] = jnp.zeros(ref.shape[1:], jnp.float32)


def fill(copies, source, ref, plane):
    return copies.start(source, ref.at[plane, PAD : PAD + N, :])


def lateral(row, here, fx, fy):
    v = window(*here, row)
    f = window(*fx, row)
    mid = v[PAD : PAD + CH]
    g = at(*fy, row)
    total = f[PAD : PAD + CH] * shifted(v, 1) + shifted(f * v, -1)
    return total + (g * left(mid) + right(g * mid))


def inverse(v):
    return 1.0 / v


def prepare(coef, p, row):
    win = window(coef, p, row)
    b = win[PAD : PAD + CH]
    down = shifted(win, 1)
    lane = lane_iota(b.shape)
    nxt = jnp.where(lane == N - 1, 0.0, left(b))
    prv = jnp.where(lane == 0, 0.0, right(b))
    over = at(coef, p + 1, row)
    around = (down + shifted(win, -1)) + (nxt + prv) + (at(coef, p - 1, row) + over)
    fy = jnp.where(lane == N - 1, 0.0, 0.5 * (b + nxt))
    return 3.0 * b + 0.5 * around, 0.5 * (b + down), fy, 0.5 * (b + over)


def pair_matrix(rows, cols):
    i = lax.broadcasted_iota(jnp.int32, (rows, cols), 0)
    j = lax.broadcasted_iota(jnp.int32, (rows, cols), 1)
    same = i // 2 == j if rows > cols else j // 2 == i
    return jnp.where(same, 1.0, 0.0).astype(jnp.bfloat16)


def dot(x, y):
    total = None
    for _ in range(3):
        part = x.astype(jnp.bfloat16)
        x = x - part.astype(jnp.float32)
        term = jnp.dot(part, y, preferred_element_type=jnp.float32)
        total = term if total is None else total + term
    return total


def first_kernel(g, b, bs, out, coef, sems):
    _, par, _ = position()
    inner = 1 - par
    copies = Copies(sems)
    started = [fill(copies, bs.at[par], coef, 2), fill(copies, b.at[inner], coef, 1), fill(copies, b.at[par], coef, 0)]
    clear_pads(coef, [1])
    for copy in started:
        copy.wait()

    @pl.loop(0, N // CH)
    def _(chunk):
        row = rows_of(chunk)
        diag = prepare(coef, 1, row)[0]
        out[0, pl.ds(row, CH), :] = g[par, pl.ds(row, CH), :]
        out[1, pl.ds(row, CH), :] = g[inner, pl.ds(row, CH), :] / (CENTER * diag)


(FXO, FXA, FYO, FYA, IVO, IVA, IVI, Z0, Z1, Z2, Z3, Z4, XA, XI, PA, PI, DA, EB, PB, X2B, COARSE_AT, STATE) = range(22)


def ready_kernel(g, gs, b, bs, bx, sent, state, xa, coef, rhs, mine, red, cpl, sems):
    del sent
    _, par, _ = position()
    inner = 1 - par
    alive = outer_mask()
    O2, O1, A, B, I1, I2 = range(6)
    FXB, FXI, FYB, FYI, IVB, DB, XB, RB = range(8)
    copies = Copies(sems)
    source = {O2: bx.at[par], O1: bx.at[inner], A: b.at[par], B: b.at[inner], I1: bs.at[par], I2: bs.at[inner]}
    given = [g.at[par], g.at[inner], gs.at[par]]
    started = [fill(copies, ref, coef, p) for p, ref in source.items()]
    started += [copies.start(ref, rhs.at[k]) for k, ref in enumerate(given)]
    clear_pads(coef, range(6))
    clear_pads(state, (FXO, FXA, XA, XI, EB))
    clear_pads(mine, (FXB, FXI, XB))
    for copy in started:
        copy.wait()
    clear_outside([(coef, O2), (coef, O1)])
    keep = {
        O1: ((state, FXO), (state, FYO), (state, IVO), (state, Z1), None, None),
        A: ((state, FXA), (state, FYA), (state, IVA), (state, Z2), (state, DA), (state, XA)),
        B: ((mine, FXB), (mine, FYB), (mine, IVB), (state, Z3), (mine, DB), (mine, XB)),
        I1: ((mine, FXI), (mine, FYI), (state, IVI), (state, Z4), None, (state, XI)),
    }

    @pl.loop(0, N // CH)
    def _(chunk):
        row = rows_of(chunk)
        put(state, Z0, row, 0.5 * (at(coef, O2, row) + at(coef, O1, row)))
        for k, p in enumerate((O1, A, B, I1)):
            diag, fx, fy, fz = prepare(coef, p, row)
            to_fx, to_fy, to_iv, to_fz, to_dg, to_x = keep[p]
            inv = 1.0 / diag
            if p == O1:
                inv = inv * alive
            put(*to_fx, row, fx)
            put(*to_fy, row, fy)
            put(*to_iv, row, inv)
            put(*to_fz, row, fz)
            if to_dg:
                put(*to_dg, row, diag)
            if to_x:
                x1 = rhs[k - 1, pl.ds(row, CH), :] * inv * (1.0 / CENTER)
                put(*to_x, row, x1)
                if p == A:
                    xa[pl.ds(row, CH), :] = x1
        for k, (p, q) in enumerate(((A, B), (O1, O2), (I1, I2))):
            red[pl.ds(k * N + row, CH), :] = at(coef, p, row) + at(coef, q, row)

    step_a, step_b = FINE[0]
    left_over = 1.0 - 1.0 / CENTER

    @pl.loop(0, N // CH)
    def _(chunk):
        row = rows_of(chunk)
        here = at(mine, XB, row)
        part = lateral(row, (state, XA), (state, FXA), (state, FYA)) + at(state, Z2, row) * here
        put(state, PA, row, part + left_over * rhs[0, pl.ds(row, CH), :])
        part = lateral(row, (state, XI), (mine, FXI), (mine, FYI)) + at(state, Z3, row) * here
        put(state, PI, row, part + left_over * rhs[2, pl.ds(row, CH), :])
        res = lateral(row, (mine, XB), (mine, FXB), (mine, FYB)) + left_over * rhs[1, pl.ds(row, CH), :]
        res = res + (at(state, Z2, row) * at(state, XA, row) + at(state, Z3, row) * at(state, XI, row))
        move = step_a * here + step_b * (at(mine, IVB, row) * res)
        put(state, EB, row, move)
        put(state, X2B, row, here + move)
        put(mine, RB, row, res - at(mine, DB, row) * move)

    @pl.loop(0, N // CH)
    def _(chunk):
        row = rows_of(chunk)
        put(state, PB, row, at(mine, RB, row) + lateral(row, (state, EB), (mine, FXB), (mine, FYB)))

    cpl[...] = dot(red[...], pair_matrix(N, NC))
    bc, bo, bi = (
        0.125 * (cpl[pl.ds(k * N, NC, 2), :] + cpl[pl.ds(k * N + 1, NC, 2), :]) for k in range(3)
    )
    row_at = lax.broadcasted_iota(jnp.int32, (NC, NC), 0)
    lane = lane_iota((NC, NC))
    around = (
        jnp.where(lane == NC - 1, 0.0, left(bc))
        + jnp.where(lane == 0, 0.0, right(bc))
        + jnp.where(row_at == NC - 1, 0.0, pltpu.roll(bc, NC - 1, 0))
        + jnp.where(row_at == 0, 0.0, pltpu.roll(bc, 1, 0))
    )
    diag = 0.25 * (3.0 * bc + 0.5 * (around + bo + bi))
    state[COARSE_AT, 0:NC, 0:NC] = bc
    state[COARSE_AT, 0:NC, NC:N] = 1.0 / (CENTER * diag)


SPLIT = 2
HELD = 5


def pre_kernel(bs, bx, state, sx, xi, pack, side, x1, e2, part, red, cpl, packed, own, zeros, sems):
    _, par, _ = position()
    inner = 1 - par
    copies = Copies(sems)
    leaving = [copies.start(bs.at[par], side.at[2])]
    beyond = outer_mask() == 0.0

    @pl.when(beyond)
    def _():
        zeros[...] = jnp.zeros((N, N), jnp.float32)
        copies.again(zeros, side.at[3])

    @pl.when(jnp.logical_not(beyond))
    def _():
        copies.again(bx.at[inner], side.at[3])

    leaving.append(copies.handle(bx.at[inner], side.at[3]))
    clear_pads(x1, [0])
    clear_pads(e2, [0])

    @pl.loop(0, N // CH)
    def _(chunk):
        row = rows_of(chunk)
        put(x1, 0, row, sx[0, pl.ds(row, CH), :] * at(state, IVO, row) * (1.0 / CENTER))

    step_a, step_b = FINE[0]

    @pl.loop(0, N // CH)
    def _(chunk):
        row = rows_of(chunk)
        here = at(x1, 0, row)
        res = lateral(row, (x1, 0), (state, FXO), (state, FYO)) + (1.0 - 1.0 / CENTER) * sx[0, pl.ds(row, CH), :]
        res = res + (at(state, Z0, row) * sx[1, pl.ds(row, CH), :] + at(state, Z1, row) * at(state, XA, row))
        e2o = step_a * here + step_b * (at(state, IVO, row) * res)
        res = at(state, PA, row) + at(state, Z1, row) * here
        e2a = step_a * at(state, XA, row) + step_b * (at(state, IVA, row) * res)
        put(e2, 0, row, e2a)
        own[2, pl.ds(row, CH), :] = at(state, XA, row) + e2a
        own[3, pl.ds(row, CH), :] = at(state, X2B, row)
        res = res - at(state, DA, row) * e2a
        part[pl.ds(row, CH), :] = res + (at(state, Z1, row) * e2o + at(state, Z2, row) * at(state, EB, row))
        res = at(state, PI, row) + at(state, Z4, row) * xi[pl.ds(row, CH), :]
        e2i = step_a * at(state, XI, row) + step_b * (at(state, IVI, row) * res)
        own[1, pl.ds(row, CH), :] = at(state, PB, row) + (at(state, Z2, row) * e2a + at(state, Z3, row) * e2i)

    leaving += [copies.start(own.at[1], side.at[1]), copies.start(own.at[2:4], side.at[4:6])]

    @pl.loop(0, N // CH)
    def _(chunk):
        row = rows_of(chunk)
        res = part[pl.ds(row, CH), :] + lateral(row, (e2, 0), (state, FXA), (state, FYA))
        own[0, pl.ds(row, CH), :] = res
        red[pl.ds(row, CH), :] = res + own[1, pl.ds(row, CH), :]

    leaving.append(copies.start(own.at[0], side.at[0]))
    cpl[0:N, :] = dot(red[...], pair_matrix(N, NC))
    rc = 0.125 * (cpl[pl.ds(0, NC, 2), :] + cpl[pl.ds(1, NC, 2), :])
    fields = (rc * state[COARSE_AT, 0:NC, NC:N], state[COARSE_AT, 0:NC, 0:NC])
    for k, field in enumerate(fields):
        base = k * (NC + 16)
        cpl[base : base + 8, :] = jnp.zeros((8, NC), jnp.float32)
        cpl[base + NC + 8 : base + NC + 16, :] = jnp.zeros((8, NC), jnp.float32)
        cpl[base + 8 : base + NC + 8, :] = field
    each = NC // 2 // SPLIT
    for part in range(SPLIT):
        for odd, first in ((0, 4), (1, 9)):
            for k in range(2):
                for j in range(HELD):
                    rows = cpl[pl.ds(k * (NC + 16) + first + j + part * each * 2, each, 2), :]
                    packed[pl.ds(part * each * 4 * HELD + (odd * 2 + k) * HELD + j, each, 4 * HELD), :] = rows
        piece = pl.ds(part * each * 4 * HELD, each * 4 * HELD)
        leaving.append(copies.start(packed.at[piece], pack.at[piece]))
    for copy in leaving:
        copy.wait()


def coarse_kernel(recv, other, pack, cpl, packed, sems):
    index, par, _ = position()
    rows = 2 * HELD
    planes = recv.shape[0] // rows
    plane_at = lax.broadcasted_iota(jnp.int32, (planes, NC), 0)
    lane = lane_iota((planes, NC))

    def up(v):
        return pltpu.roll(v, planes - 1, 0)

    def down(v):
        return pltpu.roll(v, 1, 0)

    def row_of(field, n):
        if n >= 0:
            return recv[pl.ds(field * HELD + jnp.where(par == 0, 4 - n, n), planes, rows), :]
        return other[pl.ds(field * HELD + jnp.where(par == 0, -n - 1, 5 + n), planes, rows), :]

    u1 = {j: row_of(0, j) for j in range(-4, 5)}
    bc = {j: row_of(1, j) for j in range(-4, 5)}
    fr = {j: 0.125 * (bc[j] + bc[j + 1]) for j in range(-4, 4)}
    fz, fy, dg, iv = {}, {}, {}, {}
    for j in range(-3, 4):
        zn = jnp.where(plane_at == planes - 1, 0.0, up(bc[j]))
        zp = jnp.where(plane_at == 0, 0.0, down(bc[j]))
        yn = jnp.where(lane == NC - 1, 0.0, left(bc[j]))
        yp = jnp.where(lane == 0, 0.0, right(bc[j]))
        fz[j] = jnp.where(plane_at == planes - 1, 0.0, 0.125 * (bc[j] + zn))
        fy[j] = jnp.where(lane == NC - 1, 0.0, 0.125 * (bc[j] + yn))
        dg[j] = 0.75 * bc[j] + 0.125 * (zn + zp + yn + yp + bc[j - 1] + bc[j + 1])
        row = index + jnp.where(par == 0, -j, j)
        inside = (row >= 0) & (row < NC)
        iv[j] = jnp.where(inside, 1.0 / jnp.where(inside, dg[j], 1.0), 0.0)

    def off(v, j):
        total = fr[j] * v[j + 1] + fr[j - 1] * v[j - 1]
        total = total + fz[j] * up(v[j]) + down(fz[j] * v[j])
        return total + fy[j] * left(v[j]) + right(fy[j] * v[j])

    reach = 3
    res = {j: (CENTER - 1.0) * dg[j] * u1[j] + off(u1, j) for j in range(-reach, reach + 1)}
    step = u1
    total = u1[0]
    for k, (step_a, step_b) in enumerate(COARSE):
        step = {j: step_a * step[j] + step_b * iv[j] * res[j] for j in range(-reach, reach + 1)}
        total = total + step[0]
        reach -= 1
        res = {j: res[j] - dg[j] * step[j] + off(step, j) for j in range(-reach, reach + 1)}
    groups = lax.axis_size("grp")
    each = planes // groups
    column = jnp.sum(res[0].reshape(groups, each, NC), axis=1, keepdims=True)
    weight = jnp.sum(dg[0].reshape(groups, each, NC), axis=1, keepdims=True)
    lift = jnp.broadcast_to(column / weight, (groups, each, NC)).reshape(planes, NC)
    cpl[0:8, :] = jnp.zeros((8, NC), jnp.float32)
    cpl[planes + 8 : planes + 16, :] = jnp.zeros((8, NC), jnp.float32)
    cpl[8 : planes + 8, :] = total + lift
    copies, leaving = Copies(sems), []
    half = planes // 2
    for part in range(2):
        for k in range(5):
            packed[pl.ds(part * half * 5 + k, half, 5), :] = cpl[pl.ds(6 + k + part * half, half), :]
        piece = pl.ds(part * half * 5, half * 5)
        leaving.append(copies.start(packed.at[piece], pack.at[piece]))
    for copy in leaving:
        copy.wait()


def post_kernel(
    b, bs, bx, own, over, side, w, x5, r5,
    coef, fx, fy, fz, iv, dg, before, x2v, pw, r3, e4, r4, e5, half, wide, x5v, r5v, sems,
):
    _, par, _ = position()
    inner = 1 - par
    order = (par, inner)
    alive = outer_mask()
    copies = Copies(sems)
    source = (over.at[2], bx.at[par], bx.at[inner], b.at[par], b.at[inner], bs.at[par], bs.at[inner], side.at[3])
    earlier = (over.at[1], over.at[0], own.at[0], own.at[1], side.at[1], side.at[0])
    started = {}
    for p in range(8):
        started[p] = [fill(copies, source[p], coef, p)]
        if 1 <= p <= 6:
            started[p].append(copies.start(earlier[p - 1], before.at[p - 1]))
    x2_copy = copies.start(own.at[4:6], x2v)
    clear_pads(coef, range(8))
    clear_pads(fx, range(4))
    clear_pads(pw, range(5))
    clear_pads(e4, range(6))
    clear_pads(e5, range(4))
    spread = dot(w[...], 0.5 * pair_matrix(NC, N))
    for side in (0, 1):
        wide[side] = spread[:, side * NC : (side + 1) * NC]
    held = (0, 1, 1, 2, 2, 3, 3, 4)
    for k in range(5):
        z = jnp.where(par == 0, k, 4 - k)
        for side in (0, 1):
            part = wide[side, pl.ds(z, NC, 5), :]
            half[pl.ds(0, NC, 2), :] = part
            half[pl.ds(1, NC, 2), :] = part
            pw[k, PAD : PAD + N, side * NC : (side + 1) * NC] = half[...]

    def arrived(planes):
        for p in planes:
            for copy in started[p]:
                copy.wait()

    arrived(range(3))
    clear_outside([(coef, 0), (coef, 1), (coef, 2)])

    @whole_planes
    def _(row):
        for k in range(6):
            p = k + 1
            if k > 0:
                arrived([p + 1])
            win = window(coef, p, row)
            ahead = pltpu.roll(win, win.shape[0] - 1, 0)
            mid = win[PAD : PAD + CH]
            lane = lane_iota(mid.shape)
            nxt = jnp.where(lane == N - 1, 0.0, left(mid))
            prv = jnp.where(lane == 0, 0.0, right(mid))
            under, over = at(coef, p - 1, row), at(coef, p + 1, row)
            around = (ahead[PAD : PAD + CH] + shifted(win, -1)) + (nxt + prv) + (under + over)
            diag = 6.0 * mid + around
            if k < 2:
                inv = alive * inverse(jnp.where(diag > 0.0, diag, 1.0))
            else:
                inv = inverse(diag)
            fxw = win + ahead
            fyc = jnp.where(lane == N - 1, 0.0, mid + nxt)
            below, above = mid + under, mid + over
            if 1 <= k <= 4:
                put(fx, k - 1, row, fxw[PAD : PAD + CH])
                fy[k - 1, pl.ds(row, CH), :] = fyc
                fz[k - 1, pl.ds(row, CH), :] = below
                iv[k - 1, pl.ds(row, CH), :] = inv
                if k == 4:
                    fz[4, pl.ds(row, CH), :] = above
            if k in (2, 3):
                dg[k - 2, pl.ds(row, CH), :] = diag
            v = window(pw, held[p], row)
            here = v[PAD : PAD + CH]
            total = fxw[PAD : PAD + CH] * shifted(v, 1) + shifted(fxw * v, -1)
            total = total + (fyc * left(here) + right(fyc * here))
            total = total + (below * at(pw, held[p - 1], row) + above * at(pw, held[p + 1], row))
            res = (before[k, pl.ds(row, CH), :] - diag * here) + total
            if 1 <= k <= 4:
                r3[k - 1, pl.ds(row, CH), :] = res
            put(e4, k, row, (1.0 / CENTER) * (inv * res))

    x2_copy.wait()
    step_a, step_b = FINE[0]

    def off(v, k, shift, row):
        win, f = window(v, k + shift, row), window(fx, k, row)
        here = win[PAD : PAD + CH]
        g = fy[k, pl.ds(row, CH), :]
        total = f[PAD : PAD + CH] * shifted(win, 1) + shifted(f * win, -1)
        total = total + (g * left(here) + right(g * here))
        total = total + fz[k, pl.ds(row, CH), :] * at(v, k + shift - 1, row)
        return total + fz[k + 1, pl.ds(row, CH), :] * at(v, k + shift + 1, row)

    @whole_planes
    def _(row):
        for k in range(4):
            res = off(e4, k, 1, row) + (1.0 - 1.0 / CENTER) * r3[k, pl.ds(row, CH), :]
            here = at(e4, k + 1, row)
            move = step_a * here + step_b * (iv[k, pl.ds(row, CH), :] * res)
            put(e5, k, row, move)
            if k in (1, 2):
                r4[k - 1, pl.ds(row, CH), :] = res
                x5v[k - 1, pl.ds(row, CH), :] = x2v[k - 1, pl.ds(row, CH), :] + 2.0 * (at(pw, held[k + 2], row) + (here + move))

    leaving = [copies.start(x5v.at[k], x5.at[order[k]]) for k in range(2)]

    @whole_planes
    def _(row):
        for k in (1, 2):
            res = r4[k - 1, pl.ds(row, CH), :] - dg[k - 1, pl.ds(row, CH), :] * at(e5, k, row)
            r5v[k - 1, pl.ds(row, CH), :] = res + off(e5, k, 0, row)
            leaving.append(copies.start(r5v.at[k - 1], r5.at[order[k - 1]]))

    for copy in leaving:
        copy.wait()


def call(kernel, outs, scratch, sems, cost, *operands, limit=24):
    return pl.pallas_call(
        kernel,
        out_shape=[jax.ShapeDtypeStruct(s, jnp.float32) for s, _ in outs],
        in_specs=[spec for _, spec in operands],
        out_specs=[spec for _, spec in outs],
        scratch_shapes=[pltpu.VMEM(s, jnp.float32) for s in scratch] + [pltpu.SemaphoreType.DMA((sems,))],
        compiler_params=pltpu.CompilerParams(vmem_limit_bytes=limit * 1024 * 1024),
        cost_estimate=pl.CostEstimate(flops=cost, bytes_accessed=cost, transcendentals=0),
    )(*(array for array, _ in operands))


def local(right_side, conductivity):
    total = lax.axis_size("grp") * lax.axis_size("slab")
    inside = [(i, i ^ 1) for i in range(total)]
    across = [(i, (i + 1) % total) for i in range(1, total, 2)] + [((i + 1) % total, i) for i in range(1, total, 2)]

    def swap(v):
        return lax.ppermute(v, AXES, inside)

    between = [pair for pair in across if abs(pair[0] - pair[1]) == 1]

    def cross(v, ends=True):
        return lax.ppermute(v, AXES, across if ends else between)

    def everywhere(v):
        rows = v.shape[0]
        return lax.all_to_all(v.reshape(rows, 1, NC), AXES, 0, 0, tiled=True).reshape(rows, NC)

    plane, padded = (N, N), (N + 2 * PAD, N)
    two = (2,) + plane
    g, b = right_side, conductivity
    bs = swap(b)
    bx = cross(b)
    gs = swap(g)
    (send,) = call(first_kernel, [(two, VM)], [(3,) + padded], 3, 1 << 20, (g, VM), (b, ANY), (bs, ANY))
    sx = cross(send, False)
    state, xa = call(
        ready_kernel,
        [((STATE,) + padded, VM), (plane, VM)],
        [(6,) + padded, (3,) + plane, (8,) + padded, (3 * N, N), (3 * N, NC)],
        9,
        6 << 20,
        (g, ANY), (gs, ANY), (b, ANY), (bs, ANY), (bx, ANY), (send, ANY),
    )
    xi = swap(xa)
    pack, side = call(
        pre_kernel,
        [((2 * HELD * total, NC), HBM), ((6,) + plane, HBM)],
        [(1,) + padded, (1,) + padded, plane, plane, (2 * (NC + 16), NC), (2 * HELD * total, NC), (4,) + plane, plane],
        5 + SPLIT,
        6 << 20,
        (bs, ANY), (bx, ANY), (state, VM), (sx, VM), (xi, VM),
    )
    from_over = cross(side)
    from_side = swap(side)
    own = swap(from_side)
    got = everywhere(pack)
    (back,) = call(
        coarse_kernel,
        [((5 * NC, NC), HBM)],
        [(total + 16, NC), (5 * NC, NC)],
        2,
        4 << 20,
        (got, VM), (swap(got), VM),
    )
    w = everywhere(back)
    x5, r5 = call(
        post_kernel,
        [(two, HBM), (two, HBM)],
        [(8,) + padded, (4,) + padded, (4,) + plane, (5,) + plane, (4,) + plane, two, (6,) + plane, two, (5,) + padded, (4,) + plane, (6,) + padded, two, (4,) + padded, (N, NC), (2, 5 * NC, NC), two, two],
        20,
        8 << 20,
        (b, ANY), (bs, ANY), (bx, ANY), (own, ANY), (from_over, ANY), (from_side, ANY), (w, VM),
    )
    return x5, r5


def solution(mesh):
    spec = P(AXES, None, None)
    return jax.shard_map(
        local, mesh=mesh, in_specs=(spec, spec), out_specs=(spec, spec), check_vma=False
    )
```

```python
import functools

import jax
import jax.numpy as jnp
from jax import lax
from jax.experimental import pallas as pl
from jax.experimental.pallas import tpu as pltpu
from jax.sharding import PartitionSpec as P

KF = 2
KC = 4

LOWER = 0.25
UPPER = 2.0
CENTER = (UPPER + LOWER) / 2.0
HALF = (UPPER - LOWER) / 2.0
RATIO = CENTER / HALF

AXES = ("grp", "slab")
N = 256
NC = 128
PAD = 8
CH = 256
VM = pl.BlockSpec(memory_space=pltpu.VMEM)
ANY = pl.BlockSpec(memory_space=pl.ANY)
HBM = pl.BlockSpec(memory_space=pltpu.HBM)


def chebyshev_factors(count):
    rho = 1.0 / RATIO
    found = []
    for _ in range(count - 1):
        new = 1.0 / (2.0 * RATIO - rho)
        found.append((new * rho, 2.0 * new / HALF))
        rho = new
    return found


FINE = chebyshev_factors(KF)
COARSE = chebyshev_factors(KC)


def position():
    grp, slab = lax.axis_index("grp"), lax.axis_index("slab")
    slabs = lax.axis_size("slab")
    total = lax.axis_size("grp") * slabs
    index = grp * slabs + slab
    return index, lax.rem(slab, 2), total


def outer_mask():
    index, _, total = position()
    return jnp.where((index == 0) | (index == total - 1), 0.0, 1.0).astype(jnp.float32)


def lane_iota(shape):
    return lax.broadcasted_iota(jnp.int32, shape, len(shape) - 1)


def rows_of(chunk):
    return pl.multiple_of(chunk * CH, CH)


def whole_planes(body):
    assert CH == N
    body(0)


def at(ref, plane, row):
    return ref[plane, pl.ds(row + PAD, CH), :]


def window(ref, plane, row):
    return ref[plane, pl.ds(row, CH + 2 * PAD), :]


def shifted(win, by):
    return pltpu.roll(win, (-by) % win.shape[0], 0)[PAD : PAD + CH]


def put(ref, plane, row, value):
    ref[plane, pl.ds(row + PAD, CH), :] = value


def clear_pads(ref, planes):
    for p in planes:
        ref[p, 0:PAD, :] = jnp.zeros((PAD, N), jnp.float32)
        ref[p, PAD + N : 2 * PAD + N, :] = jnp.zeros((PAD, N), jnp.float32)


def left(v):
    return pltpu.roll(v, v.shape[-1] - 1, v.ndim - 1)


def right(v):
    return pltpu.roll(v, 1, v.ndim - 1)


class Copies:
    def __init__(self, sems):
        self.sems, self.used = sems, 0

    def start(self, source, target):
        copy = pltpu.make_async_copy(source, target, self.sems.at[self.used])
        self.used += 1
        copy.start()
        return copy

    def again(self, source, target):
        pltpu.make_async_copy(source, target, self.sems.at[self.used]).start()

    def handle(self, source, target):
        copy = pltpu.make_async_copy(source, target, self.sems.at[self.used])
        self.used += 1
        return copy


def clear_outside(refs):
    @pl.when(outer_mask() == 0.0)
    def _():
        for ref, plane in refs:
            ref[plane] = jnp.zeros(ref.shape[1:], jnp.float32)


def fill(copies, source, ref, plane):
    return copies.start(source, ref.at[plane, PAD : PAD + N, :])


def lateral(row, here, fx, fy):
    v = window(*here, row)
    f = window(*fx, row)
    mid = v[PAD : PAD + CH]
    g = at(*fy, row)
    total = f[PAD : PAD + CH] * shifted(v, 1) + shifted(f * v, -1)
    return total + (g * left(mid) + right(g * mid))


def inverse(v):
    return 1.0 / v


def prepare(coef, p, row):
    win = window(coef, p, row)
    b = win[PAD : PAD + CH]
    down = shifted(win, 1)
    lane = lane_iota(b.shape)
    nxt = jnp.where(lane == N - 1, 0.0, left(b))
    prv = jnp.where(lane == 0, 0.0, right(b))
    over = at(coef, p + 1, row)
    around = (down + shifted(win, -1)) + (nxt + prv) + (at(coef, p - 1, row) + over)
    fy = jnp.where(lane == N - 1, 0.0, 0.5 * (b + nxt))
    return 3.0 * b + 0.5 * around, 0.5 * (b + down), fy, 0.5 * (b + over)


def pair_matrix(rows, cols):
    i = lax.broadcasted_iota(jnp.int32, (rows, cols), 0)
    j = lax.broadcasted_iota(jnp.int32, (rows, cols), 1)
    same = i // 2 == j if rows > cols else j // 2 == i
    return jnp.where(same, 1.0, 0.0).astype(jnp.bfloat16)


def dot(x, y):
    total = None
    for _ in range(3):
        part = x.astype(jnp.bfloat16)
        x = x - part.astype(jnp.float32)
        term = jnp.dot(part, y, preferred_element_type=jnp.float32)
        total = term if total is None else total + term
    return total


def first_kernel(g, b, bs, out, coef, sems):
    _, par, _ = position()
    inner = 1 - par
    copies = Copies(sems)
    started = [fill(copies, bs.at[par], coef, 2), fill(copies, b.at[inner], coef, 1), fill(copies, b.at[par], coef, 0)]
    clear_pads(coef, [1])
    for copy in started:
        copy.wait()

    @pl.loop(0, N // CH)
    def _(chunk):
        row = rows_of(chunk)
        diag = prepare(coef, 1, row)[0]
        out[0, pl.ds(row, CH), :] = g[par, pl.ds(row, CH), :]
        out[1, pl.ds(row, CH), :] = g[inner, pl.ds(row, CH), :] / (CENTER * diag)


(FXO, FXA, FYO, FYA, IVO, IVA, IVI, Z0, Z1, Z2, Z3, Z4, XA, XI, PA, PI, DA, EB, PB, X2B, COARSE_AT, STATE) = range(22)


def ready_kernel(g, gs, b, bs, bx, sent, state, xa, coef, rhs, mine, red, cpl, sems):
    del sent
    _, par, _ = position()
    inner = 1 - par
    alive = outer_mask()
    O2, O1, A, B, I1, I2 = range(6)
    FXB, FXI, FYB, FYI, IVB, DB, XB, RB = range(8)
    copies = Copies(sems)
    source = {O2: bx.at[par], O1: bx.at[inner], A: b.at[par], B: b.at[inner], I1: bs.at[par], I2: bs.at[inner]}
    given = [g.at[par], g.at[inner], gs.at[par]]
    started = [fill(copies, ref, coef, p) for p, ref in source.items()]
    started += [copies.start(ref, rhs.at[k]) for k, ref in enumerate(given)]
    clear_pads(coef, range(6))
    clear_pads(state, (FXO, FXA, XA, XI, EB))
    clear_pads(mine, (FXB, FXI, XB))
    for copy in started:
        copy.wait()
    clear_outside([(coef, O2), (coef, O1)])
    keep = {
        O1: ((state, FXO), (state, FYO), (state, IVO), (state, Z1), None, None),
        A: ((state, FXA), (state, FYA), (state, IVA), (state, Z2), (state, DA), (state, XA)),
        B: ((mine, FXB), (mine, FYB), (mine, IVB), (state, Z3), (mine, DB), (mine, XB)),
        I1: ((mine, FXI), (mine, FYI), (state, IVI), (state, Z4), None, (state, XI)),
    }

    @pl.loop(0, N // CH)
    def _(chunk):
        row = rows_of(chunk)
        put(state, Z0, row, 0.5 * (at(coef, O2, row) + at(coef, O1, row)))
        for k, p in enumerate((O1, A, B, I1)):
            diag, fx, fy, fz = prepare(coef, p, row)
            to_fx, to_fy, to_iv, to_fz, to_dg, to_x = keep[p]
            inv = 1.0 / diag
            if p == O1:
                inv = inv * alive
            put(*to_fx, row, fx)
            put(*to_fy, row, fy)
            put(*to_iv, row, inv)
            put(*to_fz, row, fz)
            if to_dg:
                put(*to_dg, row, diag)
            if to_x:
                x1 = rhs[k - 1, pl.ds(row, CH), :] * inv * (1.0 / CENTER)
                put(*to_x, row, x1)
                if p == A:
                    xa[pl.ds(row, CH), :] = x1
        for k, (p, q) in enumerate(((A, B), (O1, O2), (I1, I2))):
            red[pl.ds(k * N + row, CH), :] = at(coef, p, row) + at(coef, q, row)

    step_a, step_b = FINE[0]
    left_over = 1.0 - 1.0 / CENTER

    @pl.loop(0, N // CH)
    def _(chunk):
        row = rows_of(chunk)
        here = at(mine, XB, row)
        part = lateral(row, (state, XA), (state, FXA), (state, FYA)) + at(state, Z2, row) * here
        put(state, PA, row, part + left_over * rhs[0, pl.ds(row, CH), :])
        part = lateral(row, (state, XI), (mine, FXI), (mine, FYI)) + at(state, Z3, row) * here
        put(state, PI, row, part + left_over * rhs[2, pl.ds(row, CH), :])
        res = lateral(row, (mine, XB), (mine, FXB), (mine, FYB)) + left_over * rhs[1, pl.ds(row, CH), :]
        res = res + (at(state, Z2, row) * at(state, XA, row) + at(state, Z3, row) * at(state, XI, row))
        move = step_a * here + step_b * (at(mine, IVB, row) * res)
        put(state, EB, row, move)
        put(state, X2B, row, here + move)
        put(mine, RB, row, res - at(mine, DB, row) * move)

    @pl.loop(0, N // CH)
    def _(chunk):
        row = rows_of(chunk)
        put(state, PB, row, at(mine, RB, row) + lateral(row, (state, EB), (mine, FXB), (mine, FYB)))

    cpl[...] = dot(red[...], pair_matrix(N, NC))
    bc, bo, bi = (
        0.125 * (cpl[pl.ds(k * N, NC, 2), :] + cpl[pl.ds(k * N + 1, NC, 2), :]) for k in range(3)
    )
    row_at = lax.broadcasted_iota(jnp.int32, (NC, NC), 0)
    lane = lane_iota((NC, NC))
    around = (
        jnp.where(lane == NC - 1, 0.0, left(bc))
        + jnp.where(lane == 0, 0.0, right(bc))
        + jnp.where(row_at == NC - 1, 0.0, pltpu.roll(bc, NC - 1, 0))
        + jnp.where(row_at == 0, 0.0, pltpu.roll(bc, 1, 0))
    )
    diag = 0.25 * (3.0 * bc + 0.5 * (around + bo + bi))
    state[COARSE_AT, 0:NC, 0:NC] = bc
    state[COARSE_AT, 0:NC, NC:N] = 1.0 / (CENTER * diag)


SPLIT = 2
HELD = 5


def pre_kernel(bs, bx, state, sx, xi, pack, side, x1, e2, part, red, cpl, packed, own, zeros, sems):
    _, par, _ = position()
    inner = 1 - par
    copies = Copies(sems)
    leaving = [copies.start(bs.at[par], side.at[2])]
    beyond = outer_mask() == 0.0

    @pl.when(beyond)
    def _():
        zeros[...] = jnp.zeros((N, N), jnp.float32)
        copies.again(zeros, side.at[3])

    @pl.when(jnp.logical_not(beyond))
    def _():
        copies.again(bx.at[inner], side.at[3])

    leaving.append(copies.handle(bx.at[inner], side.at[3]))
    clear_pads(x1, [0])
    clear_pads(e2, [0])

    @pl.loop(0, N // CH)
    def _(chunk):
        row = rows_of(chunk)
        put(x1, 0, row, sx[0, pl.ds(row, CH), :] * at(state, IVO, row) * (1.0 / CENTER))

    step_a, step_b = FINE[0]

    @pl.loop(0, N // CH)
    def _(chunk):
        row = rows_of(chunk)
        here = at(x1, 0, row)
        res = lateral(row, (x1, 0), (state, FXO), (state, FYO)) + (1.0 - 1.0 / CENTER) * sx[0, pl.ds(row, CH), :]
        res = res + (at(state, Z0, row) * sx[1, pl.ds(row, CH), :] + at(state, Z1, row) * at(state, XA, row))
        e2o = step_a * here + step_b * (at(state, IVO, row) * res)
        res = at(state, PA, row) + at(state, Z1, row) * here
        e2a = step_a * at(state, XA, row) + step_b * (at(state, IVA, row) * res)
        put(e2, 0, row, e2a)
        own[2, pl.ds(row, CH), :] = at(state, XA, row) + e2a
        own[3, pl.ds(row, CH), :] = at(state, X2B, row)
        res = res - at(state, DA, row) * e2a
        part[pl.ds(row, CH), :] = res + (at(state, Z1, row) * e2o + at(state, Z2, row) * at(state, EB, row))
        res = at(state, PI, row) + at(state, Z4, row) * xi[pl.ds(row, CH), :]
        e2i = step_a * at(state, XI, row) + step_b * (at(state, IVI, row) * res)
        own[1, pl.ds(row, CH), :] = at(state, PB, row) + (at(state, Z2, row) * e2a + at(state, Z3, row) * e2i)

    leaving += [copies.start(own.at[1], side.at[1]), copies.start(own.at[2:4], side.at[4:6])]

    @pl.loop(0, N // CH)
    def _(chunk):
        row = rows_of(chunk)
        res = part[pl.ds(row, CH), :] + lateral(row, (e2, 0), (state, FXA), (state, FYA))
        own[0, pl.ds(row, CH), :] = res
        red[pl.ds(row, CH), :] = res + own[1, pl.ds(row, CH), :]

    leaving.append(copies.start(own.at[0], side.at[0]))
    cpl[0:N, :] = dot(red[...], pair_matrix(N, NC))
    rc = 0.125 * (cpl[pl.ds(0, NC, 2), :] + cpl[pl.ds(1, NC, 2), :])
    fields = (rc * state[COARSE_AT, 0:NC, NC:N], state[COARSE_AT, 0:NC, 0:NC])
    for k, field in enumerate(fields):
        base = k * (NC + 16)
        cpl[base : base + 8, :] = jnp.zeros((8, NC), jnp.float32)
        cpl[base + NC + 8 : base + NC + 16, :] = jnp.zeros((8, NC), jnp.float32)
        cpl[base + 8 : base + NC + 8, :] = field
    each = NC // 2 // SPLIT
    for part in range(SPLIT):
        for odd, first in ((0, 4), (1, 9)):
            for k in range(2):
                for j in range(HELD):
                    rows = cpl[pl.ds(k * (NC + 16) + first + j + part * each * 2, each, 2), :]
                    packed[pl.ds(part * each * 4 * HELD + (odd * 2 + k) * HELD + j, each, 4 * HELD), :] = rows
        piece = pl.ds(part * each * 4 * HELD, each * 4 * HELD)
        leaving.append(copies.start(packed.at[piece], pack.at[piece]))
    for copy in leaving:
        copy.wait()


class CoarseRows:
    def __init__(self, planes):
        self.index, self.par, _ = position()
        self.planes = planes
        self.plane_at = lax.broadcasted_iota(jnp.int32, (planes, NC), 0)
        self.lane = lane_iota((planes, NC))
        self.fr, self.fz, self.fy, self.dg, self.iv = {}, {}, {}, {}, {}

    def load(self, ref, field, n, own):
        at_n = jnp.where(self.par == 0, 4 - n, n) if own else jnp.where(self.par == 0, -n - 1, 5 + n)
        return ref[pl.ds(field * HELD + at_n, self.planes, 2 * HELD), :]

    def up(self, v):
        return pltpu.roll(v, self.planes - 1, 0)

    def down(self, v):
        return pltpu.roll(v, 1, 0)

    def prepare(self, bc, j):
        last, end = self.plane_at == self.planes - 1, self.lane == NC - 1
        zn = jnp.where(last, 0.0, self.up(bc[j]))
        zp = jnp.where(self.plane_at == 0, 0.0, self.down(bc[j]))
        yn = jnp.where(end, 0.0, left(bc[j]))
        yp = jnp.where(self.lane == 0, 0.0, right(bc[j]))
        self.fz[j] = jnp.where(last, 0.0, 0.125 * (bc[j] + zn))
        self.fy[j] = jnp.where(end, 0.0, 0.125 * (bc[j] + yn))
        self.dg[j] = 0.75 * bc[j] + 0.125 * (zn + zp + yn + yp + bc[j - 1] + bc[j + 1])
        row = self.index + jnp.where(self.par == 0, -j, j)
        inside = (row >= 0) & (row < NC)
        self.iv[j] = jnp.where(inside, 1.0 / jnp.where(inside, self.dg[j], 1.0), 0.0)

    def off(self, v, j):
        total = self.fr[j] * v[j + 1] + self.fr[j - 1] * v[j - 1]
        total = total + self.fz[j] * self.up(v[j]) + self.down(self.fz[j] * v[j])
        return total + self.fy[j] * left(v[j]) + right(self.fy[j] * v[j])


HANDED = 12


def coarse_first_kernel(recv, handed):
    m = CoarseRows(recv.shape[0] // (2 * HELD))
    u1 = {j: m.load(recv, 0, j, True) for j in range(5)}
    bc = {j: m.load(recv, 1, j, True) for j in range(5)}
    m.fr = {j: 0.125 * (bc[j] + bc[j + 1]) for j in range(4)}
    for j in (1, 2, 3):
        m.prepare(bc, j)
    (a1, b1), (a2, b2) = COARSE[:2]
    res = {j: (CENTER - 1.0) * m.dg[j] * u1[j] + m.off(u1, j) for j in (1, 2, 3)}
    step = {j: a1 * u1[j] + b1 * m.iv[j] * res[j] for j in (1, 2, 3)}
    second = res[2] - m.dg[2] * step[2] + m.off(step, 2)
    later = a2 * step[2] + b2 * m.iv[2] * second
    found = (m.fr[0], m.fr[1], m.fz[1], m.fy[1], m.dg[1], m.iv[1], res[1], step[1], step[2], later, u1[1], bc[1])
    for k, value in enumerate(found):
        handed[k] = value


def coarse_kernel(recv, other, handed, pack, cpl, packed, sems):
    planes = recv.shape[0] // (2 * HELD)
    m = CoarseRows(planes)
    u1 = {j: m.load(other, 0, j, False) for j in range(-4, 0)}
    bc = {j: m.load(other, 1, j, False) for j in range(-4, 0)}
    u1[0], bc[0] = m.load(recv, 0, 0, True), m.load(recv, 1, 0, True)
    m.fr = {j: 0.125 * (bc[j] + bc[j + 1]) for j in range(-4, 0)}
    m.fr[0], m.fr[1], m.fz[1], m.fy[1], m.dg[1], m.iv[1], near, second1, second2, third2, u1[1], bc[1] = (
        handed[k] for k in range(HANDED)
    )
    for j in range(-3, 1):
        m.prepare(bc, j)
    reach = 3
    res = {j: (CENTER - 1.0) * m.dg[j] * u1[j] + m.off(u1, j) for j in range(-reach, 1)}
    res[1] = near
    step = u1
    total = u1[0]
    known = ({1: second1, 2: second2}, {2: third2}, {})
    for (step_a, step_b), there in zip(COARSE, known, strict=True):
        moved_by = dict(there)
        for j in range(-reach, min(reach, 1) + 1):
            if j not in moved_by:
                moved_by[j] = step_a * step[j] + step_b * m.iv[j] * res[j]
        step = moved_by
        total = total + step[0]
        reach -= 1
        res = {j: res[j] - m.dg[j] * step[j] + m.off(step, j) for j in range(-reach, min(reach, 1) + 1)}
    groups = lax.axis_size("grp")
    each = planes // groups
    column = jnp.sum(res[0].reshape(groups, each, NC), axis=1, keepdims=True)
    weight = jnp.sum(m.dg[0].reshape(groups, each, NC), axis=1, keepdims=True)
    lift = jnp.broadcast_to(column / weight, (groups, each, NC)).reshape(planes, NC)
    cpl[0:8, :] = jnp.zeros((8, NC), jnp.float32)
    cpl[planes + 8 : planes + 16, :] = jnp.zeros((8, NC), jnp.float32)
    cpl[8 : planes + 8, :] = total + lift
    for k in range(5):
        packed[pl.ds(k, planes, 5), :] = cpl[pl.ds(6 + k, planes), :]
    Copies(sems).start(packed, pack).wait()


def post_kernel(
    b, bs, bx, own, over, side, w, x5, r5,
    coef, fx, fy, fz, iv, dg, before, x2v, pw, r3, e4, r4, e5, half, wide, x5v, r5v, sems,
):
    _, par, _ = position()
    inner = 1 - par
    order = (par, inner)
    alive = outer_mask()
    copies = Copies(sems)
    source = (over.at[2], bx.at[par], bx.at[inner], b.at[par], b.at[inner], bs.at[par], bs.at[inner], side.at[3])
    earlier = (over.at[1], over.at[0], own.at[0], own.at[1], side.at[1], side.at[0])
    started = {}
    for p in range(8):
        started[p] = [fill(copies, source[p], coef, p)]
        if 1 <= p <= 6:
            started[p].append(copies.start(earlier[p - 1], before.at[p - 1]))
    x2_copy = copies.start(own.at[4:6], x2v)
    clear_pads(coef, range(8))
    clear_pads(fx, range(4))
    clear_pads(pw, range(5))
    clear_pads(e4, range(6))
    clear_pads(e5, range(4))
    spread = dot(w[...], 0.5 * pair_matrix(NC, N))
    for side in (0, 1):
        wide[side] = spread[:, side * NC : (side + 1) * NC]
    held = (0, 1, 1, 2, 2, 3, 3, 4)
    for k in range(5):
        z = jnp.where(par == 0, k, 4 - k)
        for side in (0, 1):
            part = wide[side, pl.ds(z, NC, 5), :]
            half[pl.ds(0, NC, 2), :] = part
            half[pl.ds(1, NC, 2), :] = part
            pw[k, PAD : PAD + N, side * NC : (side + 1) * NC] = half[...]

    def arrived(planes):
        for p in planes:
            for copy in started[p]:
                copy.wait()

    arrived(range(3))
    clear_outside([(coef, 0), (coef, 1), (coef, 2)])

    @whole_planes
    def _(row):
        for k in range(6):
            p = k + 1
            if k > 0:
                arrived([p + 1])
            win = window(coef, p, row)
            ahead = pltpu.roll(win, win.shape[0] - 1, 0)
            mid = win[PAD : PAD + CH]
            lane = lane_iota(mid.shape)
            nxt = jnp.where(lane == N - 1, 0.0, left(mid))
            prv = jnp.where(lane == 0, 0.0, right(mid))
            under, over = at(coef, p - 1, row), at(coef, p + 1, row)
            around = (ahead[PAD : PAD + CH] + shifted(win, -1)) + (nxt + prv) + (under + over)
            diag = 6.0 * mid + around
            if k < 2:
                inv = alive * inverse(jnp.where(diag > 0.0, diag, 1.0))
            else:
                inv = inverse(diag)
            fxw = win + ahead
            fyc = jnp.where(lane == N - 1, 0.0, mid + nxt)
            below, above = mid + under, mid + over
            if 1 <= k <= 4:
                put(fx, k - 1, row, fxw[PAD : PAD + CH])
                fy[k - 1, pl.ds(row, CH), :] = fyc
                fz[k - 1, pl.ds(row, CH), :] = below
                iv[k - 1, pl.ds(row, CH), :] = inv
                if k == 4:
                    fz[4, pl.ds(row, CH), :] = above
            if k in (2, 3):
                dg[k - 2, pl.ds(row, CH), :] = diag
            v = window(pw, held[p], row)
            here = v[PAD : PAD + CH]
            total = fxw[PAD : PAD + CH] * shifted(v, 1) + shifted(fxw * v, -1)
            total = total + (fyc * left(here) + right(fyc * here))
            total = total + (below * at(pw, held[p - 1], row) + above * at(pw, held[p + 1], row))
            res = (before[k, pl.ds(row, CH), :] - diag * here) + total
            if 1 <= k <= 4:
                r3[k - 1, pl.ds(row, CH), :] = res
            put(e4, k, row, (1.0 / CENTER) * (inv * res))

    x2_copy.wait()
    step_a, step_b = FINE[0]

    def off(v, k, shift, row):
        win, f = window(v, k + shift, row), window(fx, k, row)
        here = win[PAD : PAD + CH]
        g = fy[k, pl.ds(row, CH), :]
        total = f[PAD : PAD + CH] * shifted(win, 1) + shifted(f * win, -1)
        total = total + (g * left(here) + right(g * here))
        total = total + fz[k, pl.ds(row, CH), :] * at(v, k + shift - 1, row)
        return total + fz[k + 1, pl.ds(row, CH), :] * at(v, k + shift + 1, row)

    @whole_planes
    def _(row):
        for k in range(4):
            res = off(e4, k, 1, row) + (1.0 - 1.0 / CENTER) * r3[k, pl.ds(row, CH), :]
            here = at(e4, k + 1, row)
            move = step_a * here + step_b * (iv[k, pl.ds(row, CH), :] * res)
            put(e5, k, row, move)
            if k in (1, 2):
                r4[k - 1, pl.ds(row, CH), :] = res
                x5v[k - 1, pl.ds(row, CH), :] = x2v[k - 1, pl.ds(row, CH), :] + 2.0 * (at(pw, held[k + 2], row) + (here + move))

    leaving = [copies.start(x5v.at[k], x5.at[order[k]]) for k in range(2)]

    @whole_planes
    def _(row):
        for k in (1, 2):
            res = r4[k - 1, pl.ds(row, CH), :] - dg[k - 1, pl.ds(row, CH), :] * at(e5, k, row)
            r5v[k - 1, pl.ds(row, CH), :] = res + off(e5, k, 0, row)
            leaving.append(copies.start(r5v.at[k - 1], r5.at[order[k - 1]]))

    for copy in leaving:
        copy.wait()


def call(kernel, outs, scratch, sems, cost, *operands, limit=24):
    return pl.pallas_call(
        kernel,
        out_shape=[jax.ShapeDtypeStruct(s, jnp.float32) for s, _ in outs],
        in_specs=[spec for _, spec in operands],
        out_specs=[spec for _, spec in outs],
        scratch_shapes=[pltpu.VMEM(s, jnp.float32) for s in scratch] + [pltpu.SemaphoreType.DMA((sems,))] * (sems > 0),
        compiler_params=pltpu.CompilerParams(vmem_limit_bytes=limit * 1024 * 1024),
        cost_estimate=pl.CostEstimate(flops=cost, bytes_accessed=cost, transcendentals=0),
    )(*(array for array, _ in operands))


def local(right_side, conductivity):
    total = lax.axis_size("grp") * lax.axis_size("slab")
    inside = [(i, i ^ 1) for i in range(total)]
    across = [(i, (i + 1) % total) for i in range(1, total, 2)] + [((i + 1) % total, i) for i in range(1, total, 2)]

    def swap(v):
        return lax.ppermute(v, AXES, inside)

    between = [pair for pair in across if abs(pair[0] - pair[1]) == 1]

    def cross(v, ends=True):
        return lax.ppermute(v, AXES, across if ends else between)

    def everywhere(v):
        rows = v.shape[0]
        return lax.all_to_all(v.reshape(rows, 1, NC), AXES, 0, 0, tiled=True).reshape(rows, NC)

    plane, padded = (N, N), (N + 2 * PAD, N)
    two = (2,) + plane
    g, b = right_side, conductivity
    bs = swap(b)
    bx = cross(b)
    gs = swap(g)
    (send,) = call(first_kernel, [(two, VM)], [(3,) + padded], 3, 1 << 20, (g, VM), (b, ANY), (bs, ANY))
    sx = cross(send, False)
    state, xa = call(
        ready_kernel,
        [((STATE,) + padded, VM), (plane, VM)],
        [(6,) + padded, (3,) + plane, (8,) + padded, (3 * N, N), (3 * N, NC)],
        9,
        6 << 20,
        (g, ANY), (gs, ANY), (b, ANY), (bs, ANY), (bx, ANY), (send, ANY),
    )
    xi = swap(xa)
    pack, side = call(
        pre_kernel,
        [((2 * HELD * total, NC), HBM), ((6,) + plane, HBM)],
        [(1,) + padded, (1,) + padded, plane, plane, (2 * (NC + 16), NC), (2 * HELD * total, NC), (4,) + plane, plane],
        5 + SPLIT,
        6 << 20,
        (bs, ANY), (bx, ANY), (state, VM), (sx, VM), (xi, VM),
    )
    from_over = cross(side, False)
    from_side = swap(side)
    own = swap(from_side)
    got = everywhere(pack)
    (handed,) = call(coarse_first_kernel, [((HANDED, total, NC), VM)], [], 0, 2 << 20, (got, VM))
    (back,) = call(
        coarse_kernel,
        [((5 * NC, NC), HBM)],
        [(total + 16, NC), (5 * NC, NC)],
        1,
        4 << 20,
        (got, VM), (swap(got), VM), (handed, VM),
    )
    w = everywhere(back)
    x5, r5 = call(
        post_kernel,
        [(two, HBM), (two, HBM)],
        [(8,) + padded, (4,) + padded, (4,) + plane, (5,) + plane, (4,) + plane, two, (6,) + plane, two, (5,) + padded, (4,) + plane, (6,) + padded, two, (4,) + padded, (N, NC), (2, 5 * NC, NC), two, two],
        20,
        8 << 20,
        (b, ANY), (bs, ANY), (bx, ANY), (own, ANY), (from_over, ANY), (from_side, ANY), (w, VM),
    )
    return x5, r5


def solution(mesh):
    spec = P(AXES, None, None)
    return jax.shard_map(
        local, mesh=mesh, in_specs=(spec, spec), out_specs=(spec, spec), check_vma=False
    )
```

```python
import functools

import jax
import jax.numpy as jnp
from jax import lax
from jax.experimental import pallas as pl
from jax.experimental.pallas import tpu as pltpu
from jax.sharding import PartitionSpec as P

KF = 2
KC = 4

LOWER = 0.25
UPPER = 2.0
CENTER = (UPPER + LOWER) / 2.0
HALF = (UPPER - LOWER) / 2.0
RATIO = CENTER / HALF

AXES = ("grp", "slab")
N = 256
NC = 128
PAD = 8
CH = 256
VM = pl.BlockSpec(memory_space=pltpu.VMEM)
ANY = pl.BlockSpec(memory_space=pl.ANY)
HBM = pl.BlockSpec(memory_space=pltpu.HBM)


def chebyshev_factors(count):
    rho = 1.0 / RATIO
    found = []
    for _ in range(count - 1):
        new = 1.0 / (2.0 * RATIO - rho)
        found.append((new * rho, 2.0 * new / HALF))
        rho = new
    return found


FINE = chebyshev_factors(KF)
COARSE = chebyshev_factors(KC)


def position():
    grp, slab = lax.axis_index("grp"), lax.axis_index("slab")
    slabs = lax.axis_size("slab")
    total = lax.axis_size("grp") * slabs
    index = grp * slabs + slab
    return index, lax.rem(slab, 2), total


def outer_mask():
    index, _, total = position()
    return jnp.where((index == 0) | (index == total - 1), 0.0, 1.0).astype(jnp.float32)


def lane_iota(shape):
    return lax.broadcasted_iota(jnp.int32, shape, len(shape) - 1)


def rows_of(chunk):
    return pl.multiple_of(chunk * CH, CH)


def whole_planes(body):
    assert CH == N
    body(0)


def at(ref, plane, row):
    return ref[plane, pl.ds(row + PAD, CH), :]


def window(ref, plane, row):
    return ref[plane, pl.ds(row, CH + 2 * PAD), :]


def shifted(win, by):
    return pltpu.roll(win, (-by) % win.shape[0], 0)[PAD : PAD + CH]


def put(ref, plane, row, value):
    ref[plane, pl.ds(row + PAD, CH), :] = value


def clear_pads(ref, planes):
    for p in planes:
        ref[p, 0:PAD, :] = jnp.zeros((PAD, N), jnp.float32)
        ref[p, PAD + N : 2 * PAD + N, :] = jnp.zeros((PAD, N), jnp.float32)


def left(v):
    return pltpu.roll(v, v.shape[-1] - 1, v.ndim - 1)


def right(v):
    return pltpu.roll(v, 1, v.ndim - 1)


class Copies:
    def __init__(self, sems):
        self.sems, self.used = sems, 0

    def start(self, source, target):
        copy = pltpu.make_async_copy(source, target, self.sems.at[self.used])
        self.used += 1
        copy.start()
        return copy

    def again(self, source, target):
        pltpu.make_async_copy(source, target, self.sems.at[self.used]).start()

    def handle(self, source, target):
        copy = pltpu.make_async_copy(source, target, self.sems.at[self.used])
        self.used += 1
        return copy


def clear_outside(refs):
    @pl.when(outer_mask() == 0.0)
    def _():
        for ref, plane in refs:
            ref[plane] = jnp.zeros(ref.shape[1:], jnp.float32)


def fill(copies, source, ref, plane):
    return copies.start(source, ref.at[plane, PAD : PAD + N, :])


def lateral(row, here, fx, fy):
    v = window(*here, row)
    f = window(*fx, row)
    mid = v[PAD : PAD + CH]
    g = at(*fy, row)
    total = f[PAD : PAD + CH] * shifted(v, 1) + shifted(f * v, -1)
    return total + (g * left(mid) + right(g * mid))


def inverse(v):
    return 1.0 / v


def prepare(coef, p, row):
    win = window(coef, p, row)
    b = win[PAD : PAD + CH]
    down = shifted(win, 1)
    lane = lane_iota(b.shape)
    nxt = jnp.where(lane == N - 1, 0.0, left(b))
    prv = jnp.where(lane == 0, 0.0, right(b))
    over = at(coef, p + 1, row)
    around = (down + shifted(win, -1)) + (nxt + prv) + (at(coef, p - 1, row) + over)
    fy = jnp.where(lane == N - 1, 0.0, 0.5 * (b + nxt))
    return 3.0 * b + 0.5 * around, 0.5 * (b + down), fy, 0.5 * (b + over)


def pair_matrix(rows, cols):
    i = lax.broadcasted_iota(jnp.int32, (rows, cols), 0)
    j = lax.broadcasted_iota(jnp.int32, (rows, cols), 1)
    same = i // 2 == j if rows > cols else j // 2 == i
    return jnp.where(same, 1.0, 0.0).astype(jnp.bfloat16)


def dot(x, y):
    total = None
    for _ in range(3):
        part = x.astype(jnp.bfloat16)
        x = x - part.astype(jnp.float32)
        term = jnp.dot(part, y, preferred_element_type=jnp.float32)
        total = term if total is None else total + term
    return total


def first_kernel(g, b, bs, out, coef, sems):
    _, par, _ = position()
    inner = 1 - par
    copies = Copies(sems)
    started = [fill(copies, bs.at[par], coef, 2), fill(copies, b.at[inner], coef, 1), fill(copies, b.at[par], coef, 0)]
    clear_pads(coef, [1])
    for copy in started:
        copy.wait()

    @pl.loop(0, N // CH)
    def _(chunk):
        row = rows_of(chunk)
        diag = prepare(coef, 1, row)[0]
        out[0, pl.ds(row, CH), :] = g[par, pl.ds(row, CH), :]
        out[1, pl.ds(row, CH), :] = g[inner, pl.ds(row, CH), :] / (CENTER * diag)


(FXO, FXA, FYO, FYA, IVO, IVA, IVI, Z0, Z1, Z2, Z3, Z4, XA, XI, PA, PI, DA, EB, PB, X2B, COARSE_AT, STATE) = range(22)


def ready_kernel(g, gs, b, bs, bx, sent, state, xa, coef, rhs, mine, red, cpl, sems):
    del sent
    _, par, _ = position()
    inner = 1 - par
    alive = outer_mask()
    O2, O1, A, B, I1, I2 = range(6)
    FXB, FXI, FYB, FYI, IVB, DB, XB, RB = range(8)
    copies = Copies(sems)
    source = {O2: bx.at[par], O1: bx.at[inner], A: b.at[par], B: b.at[inner], I1: bs.at[par], I2: bs.at[inner]}
    given = [g.at[par], g.at[inner], gs.at[par]]
    started = [fill(copies, ref, coef, p) for p, ref in source.items()]
    started += [copies.start(ref, rhs.at[k]) for k, ref in enumerate(given)]
    clear_pads(coef, range(6))
    clear_pads(state, (FXO, FXA, XA, XI, EB))
    clear_pads(mine, (FXB, FXI, XB))
    for copy in started:
        copy.wait()
    clear_outside([(coef, O2), (coef, O1)])
    keep = {
        O1: ((state, FXO), (state, FYO), (state, IVO), (state, Z1), None, None),
        A: ((state, FXA), (state, FYA), (state, IVA), (state, Z2), (state, DA), (state, XA)),
        B: ((mine, FXB), (mine, FYB), (mine, IVB), (state, Z3), (mine, DB), (mine, XB)),
        I1: ((mine, FXI), (mine, FYI), (state, IVI), (state, Z4), None, (state, XI)),
    }

    @pl.loop(0, N // CH)
    def _(chunk):
        row = rows_of(chunk)
        put(state, Z0, row, 0.5 * (at(coef, O2, row) + at(coef, O1, row)))
        for k, p in enumerate((O1, A, B, I1)):
            diag, fx, fy, fz = prepare(coef, p, row)
            to_fx, to_fy, to_iv, to_fz, to_dg, to_x = keep[p]
            inv = 1.0 / diag
            if p == O1:
                inv = inv * alive
            put(*to_fx, row, fx)
            put(*to_fy, row, fy)
            put(*to_iv, row, inv)
            put(*to_fz, row, fz)
            if to_dg:
                put(*to_dg, row, diag)
            if to_x:
                x1 = rhs[k - 1, pl.ds(row, CH), :] * inv * (1.0 / CENTER)
                put(*to_x, row, x1)
                if p == A:
                    xa[pl.ds(row, CH), :] = x1
        for k, (p, q) in enumerate(((A, B), (O1, O2), (I1, I2))):
            red[pl.ds(k * N + row, CH), :] = at(coef, p, row) + at(coef, q, row)

    step_a, step_b = FINE[0]
    left_over = 1.0 - 1.0 / CENTER

    @pl.loop(0, N // CH)
    def _(chunk):
        row = rows_of(chunk)
        here = at(mine, XB, row)
        part = lateral(row, (state, XA), (state, FXA), (state, FYA)) + at(state, Z2, row) * here
        put(state, PA, row, part + left_over * rhs[0, pl.ds(row, CH), :])
        part = lateral(row, (state, XI), (mine, FXI), (mine, FYI)) + at(state, Z3, row) * here
        put(state, PI, row, part + left_over * rhs[2, pl.ds(row, CH), :])
        res = lateral(row, (mine, XB), (mine, FXB), (mine, FYB)) + left_over * rhs[1, pl.ds(row, CH), :]
        res = res + (at(state, Z2, row) * at(state, XA, row) + at(state, Z3, row) * at(state, XI, row))
        move = step_a * here + step_b * (at(mine, IVB, row) * res)
        put(state, EB, row, move)
        put(state, X2B, row, here + move)
        put(mine, RB, row, res - at(mine, DB, row) * move)

    @pl.loop(0, N // CH)
    def _(chunk):
        row = rows_of(chunk)
        put(state, PB, row, at(mine, RB, row) + lateral(row, (state, EB), (mine, FXB), (mine, FYB)))

    cpl[...] = dot(red[...], pair_matrix(N, NC))
    bc, bo, bi = (
        0.125 * (cpl[pl.ds(k * N, NC, 2), :] + cpl[pl.ds(k * N + 1, NC, 2), :]) for k in range(3)
    )
    row_at = lax.broadcasted_iota(jnp.int32, (NC, NC), 0)
    lane = lane_iota((NC, NC))
    around = (
        jnp.where(lane == NC - 1, 0.0, left(bc))
        + jnp.where(lane == 0, 0.0, right(bc))
        + jnp.where(row_at == NC - 1, 0.0, pltpu.roll(bc, NC - 1, 0))
        + jnp.where(row_at == 0, 0.0, pltpu.roll(bc, 1, 0))
    )
    diag = 0.25 * (3.0 * bc + 0.5 * (around + bo + bi))
    state[COARSE_AT, 0:NC, 0:NC] = bc
    state[COARSE_AT, 0:NC, NC:N] = 1.0 / (CENTER * diag)


SPLIT = 2
HELD = 5


def pre_kernel(bs, bx, state, sx, xi, pack, side, x1, e2, part, red, cpl, packed, own, zeros, sems):
    _, par, _ = position()
    inner = 1 - par
    copies = Copies(sems)
    leaving = [copies.start(bs.at[par], side.at[2])]
    beyond = outer_mask() == 0.0

    @pl.when(beyond)
    def _():
        zeros[...] = jnp.zeros((N, N), jnp.float32)
        copies.again(zeros, side.at[3])

    @pl.when(jnp.logical_not(beyond))
    def _():
        copies.again(bx.at[inner], side.at[3])

    leaving.append(copies.handle(bx.at[inner], side.at[3]))
    clear_pads(x1, [0])
    clear_pads(e2, [0])

    @pl.loop(0, N // CH)
    def _(chunk):
        row = rows_of(chunk)
        put(x1, 0, row, sx[0, pl.ds(row, CH), :] * at(state, IVO, row) * (1.0 / CENTER))

    step_a, step_b = FINE[0]

    @pl.loop(0, N // CH)
    def _(chunk):
        row = rows_of(chunk)
        here = at(x1, 0, row)
        res = lateral(row, (x1, 0), (state, FXO), (state, FYO)) + (1.0 - 1.0 / CENTER) * sx[0, pl.ds(row, CH), :]
        res = res + (at(state, Z0, row) * sx[1, pl.ds(row, CH), :] + at(state, Z1, row) * at(state, XA, row))
        e2o = step_a * here + step_b * (at(state, IVO, row) * res)
        res = at(state, PA, row) + at(state, Z1, row) * here
        e2a = step_a * at(state, XA, row) + step_b * (at(state, IVA, row) * res)
        put(e2, 0, row, e2a)
        own[2, pl.ds(row, CH), :] = at(state, XA, row) + e2a
        own[3, pl.ds(row, CH), :] = at(state, X2B, row)
        res = res - at(state, DA, row) * e2a
        part[pl.ds(row, CH), :] = res + (at(state, Z1, row) * e2o + at(state, Z2, row) * at(state, EB, row))
        res = at(state, PI, row) + at(state, Z4, row) * xi[pl.ds(row, CH), :]
        e2i = step_a * at(state, XI, row) + step_b * (at(state, IVI, row) * res)
        own[1, pl.ds(row, CH), :] = at(state, PB, row) + (at(state, Z2, row) * e2a + at(state, Z3, row) * e2i)

    leaving += [copies.start(own.at[1], side.at[1]), copies.start(own.at[2:4], side.at[4:6])]

    @pl.loop(0, N // CH)
    def _(chunk):
        row = rows_of(chunk)
        res = part[pl.ds(row, CH), :] + lateral(row, (e2, 0), (state, FXA), (state, FYA))
        own[0, pl.ds(row, CH), :] = res
        red[pl.ds(row, CH), :] = res + own[1, pl.ds(row, CH), :]

    leaving.append(copies.start(own.at[0], side.at[0]))
    cpl[0:N, :] = dot(red[...], pair_matrix(N, NC))
    rc = 0.125 * (cpl[pl.ds(0, NC, 2), :] + cpl[pl.ds(1, NC, 2), :])
    fields = (rc * state[COARSE_AT, 0:NC, NC:N], state[COARSE_AT, 0:NC, 0:NC])
    for k, field in enumerate(fields):
        base = k * (NC + 16)
        cpl[base : base + 8, :] = jnp.zeros((8, NC), jnp.float32)
        cpl[base + NC + 8 : base + NC + 16, :] = jnp.zeros((8, NC), jnp.float32)
        cpl[base + 8 : base + NC + 8, :] = field
    each = NC // 2 // SPLIT
    for part in range(SPLIT):
        for odd, first in ((0, 4), (1, 9)):
            for k in range(2):
                for j in range(HELD):
                    rows = cpl[pl.ds(k * (NC + 16) + first + j + part * each * 2, each, 2), :]
                    packed[pl.ds(part * each * 4 * HELD + (odd * 2 + k) * HELD + j, each, 4 * HELD), :] = rows
        piece = pl.ds(part * each * 4 * HELD, each * 4 * HELD)
        leaving.append(copies.start(packed.at[piece], pack.at[piece]))
    for copy in leaving:
        copy.wait()


class CoarseRows:
    def __init__(self, planes):
        self.index, self.par, _ = position()
        self.planes = planes
        self.plane_at = lax.broadcasted_iota(jnp.int32, (planes, NC), 0)
        self.lane = lane_iota((planes, NC))
        self.fr, self.fz, self.fy, self.dg, self.iv = {}, {}, {}, {}, {}

    def load(self, ref, field, n, own):
        at_n = jnp.where(self.par == 0, 4 - n, n) if own else jnp.where(self.par == 0, -n - 1, 5 + n)
        return ref[pl.ds(field * HELD + at_n, self.planes, 2 * HELD), :]

    def up(self, v):
        return pltpu.roll(v, self.planes - 1, 0)

    def down(self, v):
        return pltpu.roll(v, 1, 0)

    def prepare(self, bc, j):
        last, end = self.plane_at == self.planes - 1, self.lane == NC - 1
        zn = jnp.where(last, 0.0, self.up(bc[j]))
        zp = jnp.where(self.plane_at == 0, 0.0, self.down(bc[j]))
        yn = jnp.where(end, 0.0, left(bc[j]))
        yp = jnp.where(self.lane == 0, 0.0, right(bc[j]))
        self.fz[j] = jnp.where(last, 0.0, 0.125 * (bc[j] + zn))
        self.fy[j] = jnp.where(end, 0.0, 0.125 * (bc[j] + yn))
        self.dg[j] = 0.75 * bc[j] + 0.125 * (zn + zp + yn + yp + bc[j + 1])
        if j == 0 and j - 1 not in bc:
            return
        self.dg[j] = self.dg[j] + 0.125 * bc[j - 1]
        row = self.index + jnp.where(self.par == 0, -j, j)
        inside = (row >= 0) & (row < NC)
        self.iv[j] = jnp.where(inside, 1.0 / jnp.where(inside, self.dg[j], 1.0), 0.0)

    def off(self, v, j):
        total = self.fr[j] * v[j + 1]
        if j - 1 in v:
            total = total + self.fr[j - 1] * v[j - 1]
        total = total + self.fz[j] * self.up(v[j]) + self.down(self.fz[j] * v[j])
        return total + self.fy[j] * left(v[j]) + right(self.fy[j] * v[j])


HANDED = 16


def coarse_first_kernel(recv, handed):
    m = CoarseRows(recv.shape[0] // (2 * HELD))
    u1 = {j: m.load(recv, 0, j, True) for j in range(5)}
    bc = {j: m.load(recv, 1, j, True) for j in range(5)}
    m.fr = {j: 0.125 * (bc[j] + bc[j + 1]) for j in range(4)}
    for j in (0, 1, 2, 3):
        m.prepare(bc, j)
    (a1, b1), (a2, b2) = COARSE[:2]
    res = {j: (CENTER - 1.0) * m.dg[j] * u1[j] + m.off(u1, j) for j in (1, 2, 3)}
    step = {j: a1 * u1[j] + b1 * m.iv[j] * res[j] for j in (1, 2, 3)}
    second = res[2] - m.dg[2] * step[2] + m.off(step, 2)
    later = a2 * step[2] + b2 * m.iv[2] * second
    found = (m.fr[0], m.fr[1], m.fz[1], m.fy[1], m.dg[1], m.iv[1], res[1], step[1], step[2], later, u1[1], bc[1])
    found += (m.fz[0], m.fy[0], m.dg[0], m.off(u1, 0))
    for k, value in enumerate(found):
        handed[k] = value


def coarse_kernel(recv, other, handed, pack, cpl, packed, sems):
    planes = recv.shape[0] // (2 * HELD)
    m = CoarseRows(planes)
    u1 = {j: m.load(other, 0, j, False) for j in range(-4, 0)}
    bc = {j: m.load(other, 1, j, False) for j in range(-4, 0)}
    u1[0], bc[0] = m.load(recv, 0, 0, True), m.load(recv, 1, 0, True)
    m.fr = {j: 0.125 * (bc[j] + bc[j + 1]) for j in range(-4, 0)}
    m.fr[0], m.fr[1], m.fz[1], m.fy[1], m.dg[1], m.iv[1], near, second1, second2, third2, u1[1], bc[1] = (
        handed[k] for k in range(12)
    )
    m.fz[0], m.fy[0], m.dg[0], here = (handed[k] for k in range(12, HANDED))
    m.dg[0] = m.dg[0] + 0.125 * bc[-1]
    m.iv[0] = 1.0 / m.dg[0]
    for j in range(-3, 0):
        m.prepare(bc, j)
    reach = 3
    res = {j: (CENTER - 1.0) * m.dg[j] * u1[j] + m.off(u1, j) for j in range(-reach, 0)}
    res[0] = (CENTER - 1.0) * m.dg[0] * u1[0] + (here + m.fr[-1] * u1[-1])
    res[1] = near
    step = u1
    total = u1[0]
    known = ({1: second1, 2: second2}, {2: third2}, {})
    for (step_a, step_b), there in zip(COARSE, known, strict=True):
        moved_by = dict(there)
        for j in range(-reach, min(reach, 1) + 1):
            if j not in moved_by:
                moved_by[j] = step_a * step[j] + step_b * m.iv[j] * res[j]
        step = moved_by
        total = total + step[0]
        reach -= 1
        res = {j: res[j] - m.dg[j] * step[j] + m.off(step, j) for j in range(-reach, min(reach, 1) + 1)}
    groups = lax.axis_size("grp")
    each = planes // groups
    column = jnp.sum(res[0].reshape(groups, each, NC), axis=1, keepdims=True)
    weight = jnp.sum(m.dg[0].reshape(groups, each, NC), axis=1, keepdims=True)
    lift = jnp.broadcast_to(column / weight, (groups, each, NC)).reshape(planes, NC)
    cpl[0:8, :] = jnp.zeros((8, NC), jnp.float32)
    cpl[planes + 8 : planes + 16, :] = jnp.zeros((8, NC), jnp.float32)
    cpl[8 : planes + 8, :] = total + lift
    for k in range(5):
        packed[pl.ds(k, planes, 5), :] = cpl[pl.ds(6 + k, planes), :]
    Copies(sems).start(packed, pack).wait()


def post_kernel(
    b, bs, bx, own, over, side, w, x5, r5,
    coef, fx, fy, fz, iv, dg, before, x2v, pw, r3, e4, r4, e5, half, wide, x5v, r5v, sems,
):
    _, par, _ = position()
    inner = 1 - par
    order = (par, inner)
    alive = outer_mask()
    copies = Copies(sems)
    source = (over.at[2], bx.at[par], bx.at[inner], b.at[par], b.at[inner], bs.at[par], bs.at[inner], side.at[3])
    earlier = (over.at[1], over.at[0], own.at[0], own.at[1], side.at[1], side.at[0])
    started = {}
    for p in range(8):
        started[p] = [fill(copies, source[p], coef, p)]
        if 1 <= p <= 6:
            started[p].append(copies.start(earlier[p - 1], before.at[p - 1]))
    x2_copy = copies.start(own.at[4:6], x2v)
    clear_pads(coef, range(8))
    clear_pads(fx, range(4))
    clear_pads(pw, range(5))
    clear_pads(e4, range(6))
    clear_pads(e5, range(4))
    spread = dot(w[...], 0.5 * pair_matrix(NC, N))
    for side in (0, 1):
        wide[side] = spread[:, side * NC : (side + 1) * NC]
    held = (0, 1, 1, 2, 2, 3, 3, 4)
    for k in range(5):
        z = jnp.where(par == 0, k, 4 - k)
        for side in (0, 1):
            part = wide[side, pl.ds(z, NC, 5), :]
            half[pl.ds(0, NC, 2), :] = part
            half[pl.ds(1, NC, 2), :] = part
            pw[k, PAD : PAD + N, side * NC : (side + 1) * NC] = half[...]

    def arrived(planes):
        for p in planes:
            for copy in started[p]:
                copy.wait()

    arrived(range(3))
    clear_outside([(coef, 0), (coef, 1), (coef, 2)])

    @whole_planes
    def _(row):
        for k in range(6):
            p = k + 1
            if k > 0:
                arrived([p + 1])
            win = window(coef, p, row)
            ahead = pltpu.roll(win, win.shape[0] - 1, 0)
            mid = win[PAD : PAD + CH]
            lane = lane_iota(mid.shape)
            nxt = jnp.where(lane == N - 1, 0.0, left(mid))
            prv = jnp.where(lane == 0, 0.0, right(mid))
            under, over = at(coef, p - 1, row), at(coef, p + 1, row)
            around = (ahead[PAD : PAD + CH] + shifted(win, -1)) + (nxt + prv) + (under + over)
            diag = 6.0 * mid + around
            if k < 2:
                inv = alive * inverse(jnp.where(diag > 0.0, diag, 1.0))
            else:
                inv = inverse(diag)
            fxw = win + ahead
            fyc = jnp.where(lane == N - 1, 0.0, mid + nxt)
            below, above = mid + under, mid + over
            if 1 <= k <= 4:
                put(fx, k - 1, row, fxw[PAD : PAD + CH])
                fy[k - 1, pl.ds(row, CH), :] = fyc
                fz[k - 1, pl.ds(row, CH), :] = below
                iv[k - 1, pl.ds(row, CH), :] = inv
                if k == 4:
                    fz[4, pl.ds(row, CH), :] = above
            if k in (2, 3):
                dg[k - 2, pl.ds(row, CH), :] = diag
            v = window(pw, held[p], row)
            here = v[PAD : PAD + CH]
            total = fxw[PAD : PAD + CH] * shifted(v, 1) + shifted(fxw * v, -1)
            total = total + (fyc * left(here) + right(fyc * here))
            total = total + (below * at(pw, held[p - 1], row) + above * at(pw, held[p + 1], row))
            res = (before[k, pl.ds(row, CH), :] - diag * here) + total
            if 1 <= k <= 4:
                r3[k - 1, pl.ds(row, CH), :] = res
            put(e4, k, row, (1.0 / CENTER) * (inv * res))

    x2_copy.wait()
    step_a, step_b = FINE[0]

    def off(v, k, shift, row):
        win, f = window(v, k + shift, row), window(fx, k, row)
        here = win[PAD : PAD + CH]
        g = fy[k, pl.ds(row, CH), :]
        total = f[PAD : PAD + CH] * shifted(win, 1) + shifted(f * win, -1)
        total = total + (g * left(here) + right(g * here))
        total = total + fz[k, pl.ds(row, CH), :] * at(v, k + shift - 1, row)
        return total + fz[k + 1, pl.ds(row, CH), :] * at(v, k + shift + 1, row)

    @whole_planes
    def _(row):
        for k in range(4):
            res = off(e4, k, 1, row) + (1.0 - 1.0 / CENTER) * r3[k, pl.ds(row, CH), :]
            here = at(e4, k + 1, row)
            move = step_a * here + step_b * (iv[k, pl.ds(row, CH), :] * res)
            put(e5, k, row, move)
            if k in (1, 2):
                r4[k - 1, pl.ds(row, CH), :] = res
                x5v[k - 1, pl.ds(row, CH), :] = x2v[k - 1, pl.ds(row, CH), :] + 2.0 * (at(pw, held[k + 2], row) + (here + move))

    leaving = [copies.start(x5v.at[k], x5.at[order[k]]) for k in range(2)]

    @whole_planes
    def _(row):
        for k in (1, 2):
            res = r4[k - 1, pl.ds(row, CH), :] - dg[k - 1, pl.ds(row, CH), :] * at(e5, k, row)
            r5v[k - 1, pl.ds(row, CH), :] = res + off(e5, k, 0, row)
            leaving.append(copies.start(r5v.at[k - 1], r5.at[order[k - 1]]))

    for copy in leaving:
        copy.wait()


def call(kernel, outs, scratch, sems, cost, *operands, limit=24):
    return pl.pallas_call(
        kernel,
        out_shape=[jax.ShapeDtypeStruct(s, jnp.float32) for s, _ in outs],
        in_specs=[spec for _, spec in operands],
        out_specs=[spec for _, spec in outs],
        scratch_shapes=[pltpu.VMEM(s, jnp.float32) for s in scratch] + [pltpu.SemaphoreType.DMA((sems,))] * (sems > 0),
        compiler_params=pltpu.CompilerParams(vmem_limit_bytes=limit * 1024 * 1024),
        cost_estimate=pl.CostEstimate(flops=cost, bytes_accessed=cost, transcendentals=0),
    )(*(array for array, _ in operands))


def local(right_side, conductivity):
    total = lax.axis_size("grp") * lax.axis_size("slab")
    inside = [(i, i ^ 1) for i in range(total)]
    across = [(i, (i + 1) % total) for i in range(1, total, 2)] + [((i + 1) % total, i) for i in range(1, total, 2)]

    def swap(v):
        return lax.ppermute(v, AXES, inside)

    between = [pair for pair in across if abs(pair[0] - pair[1]) == 1]

    def cross(v, ends=True):
        return lax.ppermute(v, AXES, across if ends else between)

    def everywhere(v):
        rows = v.shape[0]
        return lax.all_to_all(v.reshape(rows, 1, NC), AXES, 0, 0, tiled=True).reshape(rows, NC)

    plane, padded = (N, N), (N + 2 * PAD, N)
    two = (2,) + plane
    g, b = right_side, conductivity
    bs = swap(b)
    bx = cross(b)
    gs = swap(g)
    (send,) = call(first_kernel, [(two, VM)], [(3,) + padded], 3, 1 << 20, (g, VM), (b, ANY), (bs, ANY))
    sx = cross(send, False)
    state, xa = call(
        ready_kernel,
        [((STATE,) + padded, VM), (plane, VM)],
        [(6,) + padded, (3,) + plane, (8,) + padded, (3 * N, N), (3 * N, NC)],
        9,
        6 << 20,
        (g, ANY), (gs, ANY), (b, ANY), (bs, ANY), (bx, ANY), (send, ANY),
    )
    xi = swap(xa)
    pack, side = call(
        pre_kernel,
        [((2 * HELD * total, NC), HBM), ((6,) + plane, HBM)],
        [(1,) + padded, (1,) + padded, plane, plane, (2 * (NC + 16), NC), (2 * HELD * total, NC), (4,) + plane, plane],
        5 + SPLIT,
        6 << 20,
        (bs, ANY), (bx, ANY), (state, VM), (sx, VM), (xi, VM),
    )
    from_over = cross(side, False)
    from_side = swap(side)
    own = swap(from_side)
    got = everywhere(pack)
    (handed,) = call(coarse_first_kernel, [((HANDED, total, NC), VM)], [], 0, 2 << 20, (got, VM))
    (back,) = call(
        coarse_kernel,
        [((5 * NC, NC), HBM)],
        [(total + 16, NC), (5 * NC, NC)],
        1,
        4 << 20,
        (got, VM), (swap(got), VM), (handed, VM),
    )
    w = everywhere(back)
    x5, r5 = call(
        post_kernel,
        [(two, HBM), (two, HBM)],
        [(8,) + padded, (4,) + padded, (4,) + plane, (5,) + plane, (4,) + plane, two, (6,) + plane, two, (5,) + padded, (4,) + plane, (6,) + padded, two, (4,) + padded, (N, NC), (2, 5 * NC, NC), two, two],
        20,
        8 << 20,
        (b, ANY), (bs, ANY), (bx, ANY), (own, ANY), (from_over, ANY), (from_side, ANY), (w, VM),
    )
    return x5, r5


def solution(mesh):
    spec = P(AXES, None, None)
    return jax.shard_map(
        local, mesh=mesh, in_specs=(spec, spec), out_specs=(spec, spec), check_vma=False
    )
```

```python
import functools

import jax
import jax.numpy as jnp
from jax import lax
from jax.experimental import pallas as pl
from jax.experimental.pallas import tpu as pltpu
from jax.sharding import PartitionSpec as P

KF = 2
KC = 4

LOWER = 0.25
UPPER = 2.0
CENTER = (UPPER + LOWER) / 2.0
HALF = (UPPER - LOWER) / 2.0
RATIO = CENTER / HALF

AXES = ("grp", "slab")
N = 256
NC = 128
PAD = 8
CH = 256
VM = pl.BlockSpec(memory_space=pltpu.VMEM)
ANY = pl.BlockSpec(memory_space=pl.ANY)
HBM = pl.BlockSpec(memory_space=pltpu.HBM)


def chebyshev_factors(count):
    rho = 1.0 / RATIO
    found = []
    for _ in range(count - 1):
        new = 1.0 / (2.0 * RATIO - rho)
        found.append((new * rho, 2.0 * new / HALF))
        rho = new
    return found


FINE = chebyshev_factors(KF)
COARSE = chebyshev_factors(KC)


def position():
    grp, slab = lax.axis_index("grp"), lax.axis_index("slab")
    slabs = lax.axis_size("slab")
    total = lax.axis_size("grp") * slabs
    index = grp * slabs + slab
    return index, lax.rem(slab, 2), total


def outer_mask():
    index, _, total = position()
    return jnp.where((index == 0) | (index == total - 1), 0.0, 1.0).astype(jnp.float32)


def lane_iota(shape):
    return lax.broadcasted_iota(jnp.int32, shape, len(shape) - 1)


def rows_of(chunk):
    return pl.multiple_of(chunk * CH, CH)


def whole_planes(body):
    assert CH == N
    body(0)


def at(ref, plane, row):
    return ref[plane, pl.ds(row + PAD, CH), :]


def window(ref, plane, row):
    return ref[plane, pl.ds(row, CH + 2 * PAD), :]


def shifted(win, by):
    return pltpu.roll(win, (-by) % win.shape[0], 0)[PAD : PAD + CH]


def put(ref, plane, row, value):
    ref[plane, pl.ds(row + PAD, CH), :] = value


def clear_pads(ref, planes):
    for p in planes:
        ref[p, 0:PAD, :] = jnp.zeros((PAD, N), jnp.float32)
        ref[p, PAD + N : 2 * PAD + N, :] = jnp.zeros((PAD, N), jnp.float32)


def left(v):
    return pltpu.roll(v, v.shape[-1] - 1, v.ndim - 1)


def right(v):
    return pltpu.roll(v, 1, v.ndim - 1)


class Copies:
    def __init__(self, sems):
        self.sems, self.used = sems, 0

    def start(self, source, target):
        copy = pltpu.make_async_copy(source, target, self.sems.at[self.used])
        self.used += 1
        copy.start()
        return copy

    def again(self, source, target):
        pltpu.make_async_copy(source, target, self.sems.at[self.used]).start()

    def handle(self, source, target):
        copy = pltpu.make_async_copy(source, target, self.sems.at[self.used])
        self.used += 1
        return copy


def clear_outside(refs):
    @pl.when(outer_mask() == 0.0)
    def _():
        for ref, plane in refs:
            ref[plane] = jnp.zeros(ref.shape[1:], jnp.float32)


def fill(copies, source, ref, plane):
    return copies.start(source, ref.at[plane, PAD : PAD + N, :])


def lateral(row, here, fx, fy):
    v = window(*here, row)
    f = window(*fx, row)
    mid = v[PAD : PAD + CH]
    g = at(*fy, row)
    total = f[PAD : PAD + CH] * shifted(v, 1) + shifted(f * v, -1)
    return total + (g * left(mid) + right(g * mid))


def inverse(v):
    return 1.0 / v


def prepare(coef, p, row):
    win = window(coef, p, row)
    b = win[PAD : PAD + CH]
    down = shifted(win, 1)
    lane = lane_iota(b.shape)
    nxt = jnp.where(lane == N - 1, 0.0, left(b))
    prv = jnp.where(lane == 0, 0.0, right(b))
    over = at(coef, p + 1, row)
    around = (down + shifted(win, -1)) + (nxt + prv) + (at(coef, p - 1, row) + over)
    fy = jnp.where(lane == N - 1, 0.0, 0.5 * (b + nxt))
    return 3.0 * b + 0.5 * around, 0.5 * (b + down), fy, 0.5 * (b + over)


def pair_matrix(rows, cols):
    i = lax.broadcasted_iota(jnp.int32, (rows, cols), 0)
    j = lax.broadcasted_iota(jnp.int32, (rows, cols), 1)
    same = i // 2 == j if rows > cols else j // 2 == i
    return jnp.where(same, 1.0, 0.0).astype(jnp.bfloat16)


def dot(x, y):
    total = None
    for _ in range(3):
        part = x.astype(jnp.bfloat16)
        x = x - part.astype(jnp.float32)
        term = jnp.dot(part, y, preferred_element_type=jnp.float32)
        total = term if total is None else total + term
    return total


def first_kernel(g, b, bs, out, coef, sems):
    _, par, _ = position()
    inner = 1 - par
    copies = Copies(sems)
    started = [fill(copies, bs.at[par], coef, 2), fill(copies, b.at[inner], coef, 1), fill(copies, b.at[par], coef, 0)]
    clear_pads(coef, [1])
    for copy in started:
        copy.wait()

    @pl.loop(0, N // CH)
    def _(chunk):
        row = rows_of(chunk)
        diag = prepare(coef, 1, row)[0]
        out[0, pl.ds(row, CH), :] = g[par, pl.ds(row, CH), :]
        out[1, pl.ds(row, CH), :] = g[inner, pl.ds(row, CH), :] / (CENTER * diag)


(FXO, FXA, FYO, FYA, IVO, IVA, IVI, Z0, Z1, Z2, Z3, Z4, XA, XI, PA, PI, DA, EB, PB, X2B, COARSE_AT, STATE) = range(22)


def ready_kernel(g, gs, b, bs, bx, sent, state, xa, coef, rhs, mine, red, cpl, sems):
    del sent
    _, par, _ = position()
    inner = 1 - par
    alive = outer_mask()
    O2, O1, A, B, I1, I2 = range(6)
    FXB, FXI, FYB, FYI, IVB, DB, XB, RB = range(8)
    copies = Copies(sems)
    source = {O2: bx.at[par], O1: bx.at[inner], A: b.at[par], B: b.at[inner], I1: bs.at[par], I2: bs.at[inner]}
    given = [g.at[par], g.at[inner], gs.at[par]]
    started = [fill(copies, ref, coef, p) for p, ref in source.items()]
    started += [copies.start(ref, rhs.at[k]) for k, ref in enumerate(given)]
    clear_pads(coef, range(6))
    clear_pads(state, (FXO, FXA, XA, XI, EB))
    clear_pads(mine, (FXB, FXI, XB))
    for copy in started:
        copy.wait()
    clear_outside([(coef, O2), (coef, O1)])
    keep = {
        O1: ((state, FXO), (state, FYO), (state, IVO), (state, Z1), None, None),
        A: ((state, FXA), (state, FYA), (state, IVA), (state, Z2), (state, DA), (state, XA)),
        B: ((mine, FXB), (mine, FYB), (mine, IVB), (state, Z3), (mine, DB), (mine, XB)),
        I1: ((mine, FXI), (mine, FYI), (state, IVI), (state, Z4), None, (state, XI)),
    }

    @pl.loop(0, N // CH)
    def _(chunk):
        row = rows_of(chunk)
        put(state, Z0, row, 0.5 * (at(coef, O2, row) + at(coef, O1, row)))
        for k, p in enumerate((O1, A, B, I1)):
            diag, fx, fy, fz = prepare(coef, p, row)
            to_fx, to_fy, to_iv, to_fz, to_dg, to_x = keep[p]
            inv = 1.0 / diag
            if p == O1:
                inv = inv * alive
            put(*to_fx, row, fx)
            put(*to_fy, row, fy)
            put(*to_iv, row, inv)
            put(*to_fz, row, fz)
            if to_dg:
                put(*to_dg, row, diag)
            if to_x:
                x1 = rhs[k - 1, pl.ds(row, CH), :] * inv * (1.0 / CENTER)
                put(*to_x, row, x1)
                if p == A:
                    xa[pl.ds(row, CH), :] = x1
        for k, (p, q) in enumerate(((A, B), (O1, O2), (I1, I2))):
            red[pl.ds(k * N + row, CH), :] = at(coef, p, row) + at(coef, q, row)

    step_a, step_b = FINE[0]
    left_over = 1.0 - 1.0 / CENTER

    @pl.loop(0, N // CH)
    def _(chunk):
        row = rows_of(chunk)
        here = at(mine, XB, row)
        part = lateral(row, (state, XA), (state, FXA), (state, FYA)) + at(state, Z2, row) * here
        put(state, PA, row, part + left_over * rhs[0, pl.ds(row, CH), :])
        part = lateral(row, (state, XI), (mine, FXI), (mine, FYI)) + at(state, Z3, row) * here
        put(state, PI, row, part + left_over * rhs[2, pl.ds(row, CH), :])
        res = lateral(row, (mine, XB), (mine, FXB), (mine, FYB)) + left_over * rhs[1, pl.ds(row, CH), :]
        res = res + (at(state, Z2, row) * at(state, XA, row) + at(state, Z3, row) * at(state, XI, row))
        move = step_a * here + step_b * (at(mine, IVB, row) * res)
        put(state, EB, row, move)
        put(state, X2B, row, here + move)
        put(mine, RB, row, res - at(mine, DB, row) * move)

    @pl.loop(0, N // CH)
    def _(chunk):
        row = rows_of(chunk)
        put(state, PB, row, at(mine, RB, row) + lateral(row, (state, EB), (mine, FXB), (mine, FYB)))

    cpl[...] = dot(red[...], pair_matrix(N, NC))
    bc, bo, bi = (
        0.125 * (cpl[pl.ds(k * N, NC, 2), :] + cpl[pl.ds(k * N + 1, NC, 2), :]) for k in range(3)
    )
    row_at = lax.broadcasted_iota(jnp.int32, (NC, NC), 0)
    lane = lane_iota((NC, NC))
    around = (
        jnp.where(lane == NC - 1, 0.0, left(bc))
        + jnp.where(lane == 0, 0.0, right(bc))
        + jnp.where(row_at == NC - 1, 0.0, pltpu.roll(bc, NC - 1, 0))
        + jnp.where(row_at == 0, 0.0, pltpu.roll(bc, 1, 0))
    )
    diag = 0.25 * (3.0 * bc + 0.5 * (around + bo + bi))
    state[COARSE_AT, 0:NC, 0:NC] = bc
    state[COARSE_AT, 0:NC, NC:N] = 1.0 / (CENTER * diag)


SPLIT = 4
HELD = 5


def pre_kernel(bs, bx, state, sx, xi, pack, side, x1, e2, part, red, cpl, packed, own, zeros, sems):
    _, par, _ = position()
    inner = 1 - par
    copies = Copies(sems)
    leaving = [copies.start(bs.at[par], side.at[2])]
    beyond = outer_mask() == 0.0

    @pl.when(beyond)
    def _():
        zeros[...] = jnp.zeros((N, N), jnp.float32)
        copies.again(zeros, side.at[3])

    @pl.when(jnp.logical_not(beyond))
    def _():
        copies.again(bx.at[inner], side.at[3])

    leaving.append(copies.handle(bx.at[inner], side.at[3]))
    clear_pads(x1, [0])
    clear_pads(e2, [0])

    @pl.loop(0, N // CH)
    def _(chunk):
        row = rows_of(chunk)
        put(x1, 0, row, sx[0, pl.ds(row, CH), :] * at(state, IVO, row) * (1.0 / CENTER))

    step_a, step_b = FINE[0]

    @pl.loop(0, N // CH)
    def _(chunk):
        row = rows_of(chunk)
        here = at(x1, 0, row)
        res = lateral(row, (x1, 0), (state, FXO), (state, FYO)) + (1.0 - 1.0 / CENTER) * sx[0, pl.ds(row, CH), :]
        res = res + (at(state, Z0, row) * sx[1, pl.ds(row, CH), :] + at(state, Z1, row) * at(state, XA, row))
        e2o = step_a * here + step_b * (at(state, IVO, row) * res)
        res = at(state, PA, row) + at(state, Z1, row) * here
        e2a = step_a * at(state, XA, row) + step_b * (at(state, IVA, row) * res)
        put(e2, 0, row, e2a)
        own[2, pl.ds(row, CH), :] = at(state, XA, row) + e2a
        own[3, pl.ds(row, CH), :] = at(state, X2B, row)
        res = res - at(state, DA, row) * e2a
        part[pl.ds(row, CH), :] = res + (at(state, Z1, row) * e2o + at(state, Z2, row) * at(state, EB, row))
        res = at(state, PI, row) + at(state, Z4, row) * xi[pl.ds(row, CH), :]
        e2i = step_a * at(state, XI, row) + step_b * (at(state, IVI, row) * res)
        own[1, pl.ds(row, CH), :] = at(state, PB, row) + (at(state, Z2, row) * e2a + at(state, Z3, row) * e2i)

    leaving += [copies.start(own.at[1], side.at[1]), copies.start(own.at[2:4], side.at[4:6])]

    @pl.loop(0, N // CH)
    def _(chunk):
        row = rows_of(chunk)
        res = part[pl.ds(row, CH), :] + lateral(row, (e2, 0), (state, FXA), (state, FYA))
        own[0, pl.ds(row, CH), :] = res
        red[pl.ds(row, CH), :] = res + own[1, pl.ds(row, CH), :]

    leaving.append(copies.start(own.at[0], side.at[0]))
    cpl[0:N, :] = dot(red[...], pair_matrix(N, NC))
    rc = 0.125 * (cpl[pl.ds(0, NC, 2), :] + cpl[pl.ds(1, NC, 2), :])
    fields = (rc * state[COARSE_AT, 0:NC, NC:N], state[COARSE_AT, 0:NC, 0:NC])
    for k, field in enumerate(fields):
        base = k * (NC + 16)
        cpl[base : base + 8, :] = jnp.zeros((8, NC), jnp.float32)
        cpl[base + NC + 8 : base + NC + 16, :] = jnp.zeros((8, NC), jnp.float32)
        cpl[base + 8 : base + NC + 8, :] = field
    each = NC // 2 // SPLIT
    for part in range(SPLIT):
        for odd, first in ((0, 4), (1, 9)):
            for k in range(2):
                for j in range(HELD):
                    rows = cpl[pl.ds(k * (NC + 16) + first + j + part * each * 2, each, 2), :]
                    packed[pl.ds(part * each * 4 * HELD + (odd * 2 + k) * HELD + j, each, 4 * HELD), :] = rows
        piece = pl.ds(part * each * 4 * HELD, each * 4 * HELD)
        leaving.append(copies.start(packed.at[piece], pack.at[piece]))
    for copy in leaving:
        copy.wait()


class CoarseRows:
    def __init__(self, planes):
        self.index, self.par, _ = position()
        self.planes = planes
        self.plane_at = lax.broadcasted_iota(jnp.int32, (planes, NC), 0)
        self.lane = lane_iota((planes, NC))
        self.fr, self.fz, self.fy, self.dg, self.iv = {}, {}, {}, {}, {}

    def load(self, ref, field, n, own):
        at_n = jnp.where(self.par == 0, 4 - n, n) if own else jnp.where(self.par == 0, -n - 1, 5 + n)
        return ref[pl.ds(field * HELD + at_n, self.planes, 2 * HELD), :]

    def up(self, v):
        return pltpu.roll(v, self.planes - 1, 0)

    def down(self, v):
        return pltpu.roll(v, 1, 0)

    def prepare(self, bc, j):
        last, end = self.plane_at == self.planes - 1, self.lane == NC - 1
        zn = jnp.where(last, 0.0, self.up(bc[j]))
        zp = jnp.where(self.plane_at == 0, 0.0, self.down(bc[j]))
        yn = jnp.where(end, 0.0, left(bc[j]))
        yp = jnp.where(self.lane == 0, 0.0, right(bc[j]))
        self.fz[j] = jnp.where(last, 0.0, 0.125 * (bc[j] + zn))
        self.fy[j] = jnp.where(end, 0.0, 0.125 * (bc[j] + yn))
        self.dg[j] = 0.75 * bc[j] + 0.125 * (zn + zp + yn + yp + bc[j + 1])
        if j == 0 and j - 1 not in bc:
            return
        self.dg[j] = self.dg[j] + 0.125 * bc[j - 1]
        row = self.index + jnp.where(self.par == 0, -j, j)
        inside = (row >= 0) & (row < NC)
        self.iv[j] = jnp.where(inside, 1.0 / jnp.where(inside, self.dg[j], 1.0), 0.0)

    def off(self, v, j):
        total = self.fr[j] * v[j + 1]
        if j - 1 in v:
            total = total + self.fr[j - 1] * v[j - 1]
        total = total + self.fz[j] * self.up(v[j]) + self.down(self.fz[j] * v[j])
        return total + self.fy[j] * left(v[j]) + right(self.fy[j] * v[j])


HANDED = 16


def coarse_first_kernel(recv, handed):
    m = CoarseRows(recv.shape[0] // (2 * HELD))
    u1 = {j: m.load(recv, 0, j, True) for j in range(5)}
    bc = {j: m.load(recv, 1, j, True) for j in range(5)}
    m.fr = {j: 0.125 * (bc[j] + bc[j + 1]) for j in range(4)}
    for j in (0, 1, 2, 3):
        m.prepare(bc, j)
    (a1, b1), (a2, b2) = COARSE[:2]
    res = {j: (CENTER - 1.0) * m.dg[j] * u1[j] + m.off(u1, j) for j in (1, 2, 3)}
    step = {j: a1 * u1[j] + b1 * m.iv[j] * res[j] for j in (1, 2, 3)}
    second = res[2] - m.dg[2] * step[2] + m.off(step, 2)
    later = a2 * step[2] + b2 * m.iv[2] * second
    found = (m.fr[0], m.fr[1], m.fz[1], m.fy[1], m.dg[1], m.iv[1], res[1], step[1], step[2], later, u1[1], bc[1])
    found += (m.fz[0], m.fy[0], m.dg[0], m.off(u1, 0))
    for k, value in enumerate(found):
        handed[k] = value


def coarse_kernel(recv, other, handed, pack, cpl, packed, sems):
    planes = recv.shape[0] // (2 * HELD)
    m = CoarseRows(planes)
    u1 = {j: m.load(other, 0, j, False) for j in range(-4, 0)}
    bc = {j: m.load(other, 1, j, False) for j in range(-4, 0)}
    u1[0], bc[0] = m.load(recv, 0, 0, True), m.load(recv, 1, 0, True)
    m.fr = {j: 0.125 * (bc[j] + bc[j + 1]) for j in range(-4, 0)}
    m.fr[0], m.fr[1], m.fz[1], m.fy[1], m.dg[1], m.iv[1], near, second1, second2, third2, u1[1], bc[1] = (
        handed[k] for k in range(12)
    )
    m.fz[0], m.fy[0], m.dg[0], here = (handed[k] for k in range(12, HANDED))
    m.dg[0] = m.dg[0] + 0.125 * bc[-1]
    m.iv[0] = 1.0 / m.dg[0]
    for j in range(-3, 0):
        m.prepare(bc, j)
    reach = 3
    res = {j: (CENTER - 1.0) * m.dg[j] * u1[j] + m.off(u1, j) for j in range(-reach, 0)}
    res[0] = (CENTER - 1.0) * m.dg[0] * u1[0] + (here + m.fr[-1] * u1[-1])
    res[1] = near
    step = u1
    total = u1[0]
    known = ({1: second1, 2: second2}, {2: third2}, {})
    for (step_a, step_b), there in zip(COARSE, known, strict=True):
        moved_by = dict(there)
        for j in range(-reach, min(reach, 1) + 1):
            if j not in moved_by:
                moved_by[j] = step_a * step[j] + step_b * m.iv[j] * res[j]
        step = moved_by
        total = total + step[0]
        reach -= 1
        res = {j: res[j] - m.dg[j] * step[j] + m.off(step, j) for j in range(-reach, min(reach, 1) + 1)}
    groups = lax.axis_size("grp")
    each = planes // groups
    column = jnp.sum(res[0].reshape(groups, each, NC), axis=1, keepdims=True)
    weight = jnp.sum(m.dg[0].reshape(groups, each, NC), axis=1, keepdims=True)
    lift = jnp.broadcast_to(column / weight, (groups, each, NC)).reshape(planes, NC)
    cpl[0:8, :] = jnp.zeros((8, NC), jnp.float32)
    cpl[planes + 8 : planes + 16, :] = jnp.zeros((8, NC), jnp.float32)
    cpl[8 : planes + 8, :] = total + lift
    for k in range(5):
        packed[pl.ds(k, planes, 5), :] = cpl[pl.ds(6 + k, planes), :]
    Copies(sems).start(packed, pack).wait()


def post_kernel(
    b, bs, bx, own, over, side, w, x5, r5,
    coef, fx, fy, fz, iv, dg, before, x2v, pw, r3, e4, r4, e5, half, wide, x5v, r5v, sems,
):
    _, par, _ = position()
    inner = 1 - par
    order = (par, inner)
    alive = outer_mask()
    copies = Copies(sems)
    source = (over.at[2], bx.at[par], bx.at[inner], b.at[par], b.at[inner], bs.at[par], bs.at[inner], side.at[3])
    earlier = (over.at[1], over.at[0], own.at[0], own.at[1], side.at[1], side.at[0])
    started = {}
    for p in range(8):
        started[p] = [fill(copies, source[p], coef, p)]
        if 1 <= p <= 6:
            started[p].append(copies.start(earlier[p - 1], before.at[p - 1]))
    x2_copy = copies.start(own.at[4:6], x2v)
    clear_pads(coef, range(8))
    clear_pads(fx, range(4))
    clear_pads(pw, range(5))
    clear_pads(e4, range(6))
    clear_pads(e5, range(4))
    spread = dot(w[...], 0.5 * pair_matrix(NC, N))
    for side in (0, 1):
        wide[side] = spread[:, side * NC : (side + 1) * NC]
    held = (0, 1, 1, 2, 2, 3, 3, 4)
    for k in range(5):
        z = jnp.where(par == 0, k, 4 - k)
        for side in (0, 1):
            part = wide[side, pl.ds(z, NC, 5), :]
            half[pl.ds(0, NC, 2), :] = part
            half[pl.ds(1, NC, 2), :] = part
            pw[k, PAD : PAD + N, side * NC : (side + 1) * NC] = half[...]

    def arrived(planes):
        for p in planes:
            for copy in started[p]:
                copy.wait()

    arrived(range(3))
    clear_outside([(coef, 0), (coef, 1), (coef, 2)])

    @whole_planes
    def _(row):
        for k in range(6):
            p = k + 1
            if k > 0:
                arrived([p + 1])
            win = window(coef, p, row)
            ahead = pltpu.roll(win, win.shape[0] - 1, 0)
            mid = win[PAD : PAD + CH]
            lane = lane_iota(mid.shape)
            nxt = jnp.where(lane == N - 1, 0.0, left(mid))
            prv = jnp.where(lane == 0, 0.0, right(mid))
            under, over = at(coef, p - 1, row), at(coef, p + 1, row)
            around = (ahead[PAD : PAD + CH] + shifted(win, -1)) + (nxt + prv) + (under + over)
            diag = 6.0 * mid + around
            if k < 2:
                inv = alive * inverse(jnp.where(diag > 0.0, diag, 1.0))
            else:
                inv = inverse(diag)
            fxw = win + ahead
            fyc = jnp.where(lane == N - 1, 0.0, mid + nxt)
            below, above = mid + under, mid + over
            if 1 <= k <= 4:
                put(fx, k - 1, row, fxw[PAD : PAD + CH])
                fy[k - 1, pl.ds(row, CH), :] = fyc
                fz[k - 1, pl.ds(row, CH), :] = below
                iv[k - 1, pl.ds(row, CH), :] = inv
                if k == 4:
                    fz[4, pl.ds(row, CH), :] = above
            if k in (2, 3):
                dg[k - 2, pl.ds(row, CH), :] = diag
            v = window(pw, held[p], row)
            here = v[PAD : PAD + CH]
            total = fxw[PAD : PAD + CH] * shifted(v, 1) + shifted(fxw * v, -1)
            total = total + (fyc * left(here) + right(fyc * here))
            total = total + (below * at(pw, held[p - 1], row) + above * at(pw, held[p + 1], row))
            res = (before[k, pl.ds(row, CH), :] - diag * here) + total
            if 1 <= k <= 4:
                r3[k - 1, pl.ds(row, CH), :] = res
            put(e4, k, row, (1.0 / CENTER) * (inv * res))

    x2_copy.wait()
    step_a, step_b = FINE[0]

    def off(v, k, shift, row):
        win, f = window(v, k + shift, row), window(fx, k, row)
        here = win[PAD : PAD + CH]
        g = fy[k, pl.ds(row, CH), :]
        total = f[PAD : PAD + CH] * shifted(win, 1) + shifted(f * win, -1)
        total = total + (g * left(here) + right(g * here))
        total = total + fz[k, pl.ds(row, CH), :] * at(v, k + shift - 1, row)
        return total + fz[k + 1, pl.ds(row, CH), :] * at(v, k + shift + 1, row)

    @whole_planes
    def _(row):
        for k in range(4):
            res = off(e4, k, 1, row) + (1.0 - 1.0 / CENTER) * r3[k, pl.ds(row, CH), :]
            here = at(e4, k + 1, row)
            move = step_a * here + step_b * (iv[k, pl.ds(row, CH), :] * res)
            put(e5, k, row, move)
            if k in (1, 2):
                r4[k - 1, pl.ds(row, CH), :] = res
                x5v[k - 1, pl.ds(row, CH), :] = x2v[k - 1, pl.ds(row, CH), :] + 2.0 * (at(pw, held[k + 2], row) + (here + move))

    leaving = [copies.start(x5v.at[k], x5.at[order[k]]) for k in range(2)]

    @whole_planes
    def _(row):
        for k in (1, 2):
            res = r4[k - 1, pl.ds(row, CH), :] - dg[k - 1, pl.ds(row, CH), :] * at(e5, k, row)
            r5v[k - 1, pl.ds(row, CH), :] = res + off(e5, k, 0, row)
            leaving.append(copies.start(r5v.at[k - 1], r5.at[order[k - 1]]))

    for copy in leaving:
        copy.wait()


def call(kernel, outs, scratch, sems, cost, *operands, limit=24):
    return pl.pallas_call(
        kernel,
        out_shape=[jax.ShapeDtypeStruct(s, jnp.float32) for s, _ in outs],
        in_specs=[spec for _, spec in operands],
        out_specs=[spec for _, spec in outs],
        scratch_shapes=[pltpu.VMEM(s, jnp.float32) for s in scratch] + [pltpu.SemaphoreType.DMA((sems,))] * (sems > 0),
        compiler_params=pltpu.CompilerParams(vmem_limit_bytes=limit * 1024 * 1024),
        cost_estimate=pl.CostEstimate(flops=cost, bytes_accessed=cost, transcendentals=0),
    )(*(array for array, _ in operands))


def local(right_side, conductivity):
    total = lax.axis_size("grp") * lax.axis_size("slab")
    inside = [(i, i ^ 1) for i in range(total)]
    across = [(i, (i + 1) % total) for i in range(1, total, 2)] + [((i + 1) % total, i) for i in range(1, total, 2)]

    def swap(v):
        return lax.ppermute(v, AXES, inside)

    between = [pair for pair in across if abs(pair[0] - pair[1]) == 1]

    def cross(v, ends=True):
        return lax.ppermute(v, AXES, across if ends else between)

    def everywhere(v):
        rows = v.shape[0]
        return lax.all_to_all(v.reshape(rows, 1, NC), AXES, 0, 0, tiled=True).reshape(rows, NC)

    plane, padded = (N, N), (N + 2 * PAD, N)
    two = (2,) + plane
    g, b = right_side, conductivity
    bs = swap(b)
    bx = cross(b)
    gs = swap(g)
    (send,) = call(first_kernel, [(two, VM)], [(3,) + padded], 3, 1 << 20, (g, VM), (b, ANY), (bs, ANY))
    sx = cross(send, False)
    state, xa = call(
        ready_kernel,
        [((STATE,) + padded, VM), (plane, VM)],
        [(6,) + padded, (3,) + plane, (8,) + padded, (3 * N, N), (3 * N, NC)],
        9,
        6 << 20,
        (g, ANY), (gs, ANY), (b, ANY), (bs, ANY), (bx, ANY), (send, ANY),
    )
    xi = swap(xa)
    pack, side = call(
        pre_kernel,
        [((2 * HELD * total, NC), HBM), ((6,) + plane, HBM)],
        [(1,) + padded, (1,) + padded, plane, plane, (2 * (NC + 16), NC), (2 * HELD * total, NC), (4,) + plane, plane],
        5 + SPLIT,
        6 << 20,
        (bs, ANY), (bx, ANY), (state, VM), (sx, VM), (xi, VM),
    )
    from_over = cross(side, False)
    from_side = swap(side)
    own = swap(from_side)
    got = everywhere(pack)
    (handed,) = call(coarse_first_kernel, [((HANDED, total, NC), VM)], [], 0, 2 << 20, (got, VM))
    (back,) = call(
        coarse_kernel,
        [((5 * NC, NC), HBM)],
        [(total + 16, NC), (5 * NC, NC)],
        1,
        4 << 20,
        (got, VM), (swap(got), VM), (handed, VM),
    )
    w = everywhere(back)
    x5, r5 = call(
        post_kernel,
        [(two, HBM), (two, HBM)],
        [(8,) + padded, (4,) + padded, (4,) + plane, (5,) + plane, (4,) + plane, two, (6,) + plane, two, (5,) + padded, (4,) + plane, (6,) + padded, two, (4,) + padded, (N, NC), (2, 5 * NC, NC), two, two],
        20,
        8 << 20,
        (b, ANY), (bs, ANY), (bx, ANY), (own, ANY), (from_over, ANY), (from_side, ANY), (w, VM),
    )
    return x5, r5


def solution(mesh):
    spec = P(AXES, None, None)
    return jax.shard_map(
        local, mesh=mesh, in_specs=(spec, spec), out_specs=(spec, spec), check_vma=False
    )
```
